32 devices in a mesh: wide: 8 (over z, core), narrow: 4 (over y, x).
Axes of the slice: x: 2, y: 2, z: 4, core: 2. Of those that a mesh axis runs over, the one named last changes fastest.
Arguments:
- activations: bfloat16 [6144, 4096], P('wide'), may hold values from -12 to 12
- gain: bfloat16 [4096], replicated, may hold values from 0.099609375 to 1.8984375
- w_query: bfloat16 [4096, 4096], P('wide', 'narrow'), may hold values from -0.5 to 0.5
- w_key: bfloat16 [4096, 1024], P('wide', 'narrow'), may hold values from -14 to 14
- w_value: bfloat16 [4096, 1024], P('wide', 'narrow'), may hold values from -0.09375 to 0.09375
- w_out: bfloat16 [4096, 4096], P('wide', 'narrow'), may hold values from -0.09375 to 0.09375
- cotangent: bfloat16 [6144, 4096], P('wide'), may hold values from -6 to 6
Outputs:
- outputs: bfloat16 [6144, 4096], P('wide', 'narrow')
- grad_query: float32 [4096, 4096], P('wide', 'narrow')
- grad_key: float32 [4096, 1024], P('wide', 'narrow')
- grad_value: float32 [4096, 1024], P('wide', 'narrow')
- grad_out: float32 [4096, 4096], P('wide', 'narrow')
The draws below stay inside these ranges and needn't reach their ends.
All inputs are finite; a program needn't handle non-finite values.
Results may differ from the reference program's by a relative error of at most 0.017.
The reference program's roundings to bfloat16 on the way (of `normed`, `rounded`, `mixed`, `grad_mixed`, `grad_values` and `grad_scores`) count: a program that leaves them out, or rounds other values in their place, can miss the bound.
Values may be sent and summed in bfloat16 or wider, within the bound.
No kernel may reach another device: no remote copies, remote signals or barrier semaphores. Data moves between devices by JAX's collectives and lax.ppermute only.
A program may use at most 192 MiB of HBM per device.

```python
import math
import jax
import jax.numpy as jnp
from jax import lax

D = 4096
HEADS = 32
KV = 8
HEAD_DIM = 128
SEQ = 768
TOKENS = 6144
N_WIDE = 8


def shared_query(key):
    return jax.random.truncated_normal(key, -4.0, 4.0, (D, HEADS * HEAD_DIM), jnp.float32) * D ** (-0.5)


def draw_w_query(key, part):
    shared = shared_query(key)
    return shared.astype(jnp.bfloat16)


def draw_w_key(key, part):
    key = jax.random.fold_in(key, 2)
    noise = jax.random.truncated_normal(key, -4.0, 4.0, (D, KV * HEAD_DIM), jnp.float32) * D ** (-0.5)
    return noise.astype(jnp.bfloat16)


def draw_activations(key, part):
    key = jax.random.fold_in(key, 3)
    first, second = jax.random.split(key)
    row_scale = jnp.exp(jax.random.uniform(first, (TOKENS, 1), jnp.float32, math.log(0.3), math.log(3.0)))
    base = jax.random.truncated_normal(second, -4.0, 4.0, (TOKENS, D), jnp.float32)
    return (base * row_scale).astype(jnp.bfloat16)


def shard_levels(stream_key, shape, cuts, smallest, high):
    def one(position, blocks):
        steps = jax.random.uniform(jax.random.fold_in(jax.random.fold_in(stream_key, 6), position), (blocks,), jnp.float32, smallest / len(cuts), high / len(cuts))
        return jnp.repeat(jnp.exp(steps), shape[position] // blocks).reshape((-1,) + (1,) * (len(shape) - position - 1))

    loudness = one(*cuts[0])
    for cut in cuts[1:]:
        loudness = loudness * one(*cut)
    return loudness


def centred(key, dims, scale, most, shards=(), kind=jnp.bfloat16):
    entries = scale * jax.random.normal(key, dims, jnp.float32)
    if shards:
        entries = entries * shard_levels(key, dims, shards, -0.22, 0.18)
    return jnp.clip(entries, -most, most).astype(kind)


def setup_inputs(seed: int = 0) -> dict:
    keys = jax.random.split(jax.random.key(seed), 8)
    activations = draw_activations(jax.random.fold_in(keys[7], 71), 0)
    gain = jnp.clip(1.0 + 0.18 * jax.random.normal(keys[1], (D,), jnp.float32), 0.099609375, 1.8984375).astype(jnp.bfloat16)
    w_query = draw_w_query(jax.random.fold_in(keys[7], 71), 0)
    w_key = draw_w_key(jax.random.fold_in(keys[7], 71), 0)
    w_value = centred(keys[4], (D, KV * HEAD_DIM), D ** -0.5, 0.09375, ((0, 8), (1, 4)))
    w_out = centred(keys[5], (D, HEADS * HEAD_DIM), (HEADS * HEAD_DIM) ** -0.5, 0.09375, ((0, 8), (1, 4)))
    cotangent = centred(keys[6], (TOKENS, D), 1.0, 6.0, ((0, 8),))
    return {"activations": activations, "gain": gain, "w_query": w_query, "w_key": w_key, "w_value": w_value, "w_out": w_out, "cotangent": cotangent}


epsilon = 1e-05
masked_score = -1e+30

def normalize(rows, gain):
    values32 = rows.astype(jnp.float32)
    mean_square = lax.optimization_barrier(jnp.mean(values32 * values32, axis=-1, keepdims=True))
    return (values32 * lax.rsqrt(mean_square + epsilon) * gain.astype(jnp.float32)).astype(jnp.bfloat16)

def split_heads(queries, key_rows, value_rows, width):
    length = queries.shape[0]
    groups = key_rows.shape[1] // width
    members = queries.shape[1] // key_rows.shape[1]
    query_split = queries.astype(jnp.float32).reshape(length, groups, members, width)
    key_split = key_rows.astype(jnp.float32).reshape(length, groups, width)
    value_split = value_rows.astype(jnp.float32).reshape(length, groups, width)
    return (query_split, key_split, value_split)

def attend_forward(queries, key_rows, value_rows, width):
    length = queries.shape[0]
    query_split, key_split, value_split = split_heads(queries, key_rows, value_rows, width)
    scores = jnp.einsum('sjgd,tjd->jgst', query_split, key_split) * width ** (-0.5)
    causal = lax.broadcasted_iota(jnp.int32, (length, length), 0) >= lax.broadcasted_iota(jnp.int32, (length, length), 1)
    scores = jnp.where(causal, scores, masked_score)
    highest = lax.optimization_barrier(jnp.max(scores, axis=-1, keepdims=True))
    exponent = jnp.exp(scores - highest)
    attn_probs = exponent / lax.optimization_barrier(jnp.sum(exponent, axis=-1, keepdims=True))
    rounded = attn_probs.astype(jnp.bfloat16)
    mixed = jnp.einsum('jgst,tjd->sjgd', rounded.astype(jnp.float32), value_split)
    return (attn_probs, rounded, mixed.reshape(length, -1).astype(jnp.bfloat16))

def attend_backward(attn_probs, rounded, queries, key_rows, value_rows, grad_mixed, width):
    length = queries.shape[0]
    query_split, key_split, value_split = split_heads(queries, key_rows, value_rows, width)
    grad_split = grad_mixed.astype(jnp.float32).reshape(query_split.shape)
    grad_values = jnp.einsum('jgst,sjgd->tjd', rounded.astype(jnp.float32), grad_split)
    grad_probs = jnp.einsum('sjgd,tjd->jgst', grad_split, value_split)
    inner = lax.optimization_barrier(jnp.sum(grad_probs * attn_probs, axis=-1, keepdims=True))
    grad_scores = (attn_probs * (grad_probs - inner) * width ** (-0.5)).astype(jnp.bfloat16).astype(jnp.float32)
    grad_queries = jnp.einsum('jgst,tjd->sjgd', grad_scores, key_split)
    grad_keys = jnp.einsum('jgst,sjgd->tjd', grad_scores, query_split)
    return (grad_queries.reshape(length, -1).astype(jnp.bfloat16), grad_keys.reshape(length, -1).astype(jnp.bfloat16), grad_values.reshape(length, -1).astype(jnp.bfloat16))

def rounded_term(left, right):
    product = jnp.dot(left.T, right, preferred_element_type=jnp.float32)
    return lax.optimization_barrier(product.astype(jnp.bfloat16)).astype(jnp.float32)

def reference(activations, gain, w_query, w_key, w_value, w_out, cotangent):
    width = HEAD_DIM
    batches = activations.reshape(N_WIDE, SEQ, D)
    grad_batches = cotangent.reshape(N_WIDE, SEQ, D)

    def one_batch(sums, inputs):
        rows, grad_rows = inputs
        normed = normalize(rows, gain)
        queries = jnp.dot(normed, w_query, preferred_element_type=jnp.float32).astype(jnp.bfloat16)
        key_rows = jnp.dot(normed, w_key, preferred_element_type=jnp.float32).astype(jnp.bfloat16)
        value_rows = jnp.dot(normed, w_value, preferred_element_type=jnp.float32).astype(jnp.bfloat16)
        attn_probs, rounded, mixed = attend_forward(queries, key_rows, value_rows, width)
        projected = jnp.dot(mixed, w_out.T, preferred_element_type=jnp.float32)
        outputs = (rows.astype(jnp.float32) + projected).astype(jnp.bfloat16)
        grad_mixed = jnp.dot(grad_rows, w_out, preferred_element_type=jnp.float32).astype(jnp.bfloat16)
        grad_queries, grad_keys, grad_values = attend_backward(attn_probs, rounded, queries, key_rows, value_rows, grad_mixed, width)
        terms = (rounded_term(normed, grad_queries), rounded_term(normed, grad_keys), rounded_term(normed, grad_values), rounded_term(grad_rows, mixed))
        return (tuple((running + term for running, term in zip(sums, terms))), outputs)
    initial = (jnp.zeros(w_query.shape, jnp.float32), jnp.zeros(w_key.shape, jnp.float32), jnp.zeros(w_value.shape, jnp.float32), jnp.zeros(w_out.shape, jnp.float32))
    sums, outputs = lax.scan(one_batch, initial, (batches, grad_batches))
    return (outputs.reshape(TOKENS, D), sums[0], sums[1], sums[2], sums[3])
```

```python
import functools
import jax
import jax.numpy as jnp
from jax import lax
from jax.experimental import pallas as pl
from jax.experimental.pallas import tpu as pltpu
from jax.sharding import PartitionSpec as P

HEAD_DIM = 128
BLOCK = 256
EPSILON = 1e-05
MASKED = -1e30
F32 = jnp.float32
BF16 = jnp.bfloat16


def normalize(rows, gain):
    values32 = rows.astype(F32)
    mean_square = jnp.mean(values32 * values32, axis=-1, keepdims=True)
    return (values32 * lax.rsqrt(mean_square + EPSILON) * gain.astype(F32)).astype(BF16)


def nt(a, b):
    return lax.dot_general(a, b, (((1,), (1,)), ((), ())), preferred_element_type=F32)


def nn(a, b):
    return lax.dot_general(a, b, (((1,), (0,)), ((), ())), preferred_element_type=F32)


def row_product(a, b):
    return lax.dot_general(a, b, (((0,), (0,)), ((), ())), preferred_element_type=F32)


def masked_scores(keys, queries, start, size):
    scores = nt(keys, queries) * HEAD_DIM ** (-0.5)
    key_at = lax.broadcasted_iota(jnp.int32, (size, size), 0)
    query_at = lax.broadcasted_iota(jnp.int32, (size, size), 1)
    last = jnp.where(key_at <= query_at, scores[start:], MASKED)
    if start == 0:
        return last
    return jnp.concatenate([scores[:start], last], axis=0)


def forward_kernel(members, block, qkv_ref, mixed_ref, lse_ref):
    length = qkv_ref.shape[0]
    width = HEAD_DIM
    key_col, value_col = members * width, (members + 1) * width
    values_t = qkv_ref[:, value_col : value_col + width].T
    for h in range(members):
        for start in range(0, length, block):
            stop = start + block
            queries = qkv_ref[start:stop, h * width : (h + 1) * width]
            keys = qkv_ref[:stop, key_col : key_col + width]
            scores = masked_scores(keys, queries, start, block)
            highest = jnp.max(scores, axis=0, keepdims=True)
            exponent = jnp.exp(scores - highest)
            total = jnp.sum(exponent, axis=0, keepdims=True)
            rounded = (exponent * (1.0 / total)).astype(BF16)
            mixed_t = nn(values_t[:, :stop], rounded)
            mixed_ref[start:stop, h * width : (h + 1) * width] = mixed_t.T.astype(BF16)
            lse_ref[h : h + 1, start:stop] = highest + jnp.log(total)


def attend_forward(qkv, members, block):
    length = qkv.shape[0]
    width = HEAD_DIM
    vmem = pl.BlockSpec(memory_space=pltpu.VMEM)
    return pl.pallas_call(
        functools.partial(forward_kernel, members, block),
        out_shape=(
            jax.ShapeDtypeStruct((length, members * width), BF16),
            jax.ShapeDtypeStruct((members, length), F32),
        ),
        in_specs=[vmem],
        out_specs=(vmem, vmem),
        compiler_params=pltpu.CompilerParams(vmem_limit_bytes=40 * 2**20),
        cost_estimate=pl.CostEstimate(
            flops=8 * members * length * length * width,
            bytes_accessed=8 * length * members * width,
            transcendentals=members * length * length,
        ),
        name="attend_forward",
    )(qkv)


def backward_kernel(members, block, qkv_ref, grad_ref, lse_ref, out_ref, gk_ref, gv_ref):
    length = qkv_ref.shape[0]
    width = HEAD_DIM
    key_col, value_col = members * width, (members + 1) * width
    keys_t = qkv_ref[:, key_col : key_col + width].T
    gk_ref[...] = jnp.zeros_like(gk_ref)
    gv_ref[...] = jnp.zeros_like(gv_ref)
    for h in range(members):
        cols = slice(h * width, (h + 1) * width)
        for start in range(0, length, block):
            stop = start + block
            queries = qkv_ref[start:stop, cols]
            grads = grad_ref[start:stop, cols]
            keys = qkv_ref[:stop, key_col : key_col + width]
            values = qkv_ref[:stop, value_col : value_col + width]
            scores = masked_scores(keys, queries, start, block)
            probs = jnp.exp(scores - lse_ref[h : h + 1, start:stop])
            grad_probs = nt(values, grads)
            gv_ref[:stop, :] += nn(probs.astype(BF16), grads)
            inner = jnp.sum(grad_probs * probs, axis=0, keepdims=True)
            grad_scores = (probs * (grad_probs - inner) * width ** (-0.5)).astype(BF16)
            gk_ref[:stop, :] += nn(grad_scores, queries)
            out_ref[start:stop, cols] = nn(keys_t[:, :stop], grad_scores).T.astype(BF16)
    out_ref[:, key_col : key_col + width] = gk_ref[...].astype(BF16)
    out_ref[:, value_col : value_col + width] = gv_ref[...].astype(BF16)


def attend_backward(qkv, grad_mixed, lse, members, block):
    length = qkv.shape[0]
    width = HEAD_DIM
    vmem = pl.BlockSpec(memory_space=pltpu.VMEM)
    return pl.pallas_call(
        functools.partial(backward_kernel, members, block),
        out_shape=jax.ShapeDtypeStruct(qkv.shape, BF16),
        in_specs=[vmem, vmem, vmem],
        out_specs=vmem,
        scratch_shapes=[pltpu.VMEM((length, width), F32), pltpu.VMEM((length, width), F32)],
        compiler_params=pltpu.CompilerParams(vmem_limit_bytes=40 * 2**20),
        cost_estimate=pl.CostEstimate(
            flops=20 * members * length * length * width,
            bytes_accessed=8 * length * members * width,
            transcendentals=members * length * length,
        ),
        name="attend_backward",
    )(qkv, grad_mixed, lse)


def take(blocks, at):
    return lax.dynamic_index_in_dim(blocks, at, 0, keepdims=False)


class Order:
    def __init__(self):
        self.last = None

    def __call__(self, compute, *operands):
        if self.last is not None:
            tied = lax.optimization_barrier((self.last, *operands))
            operands = tied[1:]
        result = compute(*operands)
        self.last = jax.tree.leaves(result)[0]
        return result

    def after(self, operand):
        return operand if self.last is None else lax.optimization_barrier((self.last, operand))[1]


class LineSum:
    def __init__(self, order, chips):
        self.order, self.chips = order, chips
        self.chip = lax.axis_index("wide") // 2
        self.up = self.down = None

    def swap(self, send):
        pairs = [(w, w ^ 1) for w in range(2 * self.chips)]
        self.received = lax.ppermute(send, "wide", pairs)

    def add_cores(self, keep):
        def add(keep, received):
            return (keep.astype(F32) + received.astype(F32)).astype(BF16)

        both = self.order(add, keep, self.received)
        self.both = both.reshape(self.chips, -1, both.shape[-1])

    def hop(self, t):
        chips, chip, far = self.chips, self.chip, self.chips - t

        def messages(both, *arrived):
            up = take(both, jnp.minimum(chip + far, chips - 1))
            down = take(both, jnp.maximum(chip - far, 0))
            if arrived:
                up = (up.astype(F32) + arrived[0].astype(F32)).astype(BF16)
                down = (down.astype(F32) + arrived[1].astype(F32)).astype(BF16)
            return up, down

        arrived = () if self.up is None else (self.up, self.down)
        up, down = self.order(messages, self.both, *arrived)
        self.up = lax.ppermute(up, "wide", [(w, w + 2) for w in range(2 * t)])
        self.down = lax.ppermute(down, "wide", [(w, w - 2) for w in range(2 * far, 2 * chips)])

    def total(self):
        def add(both, *arrived):
            result = take(both, self.chip).astype(F32)
            for part in arrived:
                result = result + part.astype(F32)
            return result

        arrived = () if self.up is None else (self.up, self.down)
        return self.order(add, self.both, *arrived)


def shards(wide, activations, gain, w_query, w_key, w_value, w_out, cotangent):
    width = HEAD_DIM
    length, features = activations.shape
    chips = wide // 2
    groups = w_key.shape[1] // width
    members = w_query.shape[1] // w_key.shape[1]
    block = BLOCK if length % BLOCK == 0 else length
    span = members * width
    rows = features // wide
    core = lax.axis_index("wide") % 2
    order = Order()

    def gathered(piece):
        return lax.all_gather(piece, "wide", axis=0, tiled=True)

    def columns(g):
        cols = slice(g * span, (g + 1) * span)
        heads = slice(g * width, (g + 1) * width)
        return jnp.concatenate([w_query[:, cols], w_key[:, heads], w_value[:, heads]], axis=1)

    def out_columns(g):
        return w_out[:, g * span : (g + 1) * span]

    def halves(array):
        split = array.reshape(length, chips, 2, rows)
        own = lax.dynamic_index_in_dim(split, core, 2, keepdims=False)
        other = lax.dynamic_index_in_dim(split, 1 - core, 2, keepdims=False)
        return own.reshape(length, chips * rows), other.reshape(length, chips * rows)

    def product(a, b):
        return jnp.dot(a, b, preferred_element_type=F32).astype(BF16)

    def term(a, b):
        return row_product(a, b).astype(BF16)

    weights = [None] * groups
    out_weights = [None] * groups
    weights[0] = gathered(columns(0))
    normed = order(normalize, activations, gain)
    out_weights[0] = gathered(order.after(out_columns(0)))
    normed_own, normed_other = order(halves, normed)
    cotangent_own, cotangent_other = order(halves, cotangent)

    projected = None
    pending = []

    def advance():
        for steps in list(pending):
            if next(steps, None) is None:
                pending.remove(steps)

    def steps_of(line, results):
        for t in range(1, chips):
            line.hop(t)
            yield True
        results.append(line.total())
        yield True

    def start(own, other, grads, results):
        line = LineSum(order, chips)
        line.swap(order(term, other, grads))
        line.add_cores(order(term, own, grads))
        steps = steps_of(line, results)
        next(steps)
        pending.append(steps)

    sums_out, sums_qkv = [], []
    for g in range(groups):
        qkv = order(product, normed, weights[g])
        if g + 1 < groups:
            weights[g + 1] = gathered(order.after(columns(g + 1)))
        mixed, lse = order(lambda a: attend_forward(a, members, block), qkv)
        start(cotangent_own, cotangent_other, mixed, sums_out)
        advance()
        grad_mixed = order(product, cotangent, out_weights[g])
        if g + 1 < groups:
            out_weights[g + 1] = gathered(order.after(out_columns(g + 1)))
        advance()
        if g + 1 == groups:

            def project(mixed, out_weights, *partial):
                result = nt(mixed, out_weights)
                for part in partial:
                    result = result + part
                return result.astype(BF16)

            partial = () if projected is None else (projected,)
            projected = order(project, mixed, out_weights[g], *partial)
            summed = lax.psum_scatter(projected, "narrow", scatter_dimension=1, tiled=True)
        grad_qkv = order(
            lambda a, b, c: attend_backward(a, b, c, members, block), qkv, grad_mixed, lse
        )
        advance()
        start(normed_own, normed_other, grad_qkv, sums_qkv)
        if g + 1 < groups:
            part = order(nt, mixed, out_weights[g])
            projected = part if projected is None else projected + part
            advance()
            advance()
    while pending:
        advance()

    share = summed.shape[1]
    own_columns = lax.dynamic_slice_in_dim(
        activations, lax.axis_index("narrow") * share, share, 1
    )
    outputs = (own_columns.astype(F32) + summed.astype(F32)).astype(BF16)

    def joined(pieces):
        return pieces[0] if len(pieces) == 1 else jnp.concatenate(pieces, axis=1)

    grad_query = joined([s[:, :span] for s in sums_qkv])
    grad_key = joined([s[:, span : span + width] for s in sums_qkv])
    grad_value = joined([s[:, span + width :] for s in sums_qkv])
    grad_out = joined(sums_out)
    return (outputs, grad_query, grad_key, grad_value, grad_out)


def solution(mesh):
    return jax.shard_map(
        functools.partial(shards, mesh.shape["wide"]),
        mesh=mesh,
        in_specs=(
            P("wide", None),
            P(),
            P("wide", "narrow"),
            P("wide", "narrow"),
            P("wide", "narrow"),
            P("wide", "narrow"),
            P("wide", None),
        ),
        out_specs=(
            P("wide", "narrow"),
            P("wide", "narrow"),
            P("wide", "narrow"),
            P("wide", "narrow"),
            P("wide", "narrow"),
        ),
        check_vma=False,
    )
```

```python
import functools
import jax
import jax.numpy as jnp
from jax import lax
from jax.experimental import pallas as pl
from jax.experimental.pallas import tpu as pltpu
from jax.sharding import PartitionSpec as P

HEAD_DIM = 128
BLOCK = 256
EPSILON = 1e-05
MASKED = -1e30
F32 = jnp.float32
BF16 = jnp.bfloat16


def normalize(rows, gain):
    values32 = rows.astype(F32)
    mean_square = jnp.mean(values32 * values32, axis=-1, keepdims=True)
    return (values32 * lax.rsqrt(mean_square + EPSILON) * gain.astype(F32)).astype(BF16)


def nt(a, b):
    return lax.dot_general(a, b, (((1,), (1,)), ((), ())), preferred_element_type=F32)


def nn(a, b):
    return lax.dot_general(a, b, (((1,), (0,)), ((), ())), preferred_element_type=F32)


def row_product(a, b):
    return lax.dot_general(a, b, (((0,), (0,)), ((), ())), preferred_element_type=F32)


def masked_scores(keys, queries, start, size):
    scores = nt(keys, queries) * HEAD_DIM ** (-0.5)
    key_at = lax.broadcasted_iota(jnp.int32, (size, size), 0)
    query_at = lax.broadcasted_iota(jnp.int32, (size, size), 1)
    last = jnp.where(key_at <= query_at, scores[start:], MASKED)
    if start == 0:
        return last
    return jnp.concatenate([scores[:start], last], axis=0)


def forward_kernel(members, block, qkv_ref, mixed_ref, lse_ref):
    length = qkv_ref.shape[0]
    width = HEAD_DIM
    key_col, value_col = members * width, (members + 1) * width
    values_t = qkv_ref[:, value_col : value_col + width].T
    for h in range(members):
        for start in range(0, length, block):
            stop = start + block
            queries = qkv_ref[start:stop, h * width : (h + 1) * width]
            keys = qkv_ref[:stop, key_col : key_col + width]
            scores = masked_scores(keys, queries, start, block)
            highest = jnp.max(scores, axis=0, keepdims=True)
            exponent = jnp.exp(scores - highest)
            total = jnp.sum(exponent, axis=0, keepdims=True)
            rounded = (exponent * (1.0 / total)).astype(BF16)
            mixed_t = nn(values_t[:, :stop], rounded)
            mixed_ref[start:stop, h * width : (h + 1) * width] = mixed_t.T.astype(BF16)
            lse_ref[h : h + 1, start:stop] = highest + jnp.log(total)


def attend_forward(qkv, members, block):
    length = qkv.shape[0]
    width = HEAD_DIM
    vmem = pl.BlockSpec(memory_space=pltpu.VMEM)
    return pl.pallas_call(
        functools.partial(forward_kernel, members, block),
        out_shape=(
            jax.ShapeDtypeStruct((length, members * width), BF16),
            jax.ShapeDtypeStruct((members, length), F32),
        ),
        in_specs=[vmem],
        out_specs=(vmem, vmem),
        compiler_params=pltpu.CompilerParams(vmem_limit_bytes=40 * 2**20),
        cost_estimate=pl.CostEstimate(
            flops=8 * members * length * length * width,
            bytes_accessed=8 * length * members * width,
            transcendentals=members * length * length,
        ),
        name="attend_forward",
    )(qkv)


def backward_kernel(members, block, qkv_ref, grad_ref, lse_ref, out_ref, gk_ref, gv_ref):
    length = qkv_ref.shape[0]
    width = HEAD_DIM
    key_col, value_col = members * width, (members + 1) * width
    keys_t = qkv_ref[:, key_col : key_col + width].T
    gk_ref[...] = jnp.zeros_like(gk_ref)
    gv_ref[...] = jnp.zeros_like(gv_ref)
    for h in range(members):
        cols = slice(h * width, (h + 1) * width)
        for start in range(0, length, block):
            stop = start + block
            queries = qkv_ref[start:stop, cols]
            grads = grad_ref[start:stop, cols]
            keys = qkv_ref[:stop, key_col : key_col + width]
            values = qkv_ref[:stop, value_col : value_col + width]
            scores = masked_scores(keys, queries, start, block)
            probs = jnp.exp(scores - lse_ref[h : h + 1, start:stop])
            grad_probs = nt(values, grads)
            gv_ref[:stop, :] += nn(probs.astype(BF16), grads)
            inner = jnp.sum(grad_probs * probs, axis=0, keepdims=True)
            grad_scores = (probs * (grad_probs - inner) * width ** (-0.5)).astype(BF16)
            gk_ref[:stop, :] += nn(grad_scores, queries)
            out_ref[start:stop, cols] = nn(keys_t[:, :stop], grad_scores).T.astype(BF16)
    out_ref[:, key_col : key_col + width] = gk_ref[...].astype(BF16)
    out_ref[:, value_col : value_col + width] = gv_ref[...].astype(BF16)


def attend_backward(qkv, grad_mixed, lse, members, block):
    length = qkv.shape[0]
    width = HEAD_DIM
    vmem = pl.BlockSpec(memory_space=pltpu.VMEM)
    return pl.pallas_call(
        functools.partial(backward_kernel, members, block),
        out_shape=jax.ShapeDtypeStruct(qkv.shape, BF16),
        in_specs=[vmem, vmem, vmem],
        out_specs=vmem,
        scratch_shapes=[pltpu.VMEM((length, width), F32), pltpu.VMEM((length, width), F32)],
        compiler_params=pltpu.CompilerParams(vmem_limit_bytes=40 * 2**20),
        cost_estimate=pl.CostEstimate(
            flops=20 * members * length * length * width,
            bytes_accessed=8 * length * members * width,
            transcendentals=members * length * length,
        ),
        name="attend_backward",
    )(qkv, grad_mixed, lse)


def take(blocks, at):
    return lax.dynamic_index_in_dim(blocks, at, 0, keepdims=False)


def split_kernel(chips, core_ref, x_ref, gain_ref, grad_ref, x_own, x_other, grad_own, grad_other):
    features = x_ref.shape[1]
    rows = features // (2 * chips)
    core = core_ref[0]
    total = None
    for w in range(2 * chips):
        values = x_ref[:, w * rows : (w + 1) * rows].astype(F32)
        part = jnp.sum(values * values, axis=-1, keepdims=True)
        total = part if total is None else total + part
    scale = lax.rsqrt(total / features + EPSILON)
    for side, x_out, grad_out in ((core, x_own, grad_own), (1 - core, x_other, grad_other)):
        for chip in range(chips):
            cols = pl.ds(pl.multiple_of((2 * chip + side) * rows, 128), rows)
            to = slice(chip * rows, (chip + 1) * rows)
            x_out[:, to] = (x_ref[:, cols].astype(F32) * scale * gain_ref[:, cols]).astype(BF16)
            grad_out[:, to] = grad_ref[:, cols]


def norm_and_split(core, activations, gain, cotangent, chips):
    length, features = activations.shape
    step = 128 if length % 128 == 0 else length
    whole = pl.BlockSpec((step, features), lambda i: (i, 0))
    half = pl.BlockSpec((step, features // 2), lambda i: (i, 0))
    shape = jax.ShapeDtypeStruct((length, features // 2), BF16)
    return pl.pallas_call(
        functools.partial(split_kernel, chips),
        grid=(length // step,),
        out_shape=(shape,) * 4,
        in_specs=[
            pl.BlockSpec(memory_space=pltpu.SMEM),
            whole,
            pl.BlockSpec((1, features), lambda i: (0, 0)),
            whole,
        ],
        out_specs=(half,) * 4,
        compiler_params=pltpu.CompilerParams(vmem_limit_bytes=32 * 2**20),
        cost_estimate=pl.CostEstimate(
            flops=8 * length * features,
            bytes_accessed=8 * length * features,
            transcendentals=length,
        ),
        name="norm_and_split",
    )(core.reshape(1), activations, gain.astype(F32).reshape(1, -1), cotangent)


def collect_kernel(chips, chip_ref, *refs):
    own, ups, downs = refs[0], refs[: chips], refs[chips : 2 * chips - 1]
    out, sems = refs[-2], refs[-1]
    rows = own.shape[0]
    chip = chip_ref[0]

    def place(source, r):
        at = lax.rem(chip - r + chips, chips)
        to = out.at[pl.ds(pl.multiple_of(at * rows, rows), rows), :]
        return pltpu.make_async_copy(source, to, sems.at[r])

    for r in range(chips):
        if r == 0:
            place(own, r).start()
            continue
        pl.when(chip >= r)(lambda r=r: place(ups[r], r).start())
        pl.when(chip < r)(lambda r=r: place(downs[chips - r - 1], r).start())
    for r in range(chips):
        place(own, r).wait()


def collect(chip, chips, ups, downs):
    rows, cols = ups[0].shape
    anywhere = pl.BlockSpec(memory_space=pl.ANY)
    return pl.pallas_call(
        functools.partial(collect_kernel, chips),
        out_shape=jax.ShapeDtypeStruct((chips * rows, cols), BF16),
        in_specs=[pl.BlockSpec(memory_space=pltpu.SMEM)] + [anywhere] * (len(ups) + len(downs)),
        out_specs=anywhere,
        scratch_shapes=[pltpu.SemaphoreType.DMA((chips,))],
        cost_estimate=pl.CostEstimate(
            flops=0, bytes_accessed=4 * chips * rows * cols, transcendentals=0
        ),
        name="collect",
    )(chip.reshape(1), *ups, *downs)


class Order:
    def __init__(self):
        self.last = None

    def __call__(self, compute, *operands):
        result = compute(*self.after(*operands))
        self.last = jax.tree.leaves(result)[0]
        return result

    def after(self, *operands):
        if self.last is None:
            return operands
        return lax.optimization_barrier((self.last, *operands))[1:]

    def wait(self, *arrays):
        if self.last is None:
            return arrays
        self.last, *arrays = lax.optimization_barrier((self.last, *arrays))
        return arrays


def swap_cores(array, chips):
    return lax.ppermute(array, "wide", [(w, w ^ 1) for w in range(2 * chips)])


class LineGather:
    def __init__(self, order, chips, piece):
        self.order, self.chips, self.piece = order, chips, piece
        self.chip = lax.axis_index("wide") // 2
        self.ups = []
        self.downs = []

    def hop(self):
        chips, t = self.chips, len(self.ups) or 1
        if not self.ups:
            (self.piece,) = self.order.after(self.piece)
            self.ups = [self.piece]
            up = down = self.piece
        else:
            up, down = self.wait()
        if t >= chips:
            return False
        self.ups.append(
            lax.ppermute(up, "wide", [(w, w + 2) for w in range(2 * (t - 1), 2 * (chips - 1))])
        )
        self.downs.append(
            lax.ppermute(down, "wide", [(w, w - 2) for w in range(2, 2 * (chips - t + 1))])
        )
        return True

    def wait(self):
        if not self.downs:
            return self.piece, self.piece
        self.ups[-1], self.downs[-1] = self.order.wait(self.ups[-1], self.downs[-1])
        return self.ups[-1], self.downs[-1]

    def finish(self):
        while self.hop():
            pass

    def halves(self):
        own = self.order(
            lambda *refs: collect(self.chip, self.chips, refs[: self.chips], refs[self.chips :]),
            *self.ups,
            *self.downs,
        )
        return own, swap_cores(own, self.chips)


class LineSum:
    def __init__(self, order, chips):
        self.order, self.chips = order, chips
        self.chip = lax.axis_index("wide") // 2
        self.up = self.down = self.result = None
        self.hops = 0

    def swap(self, send):
        self.received = swap_cores(send, self.chips)

    def add_cores(self, keep):
        def add(keep, received):
            return (keep.astype(F32) + received.astype(F32)).astype(BF16)

        both = self.order(add, keep, self.received)
        self.both = both.reshape(self.chips, -1, both.shape[-1])

    def advance(self):
        if self.result is not None:
            return
        self.hops += 1
        if self.hops == self.chips:
            self.result = self.total()
            return
        t, chips, chip = self.hops, self.chips, self.chip
        far = chips - t

        def messages(both, *arrived):
            up = take(both, jnp.minimum(chip + far, chips - 1))
            down = take(both, jnp.maximum(chip - far, 0))
            if arrived:
                up = (up.astype(F32) + arrived[0].astype(F32)).astype(BF16)
                down = (down.astype(F32) + arrived[1].astype(F32)).astype(BF16)
            return up, down

        arrived = () if self.up is None else (self.up, self.down)
        up, down = self.order(messages, self.both, *arrived)
        self.up = lax.ppermute(up, "wide", [(w, w + 2) for w in range(2 * t)])
        self.down = lax.ppermute(down, "wide", [(w, w - 2) for w in range(2 * far, 2 * chips)])

    def finish(self):
        while self.result is None:
            self.advance()

    def total(self):
        def add(both, *arrived):
            result = take(both, self.chip).astype(F32)
            for part in arrived:
                result = result + part.astype(F32)
            return result

        arrived = () if self.up is None else (self.up, self.down)
        return self.order(add, self.both, *arrived)


def shards(wide, activations, gain, w_query, w_key, w_value, w_out, cotangent):
    width = HEAD_DIM
    length, features = activations.shape
    chips = wide // 2
    groups = w_key.shape[1] // width
    members = w_query.shape[1] // w_key.shape[1]
    block = BLOCK if length % BLOCK == 0 else length
    span = members * width
    rows = features // wide
    core = lax.axis_index("wide") % 2
    order = Order()

    def columns(g):
        cols = slice(g * span, (g + 1) * span)
        heads = slice(g * width, (g + 1) * width)
        return jnp.concatenate([w_query[:, cols], w_key[:, heads], w_value[:, heads]], axis=1)

    def term(a, b):
        return row_product(a, b).astype(BF16)

    def product(sides, own, other):
        part = order(nn, sides[0], own)
        return order(lambda a, b, c: (c + nn(a, b)).astype(BF16), sides[1], other, part)

    def add_nt(a, b, part):
        return part + nt(a, b)

    def project(mixed, side, part):
        if part is None:
            return order(lambda a, b: nt(a, b).astype(BF16), mixed, side)
        return order(lambda a, b, c: add_nt(a, b, c).astype(BF16), mixed, side, part)

    def start_sum(sides, grads):
        line = LineSum(order, chips)
        line.swap(order(term, sides[1], grads))
        line.add_cores(order(term, sides[0], grads))
        line.advance()
        return line

    qkv_gather = [LineGather(order, chips, columns(g)) for g in range(groups)]
    out_gather = [
        LineGather(order, chips, w_out[:, g * span : (g + 1) * span]) for g in range(groups)
    ]
    qkv_sum, out_sum = [], []
    partial = [None, None]

    qkv_gather[0].hop()
    x_own, x_other, grad_own, grad_other = order(
        lambda a, b, c: norm_and_split(core, a, b, c, chips), activations, gain, cotangent
    )
    x_sides, grad_sides = (x_own, x_other), (grad_own, grad_other)
    out_gather[0].hop()
    qkv_gather[0].hop()
    qkv_gather[0].hop()
    out_gather[0].hop()
    for g in range(groups):
        more = g + 1 < groups
        qkv_gather[g].finish()
        if more:
            qkv_gather[g + 1].hop()
        own, other = qkv_gather[g].halves()
        qkv = product(x_sides, own, other)
        if g:
            qkv_sum[g - 1].advance()
        mixed, lse = order(lambda a: attend_forward(a, members, block), qkv)
        out_gather[g].hop()
        out_sum.append(start_sum(grad_sides, mixed))
        if g:
            qkv_sum[g - 1].finish()
        out_gather[g].finish()
        if more:
            qkv_gather[g + 1].hop()
            out_gather[g + 1].hop()
        own, other = out_gather[g].halves()
        if not more:
            projected = [project(mixed, side, partial[i]) for i, side in enumerate((own, other))]
            summed = [
                lax.psum_scatter(part, "narrow", scatter_dimension=1, tiled=True)
                for part in projected
            ]
        grad_mixed = product(grad_sides, own, other)
        out_sum[g].advance()
        grad_qkv = order(
            lambda a, b, c: attend_backward(a, b, c, members, block), qkv, grad_mixed, lse
        )
        out_sum[g].advance()
        qkv_sum.append(start_sum(x_sides, grad_qkv))
        if more:
            qkv_gather[g + 1].hop()
            partial = [
                order(nt, mixed, side) if part is None else order(add_nt, mixed, side, part)
                for side, part in zip((own, other), partial)
            ]
            qkv_sum[g].advance()
            out_sum[g].finish()
            out_gather[g + 1].hop()
    out_sum[-1].finish()
    qkv_sum[-1].finish()

    own, other = (part.reshape(length, -1, 1, rows) for part in summed)
    summed = jnp.where(
        core == 0,
        jnp.concatenate([own, other], axis=2),
        jnp.concatenate([other, own], axis=2),
    ).reshape(length, -1)
    share = summed.shape[1]
    own_columns = lax.dynamic_slice_in_dim(
        activations, lax.axis_index("narrow") * share, share, 1
    )
    outputs = (own_columns.astype(F32) + summed.astype(F32)).astype(BF16)

    def joined(pieces):
        return pieces[0] if len(pieces) == 1 else jnp.concatenate(pieces, axis=1)

    grad_query = joined([s.result[:, :span] for s in qkv_sum])
    grad_key = joined([s.result[:, span : span + width] for s in qkv_sum])
    grad_value = joined([s.result[:, span + width :] for s in qkv_sum])
    grad_out = joined([s.result for s in out_sum])
    return (outputs, grad_query, grad_key, grad_value, grad_out)


def solution(mesh):
    return jax.shard_map(
        functools.partial(shards, mesh.shape["wide"]),
        mesh=mesh,
        in_specs=(
            P("wide", None),
            P(),
            P("wide", "narrow"),
            P("wide", "narrow"),
            P("wide", "narrow"),
            P("wide", "narrow"),
            P("wide", None),
        ),
        out_specs=(
            P("wide", "narrow"),
            P("wide", "narrow"),
            P("wide", "narrow"),
            P("wide", "narrow"),
            P("wide", "narrow"),
        ),
        check_vma=False,
    )
```

```python
import functools
import jax
import jax.numpy as jnp
from jax import lax
from jax.experimental import pallas as pl
from jax.experimental.pallas import tpu as pltpu
from jax.sharding import PartitionSpec as P

HEAD_DIM = 128
BLOCK = 256
EPSILON = 1e-05
MASKED = -1e30
F32 = jnp.float32
BF16 = jnp.bfloat16


def normalize(rows, gain):
    values32 = rows.astype(F32)
    mean_square = jnp.mean(values32 * values32, axis=-1, keepdims=True)
    return (values32 * lax.rsqrt(mean_square + EPSILON) * gain.astype(F32)).astype(BF16)


def nt(a, b):
    return lax.dot_general(a, b, (((1,), (1,)), ((), ())), preferred_element_type=F32)


def nn(a, b):
    return lax.dot_general(a, b, (((1,), (0,)), ((), ())), preferred_element_type=F32)


def row_product(a, b):
    return lax.dot_general(a, b, (((0,), (0,)), ((), ())), preferred_element_type=F32)


def masked_scores(keys, queries, start, size):
    scores = nt(keys, queries) * HEAD_DIM ** (-0.5)
    key_at = lax.broadcasted_iota(jnp.int32, (size, size), 0)
    query_at = lax.broadcasted_iota(jnp.int32, (size, size), 1)
    last = jnp.where(key_at <= query_at, scores[start:], MASKED)
    if start == 0:
        return last
    return jnp.concatenate([scores[:start], last], axis=0)


def forward_kernel(members, block, qkv_ref, mixed_ref, lse_ref):
    length = qkv_ref.shape[0]
    width = HEAD_DIM
    key_col, value_col = members * width, (members + 1) * width
    values_t = qkv_ref[:, value_col : value_col + width].T
    for h in range(members):
        for start in range(0, length, block):
            stop = start + block
            queries = qkv_ref[start:stop, h * width : (h + 1) * width]
            keys = qkv_ref[:stop, key_col : key_col + width]
            scores = masked_scores(keys, queries, start, block)
            highest = jnp.max(scores, axis=0, keepdims=True)
            exponent = jnp.exp(scores - highest)
            total = jnp.sum(exponent, axis=0, keepdims=True)
            rounded = (exponent * (1.0 / total)).astype(BF16)
            mixed_t = nn(values_t[:, :stop], rounded)
            mixed_ref[start:stop, h * width : (h + 1) * width] = mixed_t.T.astype(BF16)
            lse_ref[h : h + 1, start:stop] = highest + jnp.log(total)


def attend_forward(qkv, members, block):
    length = qkv.shape[0]
    width = HEAD_DIM
    vmem = pl.BlockSpec(memory_space=pltpu.VMEM)
    return pl.pallas_call(
        functools.partial(forward_kernel, members, block),
        out_shape=(
            jax.ShapeDtypeStruct((length, members * width), BF16),
            jax.ShapeDtypeStruct((members, length), F32),
        ),
        in_specs=[vmem],
        out_specs=(vmem, vmem),
        compiler_params=pltpu.CompilerParams(vmem_limit_bytes=40 * 2**20),
        cost_estimate=pl.CostEstimate(
            flops=8 * members * length * length * width,
            bytes_accessed=8 * length * members * width,
            transcendentals=members * length * length,
        ),
        name="attend_forward",
    )(qkv)


def backward_kernel(members, block, qkv_ref, grad_ref, lse_ref, out_ref, gk_ref, gv_ref):
    length = qkv_ref.shape[0]
    width = HEAD_DIM
    key_col, value_col = members * width, (members + 1) * width
    keys_t = qkv_ref[:, key_col : key_col + width].T
    gk_ref[...] = jnp.zeros_like(gk_ref)
    gv_ref[...] = jnp.zeros_like(gv_ref)
    for h in range(members):
        cols = slice(h * width, (h + 1) * width)
        for start in range(0, length, block):
            stop = start + block
            queries = qkv_ref[start:stop, cols]
            grads = grad_ref[start:stop, cols]
            keys = qkv_ref[:stop, key_col : key_col + width]
            values = qkv_ref[:stop, value_col : value_col + width]
            scores = masked_scores(keys, queries, start, block)
            probs = jnp.exp(scores - lse_ref[h : h + 1, start:stop])
            grad_probs = nt(values, grads)
            gv_ref[:stop, :] += nn(probs.astype(BF16), grads)
            inner = jnp.sum(grad_probs * probs, axis=0, keepdims=True)
            grad_scores = (probs * (grad_probs - inner) * width ** (-0.5)).astype(BF16)
            gk_ref[:stop, :] += nn(grad_scores, queries)
            out_ref[start:stop, cols] = nn(keys_t[:, :stop], grad_scores).T.astype(BF16)
    out_ref[:, key_col : key_col + width] = gk_ref[...].astype(BF16)
    out_ref[:, value_col : value_col + width] = gv_ref[...].astype(BF16)


def attend_backward(qkv, grad_mixed, lse, members, block):
    length = qkv.shape[0]
    width = HEAD_DIM
    vmem = pl.BlockSpec(memory_space=pltpu.VMEM)
    return pl.pallas_call(
        functools.partial(backward_kernel, members, block),
        out_shape=jax.ShapeDtypeStruct(qkv.shape, BF16),
        in_specs=[vmem, vmem, vmem],
        out_specs=vmem,
        scratch_shapes=[pltpu.VMEM((length, width), F32), pltpu.VMEM((length, width), F32)],
        compiler_params=pltpu.CompilerParams(vmem_limit_bytes=40 * 2**20),
        cost_estimate=pl.CostEstimate(
            flops=20 * members * length * length * width,
            bytes_accessed=8 * length * members * width,
            transcendentals=members * length * length,
        ),
        name="attend_backward",
    )(qkv, grad_mixed, lse)


def take(blocks, at):
    return lax.dynamic_index_in_dim(blocks, at, 0, keepdims=False)


def split_kernel(chips, core_ref, x_ref, gain_ref, grad_ref, x_own, x_other, grad_own, grad_other):
    features = x_ref.shape[1]
    rows = features // (2 * chips)
    core = core_ref[0]
    total = None
    for w in range(2 * chips):
        values = x_ref[:, w * rows : (w + 1) * rows].astype(F32)
        part = jnp.sum(values * values, axis=-1, keepdims=True)
        total = part if total is None else total + part
    scale = lax.rsqrt(total / features + EPSILON)
    for side, x_out, grad_out in ((core, x_own, grad_own), (1 - core, x_other, grad_other)):
        for chip in range(chips):
            cols = pl.ds(pl.multiple_of((2 * chip + side) * rows, 128), rows)
            to = slice(chip * rows, (chip + 1) * rows)
            x_out[:, to] = (x_ref[:, cols].astype(F32) * scale * gain_ref[:, cols]).astype(BF16)
            grad_out[:, to] = grad_ref[:, cols]


def norm_and_split(core, activations, gain, cotangent, chips):
    length, features = activations.shape
    step = 128 if length % 128 == 0 else length
    whole = pl.BlockSpec((step, features), lambda i: (i, 0))
    half = pl.BlockSpec((step, features // 2), lambda i: (i, 0))
    shape = jax.ShapeDtypeStruct((length, features // 2), BF16)
    return pl.pallas_call(
        functools.partial(split_kernel, chips),
        grid=(length // step,),
        out_shape=(shape,) * 4,
        in_specs=[
            pl.BlockSpec(memory_space=pltpu.SMEM),
            whole,
            pl.BlockSpec((1, features), lambda i: (0, 0)),
            whole,
        ],
        out_specs=(half,) * 4,
        compiler_params=pltpu.CompilerParams(vmem_limit_bytes=32 * 2**20),
        cost_estimate=pl.CostEstimate(
            flops=8 * length * features,
            bytes_accessed=8 * length * features,
            transcendentals=length,
        ),
        name="norm_and_split",
    )(core.reshape(1), activations, gain.astype(F32).reshape(1, -1), cotangent)


def collect_kernel(chips, chip_ref, *refs):
    ups, downs, out = refs[:chips], refs[chips:-1], refs[-1]
    rows = ups[0].shape[0]
    chip = chip_ref[0]

    def store(source, at):
        out[pl.ds(pl.multiple_of(at * rows, rows), rows), :] = source[...]

    store(ups[0], chip)
    for r in range(1, chips):
        pl.when(chip >= r)(functools.partial(store, ups[r], chip - r))
        pl.when(chip < r)(functools.partial(store, downs[chips - r - 1], chip - r + chips))


def collect(chip, chips, ups, downs):
    rows, cols = ups[0].shape
    vmem = pl.BlockSpec(memory_space=pltpu.VMEM)
    return pl.pallas_call(
        functools.partial(collect_kernel, chips),
        out_shape=jax.ShapeDtypeStruct((chips * rows, cols), BF16),
        in_specs=[pl.BlockSpec(memory_space=pltpu.SMEM)] + [vmem] * (len(ups) + len(downs)),
        out_specs=vmem,
        compiler_params=pltpu.CompilerParams(vmem_limit_bytes=24 * 2**20),
        cost_estimate=pl.CostEstimate(
            flops=0, bytes_accessed=6 * chips * rows * cols, transcendentals=0
        ),
        name="collect",
    )(chip.reshape(1), *ups, *downs)


def project_kernel(count, *refs):
    out = refs[-1]
    total = None
    for mixed, side in zip(refs[:count], refs[count : 2 * count]):
        part = nt(mixed[...], side[...])
        total = part if total is None else total + part
    out[...] = total.astype(BF16)


def project(mixed, sides):
    length, span = mixed[0].shape
    features = sides[0].shape[0]
    step = 512 if features % 512 == 0 else features
    count = len(mixed)
    return pl.pallas_call(
        functools.partial(project_kernel, count),
        grid=(features // step,),
        out_shape=jax.ShapeDtypeStruct((length, features), BF16),
        in_specs=[pl.BlockSpec((length, span), lambda i: (0, 0))] * count
        + [pl.BlockSpec((step, span), lambda i: (i, 0))] * count,
        out_specs=pl.BlockSpec((length, step), lambda i: (0, i)),
        compiler_params=pltpu.CompilerParams(vmem_limit_bytes=32 * 2**20),
        cost_estimate=pl.CostEstimate(
            flops=2 * count * length * span * features,
            bytes_accessed=4 * length * features,
            transcendentals=0,
        ),
        name="project",
    )(*mixed, *sides)


class Order:
    def __init__(self):
        self.last = None

    def __call__(self, compute, *operands):
        result = compute(*self.after(*operands))
        self.last = jax.tree.leaves(result)[0]
        return result

    def after(self, *operands):
        if self.last is None:
            return operands
        least = min(range(len(operands)), key=lambda i: operands[i].size)
        tied = lax.optimization_barrier((self.last, operands[least]))[1]
        return operands[:least] + (tied,) + operands[least + 1 :]

    def wait(self, *arrays):
        if self.last is None:
            return arrays
        self.last, *arrays = lax.optimization_barrier((self.last, *arrays))
        return arrays


def swap_cores(array, chips):
    return lax.ppermute(array, "wide", [(w, w ^ 1) for w in range(2 * chips)])


class LineGather:
    def __init__(self, order, chips, piece):
        self.order, self.chips, self.piece = order, chips, piece
        self.chip = lax.axis_index("wide") // 2
        self.ups = []
        self.downs = []

    def hop(self):
        chips, t = self.chips, len(self.ups) or 1
        if not self.ups:
            (self.piece,) = self.order.after(self.piece)
            self.ups = [self.piece]
            up = down = self.piece
        else:
            up, down = self.wait()
        if t >= chips:
            return False
        self.ups.append(
            lax.ppermute(up, "wide", [(w, w + 2) for w in range(2 * (t - 1), 2 * (chips - 1))])
        )
        self.downs.append(
            lax.ppermute(down, "wide", [(w, w - 2) for w in range(2, 2 * (chips - t + 1))])
        )
        return True

    def wait(self):
        if not self.downs:
            return self.piece, self.piece
        self.ups[-1], self.downs[-1] = self.order.wait(self.ups[-1], self.downs[-1])
        return self.ups[-1], self.downs[-1]

    def finish(self):
        while self.hop():
            pass

    def halves(self):
        own = self.order(
            lambda *refs: collect(self.chip, self.chips, refs[: self.chips], refs[self.chips :]),
            *self.ups,
            *self.downs,
        )
        return own, swap_cores(own, self.chips)


class LineSum:
    def __init__(self, order, chips):
        self.order, self.chips = order, chips
        self.chip = lax.axis_index("wide") // 2
        self.up = self.down = self.result = None
        self.hops = 0

    def swap(self, send):
        self.received = swap_cores(send, self.chips)

    def add_cores(self, keep):
        def add(keep, received):
            return (keep.astype(F32) + received.astype(F32)).astype(BF16)

        both = self.order(add, keep, self.received)
        self.both = both.reshape(self.chips, -1, both.shape[-1])

    def advance(self):
        if self.result is not None:
            return
        self.hops += 1
        if self.hops == self.chips:
            self.result = self.total()
            return
        t, chips, chip = self.hops, self.chips, self.chip
        far = chips - t

        def messages(both, *arrived):
            up = take(both, jnp.minimum(chip + far, chips - 1))
            down = take(both, jnp.maximum(chip - far, 0))
            if arrived:
                up = (up.astype(F32) + arrived[0].astype(F32)).astype(BF16)
                down = (down.astype(F32) + arrived[1].astype(F32)).astype(BF16)
            return up, down

        arrived = () if self.up is None else (self.up, self.down)
        up, down = self.order(messages, self.both, *arrived)
        self.up = lax.ppermute(up, "wide", [(w, w + 2) for w in range(2 * t)])
        self.down = lax.ppermute(down, "wide", [(w, w - 2) for w in range(2 * far, 2 * chips)])

    def finish(self):
        while self.result is None:
            self.advance()

    def total(self):
        def add(both, *arrived):
            result = take(both, self.chip).astype(F32)
            for part in arrived:
                result = result + part.astype(F32)
            return result

        arrived = () if self.up is None else (self.up, self.down)
        return self.order(add, self.both, *arrived)


def shards(wide, activations, gain, w_query, w_key, w_value, w_out, cotangent):
    width = HEAD_DIM
    length, features = activations.shape
    chips = wide // 2
    groups = w_key.shape[1] // width
    members = w_query.shape[1] // w_key.shape[1]
    block = BLOCK if length % BLOCK == 0 else length
    span = members * width
    rows = features // wide
    core = lax.axis_index("wide") % 2
    order = Order()

    def columns(g):
        cols = slice(g * span, (g + 1) * span)
        heads = slice(g * width, (g + 1) * width)
        return jnp.concatenate([w_query[:, cols], w_key[:, heads], w_value[:, heads]], axis=1)

    def term(a, b):
        return row_product(a, b).astype(BF16)

    def product(sides, own, other):
        part = order(nn, sides[0], own)
        return order(lambda a, b, c: (c + nn(a, b)).astype(BF16), sides[1], other, part)

    def start_sum(sides, grads, between=None):
        line = LineSum(order, chips)
        line.swap(order(term, sides[1], grads))
        if between is not None:
            between()
        line.add_cores(order(term, sides[0], grads))
        line.advance()
        return line

    def scattered(side):
        sides = [halves[side] for halves in out_weights]
        part = order(lambda *a: project(a[:groups], a[groups:]), *all_mixed, *sides)
        return lax.psum_scatter(part, "narrow", scatter_dimension=1, tiled=True)

    gathers = []
    for g in range(groups):
        gathers.append(LineGather(order, chips, columns(g)))
        gathers.append(LineGather(order, chips, w_out[:, g * span : (g + 1) * span]))

    def hop(k):
        if k < len(gathers):
            gathers[k].hop()

    qkv_sum, out_sum = [], []
    all_mixed, out_weights = [], []

    hop(0)
    x_own, x_other, grad_own, grad_other = order(
        lambda a, b, c: norm_and_split(core, a, b, c, chips), activations, gain, cotangent
    )
    x_sides, grad_sides = (x_own, x_other), (grad_own, grad_other)
    hop(0)
    hop(1)
    hop(0)
    hop(1)
    for g in range(groups):
        a, b = 2 * g, 2 * g + 1
        more = g + 1 < groups
        gathers[a].finish()
        hop(b)
        hop(a + 2)
        own, other = gathers[a].halves()
        qkv = product(x_sides, own, other)
        if g:
            qkv_sum[g - 1].advance()
        mixed, lse = order(lambda a: attend_forward(a, members, block), qkv)
        all_mixed.append(mixed)
        out_sum.append(start_sum(grad_sides, mixed))
        if g:
            qkv_sum[g - 1].advance()
        gathers[b].finish()
        hop(a + 2)
        hop(b + 2)
        out_weights.append(gathers[b].halves())
        own, other = out_weights[g]
        if not more:
            first = scattered(0)
        grad_mixed = product(grad_sides, own, other)
        if g:
            qkv_sum[g - 1].finish()
        out_sum[g].advance()
        grad_qkv = order(
            lambda a, b, c: attend_backward(a, b, c, members, block), qkv, grad_mixed, lse
        )
        hop(a + 2)
        if more:
            qkv_sum.append(start_sum(x_sides, grad_qkv, out_sum[g].advance))
        else:
            second = []
            qkv_sum.append(
                start_sum(x_sides, grad_qkv, lambda: second.append(scattered(1)))
            )
            out_sum[g].advance()
        hop(b + 2)
        out_sum[g].finish()
    qkv_sum[-1].advance()
    grad_out = [line.result for line in out_sum]
    if groups > 1:
        grad_out = order(lambda *a: jnp.concatenate(a, axis=1), *grad_out)
    else:
        grad_out = grad_out[0]
    qkv_sum[-1].advance()

    def finish_outputs(activations, own, other):
        left, right = jnp.where(core == 0, own, other), jnp.where(core == 0, other, own)
        pieces = []
        for at in range(0, own.shape[1], rows):
            pieces += [left[:, at : at + rows], right[:, at : at + rows]]
        summed = jnp.concatenate(pieces, axis=1)
        share = summed.shape[1]
        own_columns = lax.dynamic_slice_in_dim(
            activations, lax.axis_index("narrow") * share, share, 1
        )
        return (own_columns.astype(F32) + summed.astype(F32)).astype(BF16)

    outputs = order(finish_outputs, activations, first, second[0])
    qkv_sum[-1].finish()

    def joined(pieces):
        return pieces[0] if len(pieces) == 1 else jnp.concatenate(pieces, axis=1)

    grad_query = joined([s.result[:, :span] for s in qkv_sum])
    grad_key = joined([s.result[:, span : span + width] for s in qkv_sum])
    grad_value = joined([s.result[:, span + width :] for s in qkv_sum])
    return (outputs, grad_query, grad_key, grad_value, grad_out)


def solution(mesh):
    return jax.shard_map(
        functools.partial(shards, mesh.shape["wide"]),
        mesh=mesh,
        in_specs=(
            P("wide", None),
            P(),
            P("wide", "narrow"),
            P("wide", "narrow"),
            P("wide", "narrow"),
            P("wide", "narrow"),
            P("wide", None),
        ),
        out_specs=(
            P("wide", "narrow"),
            P("wide", "narrow"),
            P("wide", "narrow"),
            P("wide", "narrow"),
            P("wide", "narrow"),
        ),
        check_vma=False,
    )
```

```python
import functools
import jax
import jax.numpy as jnp
from jax import lax
from jax.experimental import pallas as pl
from jax.experimental.pallas import tpu as pltpu
from jax.sharding import PartitionSpec as P

HEAD_DIM = 128
BLOCK = 256
EPSILON = 1e-05
MASKED = -1e30
F32 = jnp.float32
BF16 = jnp.bfloat16
SHORT = pl.CostEstimate(flops=1, bytes_accessed=1, transcendentals=0)


def normalize(rows, gain):
    values32 = rows.astype(F32)
    mean_square = jnp.mean(values32 * values32, axis=-1, keepdims=True)
    return (values32 * lax.rsqrt(mean_square + EPSILON) * gain.astype(F32)).astype(BF16)


def nt(a, b):
    return lax.dot_general(a, b, (((1,), (1,)), ((), ())), preferred_element_type=F32)


def nn(a, b):
    return lax.dot_general(a, b, (((1,), (0,)), ((), ())), preferred_element_type=F32)


def row_product(a, b):
    return lax.dot_general(a, b, (((0,), (0,)), ((), ())), preferred_element_type=F32)


def masked_scores(keys, queries, start, size):
    scores = nt(keys, queries) * HEAD_DIM ** (-0.5)
    key_at = lax.broadcasted_iota(jnp.int32, (size, size), 0)
    query_at = lax.broadcasted_iota(jnp.int32, (size, size), 1)
    last = jnp.where(key_at <= query_at, scores[start:], MASKED)
    if start == 0:
        return last
    return jnp.concatenate([scores[:start], last], axis=0)


def forward_kernel(members, block, qkv_ref, mixed_ref, lse_ref):
    length = qkv_ref.shape[0]
    width = HEAD_DIM
    key_col, value_col = members * width, (members + 1) * width
    values_t = qkv_ref[:, value_col : value_col + width].T
    for h in range(members):
        for start in range(0, length, block):
            stop = start + block
            queries = qkv_ref[start:stop, h * width : (h + 1) * width]
            keys = qkv_ref[:stop, key_col : key_col + width]
            scores = masked_scores(keys, queries, start, block)
            highest = jnp.max(scores, axis=0, keepdims=True)
            exponent = jnp.exp(scores - highest)
            total = jnp.sum(exponent, axis=0, keepdims=True)
            rounded = (exponent * (1.0 / total)).astype(BF16)
            mixed_t = nn(values_t[:, :stop], rounded)
            mixed_ref[start:stop, h * width : (h + 1) * width] = mixed_t.T.astype(BF16)
            lse_ref[h : h + 1, start:stop] = highest + jnp.log(total)


def attend_forward(qkv, members, block):
    length = qkv.shape[0]
    width = HEAD_DIM
    vmem = pl.BlockSpec(memory_space=pltpu.VMEM)
    return pl.pallas_call(
        functools.partial(forward_kernel, members, block),
        out_shape=(
            jax.ShapeDtypeStruct((length, members * width), BF16),
            jax.ShapeDtypeStruct((members, length), F32),
        ),
        in_specs=[vmem],
        out_specs=(vmem, vmem),
        compiler_params=pltpu.CompilerParams(vmem_limit_bytes=40 * 2**20),
        cost_estimate=SHORT,
        name="attend_forward",
    )(qkv)


def backward_kernel(members, block, qkv_ref, grad_ref, lse_ref, out_ref, gk_ref, gv_ref):
    length = qkv_ref.shape[0]
    width = HEAD_DIM
    key_col, value_col = members * width, (members + 1) * width
    keys_t = qkv_ref[:, key_col : key_col + width].T
    gk_ref[...] = jnp.zeros_like(gk_ref)
    gv_ref[...] = jnp.zeros_like(gv_ref)
    for h in range(members):
        cols = slice(h * width, (h + 1) * width)
        for start in range(0, length, block):
            stop = start + block
            queries = qkv_ref[start:stop, cols]
            grads = grad_ref[start:stop, cols]
            keys = qkv_ref[:stop, key_col : key_col + width]
            values = qkv_ref[:stop, value_col : value_col + width]
            scores = masked_scores(keys, queries, start, block)
            probs = jnp.exp(scores - lse_ref[h : h + 1, start:stop])
            grad_probs = nt(values, grads)
            gv_ref[:stop, :] += nn(probs.astype(BF16), grads)
            inner = jnp.sum(grad_probs * probs, axis=0, keepdims=True)
            grad_scores = (probs * (grad_probs - inner) * width ** (-0.5)).astype(BF16)
            gk_ref[:stop, :] += nn(grad_scores, queries)
            out_ref[start:stop, cols] = nn(keys_t[:, :stop], grad_scores).T.astype(BF16)
    out_ref[:, key_col : key_col + width] = gk_ref[...].astype(BF16)
    out_ref[:, value_col : value_col + width] = gv_ref[...].astype(BF16)


def attend_backward(qkv, grad_mixed, lse, members, block):
    length = qkv.shape[0]
    width = HEAD_DIM
    vmem = pl.BlockSpec(memory_space=pltpu.VMEM)
    return pl.pallas_call(
        functools.partial(backward_kernel, members, block),
        out_shape=jax.ShapeDtypeStruct(qkv.shape, BF16),
        in_specs=[vmem, vmem, vmem],
        out_specs=vmem,
        scratch_shapes=[pltpu.VMEM((length, width), F32), pltpu.VMEM((length, width), F32)],
        compiler_params=pltpu.CompilerParams(vmem_limit_bytes=40 * 2**20),
        cost_estimate=SHORT,
        name="attend_backward",
    )(qkv, grad_mixed, lse)


def take(blocks, at):
    return lax.dynamic_index_in_dim(blocks, at, 0, keepdims=False)


def split_kernel(chips, core_ref, x_ref, gain_ref, grad_ref, x_own, x_other, grad_own, grad_other):
    features = x_ref.shape[1]
    rows = features // (2 * chips)
    core = core_ref[0]
    total = None
    for w in range(2 * chips):
        values = x_ref[:, w * rows : (w + 1) * rows].astype(F32)
        part = jnp.sum(values * values, axis=-1, keepdims=True)
        total = part if total is None else total + part
    scale = lax.rsqrt(total / features + EPSILON)
    for side, x_out, grad_out in ((core, x_own, grad_own), (1 - core, x_other, grad_other)):
        for chip in range(chips):
            cols = pl.ds(pl.multiple_of((2 * chip + side) * rows, 128), rows)
            to = slice(chip * rows, (chip + 1) * rows)
            x_out[:, to] = (x_ref[:, cols].astype(F32) * scale * gain_ref[:, cols]).astype(BF16)
            grad_out[:, to] = grad_ref[:, cols]


def norm_and_split(core, activations, gain, cotangent, chips):
    length, features = activations.shape
    step = 128 if length % 128 == 0 else length
    whole = pl.BlockSpec((step, features), lambda i: (i, 0))
    half = pl.BlockSpec((step, features // 2), lambda i: (i, 0))
    shape = jax.ShapeDtypeStruct((length, features // 2), BF16)
    return pl.pallas_call(
        functools.partial(split_kernel, chips),
        grid=(length // step,),
        out_shape=(shape,) * 4,
        in_specs=[
            pl.BlockSpec(memory_space=pltpu.SMEM),
            whole,
            pl.BlockSpec((1, features), lambda i: (0, 0)),
            whole,
        ],
        out_specs=(half,) * 4,
        compiler_params=pltpu.CompilerParams(vmem_limit_bytes=32 * 2**20),
        cost_estimate=SHORT,
        name="norm_and_split",
    )(core.reshape(1), activations, gain.astype(F32).reshape(1, -1), cotangent)


def collect_kernel(chips, chip_ref, *refs):
    ups, downs, out = refs[:chips], refs[chips:-1], refs[-1]
    rows = ups[0].shape[0]
    chip = chip_ref[0]

    def store(source, at):
        out[pl.ds(pl.multiple_of(at * rows, rows), rows), :] = source[...]

    store(ups[0], chip)
    for r in range(1, chips):
        pl.when(chip >= r)(functools.partial(store, ups[r], chip - r))
        pl.when(chip < r)(functools.partial(store, downs[chips - r - 1], chip - r + chips))


def collect(chip, chips, ups, downs):
    rows, cols = ups[0].shape
    vmem = pl.BlockSpec(memory_space=pltpu.VMEM)
    return pl.pallas_call(
        functools.partial(collect_kernel, chips),
        out_shape=jax.ShapeDtypeStruct((chips * rows, cols), BF16),
        in_specs=[pl.BlockSpec(memory_space=pltpu.SMEM)] + [vmem] * (len(ups) + len(downs)),
        out_specs=vmem,
        compiler_params=pltpu.CompilerParams(vmem_limit_bytes=24 * 2**20),
        cost_estimate=SHORT,
        name="collect",
    )(chip.reshape(1), *ups, *downs)


def project_kernel(count, *refs):
    out = refs[-1]
    total = None
    for mixed, side in zip(refs[:count], refs[count : 2 * count]):
        part = nt(mixed[...], side[...])
        total = part if total is None else total + part
    out[...] = total.astype(BF16)


def project(mixed, sides):
    length, span = mixed[0].shape
    features = sides[0].shape[0]
    step = 512 if features % 512 == 0 else features
    count = len(mixed)
    return pl.pallas_call(
        functools.partial(project_kernel, count),
        grid=(features // step,),
        out_shape=jax.ShapeDtypeStruct((length, features), BF16),
        in_specs=[pl.BlockSpec((length, span), lambda i: (0, 0))] * count
        + [pl.BlockSpec((step, span), lambda i: (i, 0))] * count,
        out_specs=pl.BlockSpec((length, step), lambda i: (0, i)),
        compiler_params=pltpu.CompilerParams(vmem_limit_bytes=32 * 2**20),
        cost_estimate=SHORT,
        name="project",
    )(*mixed, *sides)


class Order:
    def __init__(self):
        self.last = None

    def __call__(self, compute, *operands):
        result = compute(*self.after(*operands))
        leaves, form = jax.tree.flatten(result)
        if len(leaves) > 1:
            leaves = lax.optimization_barrier(tuple(leaves))
        self.last = leaves[0]
        return jax.tree.unflatten(form, leaves)

    def after(self, *operands):
        if self.last is None:
            return operands
        least = min(range(len(operands)), key=lambda i: operands[i].size)
        tied = lax.optimization_barrier((self.last, operands[least]))[1]
        return operands[:least] + (tied,) + operands[least + 1 :]

    def wait(self, *arrays):
        if self.last is None:
            return arrays
        arrays = lax.optimization_barrier((self.last, *arrays))[1:]
        self.last = arrays[0]
        return arrays


def swap_cores(array, chips):
    return lax.ppermute(array, "wide", [(w, w ^ 1) for w in range(2 * chips)])


class LineGather:
    def __init__(self, order, chips, piece):
        self.order, self.chips, self.piece = order, chips, piece
        self.chip = lax.axis_index("wide") // 2
        self.ups = []
        self.downs = []

    def hop(self):
        chips, t = self.chips, len(self.ups) or 1
        if not self.ups:
            (self.piece,) = self.order.after(self.piece)
            self.ups = [self.piece]
            up = down = self.piece
        else:
            up, down = self.wait()
        if t >= chips:
            return False
        self.ups.append(
            lax.ppermute(up, "wide", [(w, w + 2) for w in range(2 * (t - 1), 2 * (chips - 1))])
        )
        self.downs.append(
            lax.ppermute(down, "wide", [(w, w - 2) for w in range(2, 2 * (chips - t + 1))])
        )
        return True

    def wait(self):
        if not self.downs:
            return self.piece, self.piece
        self.ups[-1], self.downs[-1] = self.order.wait(self.ups[-1], self.downs[-1])
        return self.ups[-1], self.downs[-1]

    def finish(self):
        while self.hop():
            pass

    def halves(self):
        own = self.order(
            lambda *refs: collect(self.chip, self.chips, refs[: self.chips], refs[self.chips :]),
            *self.ups,
            *self.downs,
        )
        return own, swap_cores(own, self.chips)


class LineSum:
    def __init__(self, order, chips):
        self.order, self.chips = order, chips
        self.chip = lax.axis_index("wide") // 2
        self.up = self.down = self.result = None
        self.hops = 0

    def swap(self, send):
        self.received = swap_cores(send, self.chips)

    def add_cores(self, keep):
        def add(keep, received):
            return (keep.astype(F32) + received.astype(F32)).astype(BF16)

        both = self.order(add, keep, self.received)
        self.both = both.reshape(self.chips, -1, both.shape[-1])

    def advance(self):
        if self.result is not None:
            return
        self.hops += 1
        if self.hops == self.chips:
            self.result = self.total()
            return
        t, chips, chip = self.hops, self.chips, self.chip
        far = chips - t

        def messages(both, *arrived):
            up = take(both, jnp.minimum(chip + far, chips - 1))
            down = take(both, jnp.maximum(chip - far, 0))
            if arrived:
                up = (up.astype(F32) + arrived[0].astype(F32)).astype(BF16)
                down = (down.astype(F32) + arrived[1].astype(F32)).astype(BF16)
            return up, down

        arrived = () if self.up is None else (self.up, self.down)
        up, down = self.order(messages, self.both, *arrived)
        self.up = lax.ppermute(up, "wide", [(w, w + 2) for w in range(2 * t)])
        self.down = lax.ppermute(down, "wide", [(w, w - 2) for w in range(2 * far, 2 * chips)])

    def finish(self):
        while self.result is None:
            self.advance()

    def total(self):
        def add(both, *arrived):
            result = take(both, self.chip).astype(F32)
            for part in arrived:
                result = result + part.astype(F32)
            return result

        arrived = () if self.up is None else (self.up, self.down)
        return self.order(add, self.both, *arrived)


def shards(wide, activations, gain, w_query, w_key, w_value, w_out, cotangent):
    width = HEAD_DIM
    length, features = activations.shape
    chips = wide // 2
    groups = w_key.shape[1] // width
    members = w_query.shape[1] // w_key.shape[1]
    block = BLOCK if length % BLOCK == 0 else length
    span = members * width
    rows = features // wide
    core = lax.axis_index("wide") % 2
    order = Order()

    def columns(g):
        cols = slice(g * span, (g + 1) * span)
        heads = slice(g * width, (g + 1) * width)
        return jnp.concatenate([w_query[:, cols], w_key[:, heads], w_value[:, heads]], axis=1)

    def term(a, b):
        return row_product(a, b).astype(BF16)

    def product(sides, own, other):
        part = order(nn, sides[0], own)
        return order(lambda a, b, c: (c + nn(a, b)).astype(BF16), sides[1], other, part)

    def start_sum(sides, grads, between=None):
        line = LineSum(order, chips)
        line.swap(order(term, sides[1], grads))
        if between is not None:
            between()
        line.add_cores(order(term, sides[0], grads))
        line.advance()
        return line

    def scattered(side):
        sides = [halves[side] for halves in out_weights]
        part = order(lambda *a: project(a[:groups], a[groups:]), *all_mixed, *sides)
        return lax.psum_scatter(part, "narrow", scatter_dimension=1, tiled=True)

    gathers = []
    for g in range(groups):
        gathers.append(LineGather(order, chips, columns(g)))
        gathers.append(LineGather(order, chips, w_out[:, g * span : (g + 1) * span]))

    def hop(k):
        if k < len(gathers):
            gathers[k].hop()

    qkv_sum, out_sum = [], []
    all_mixed, out_weights = [], []

    hop(0)
    x_own, x_other, grad_own, grad_other = order(
        lambda a, b, c: norm_and_split(core, a, b, c, chips), activations, gain, cotangent
    )
    x_sides, grad_sides = (x_own, x_other), (grad_own, grad_other)
    hop(0)
    hop(1)
    hop(0)
    hop(1)
    for g in range(groups):
        a, b = 2 * g, 2 * g + 1
        more = g + 1 < groups
        gathers[a].finish()
        hop(b)
        hop(a + 2)
        own, other = gathers[a].halves()
        qkv = product(x_sides, own, other)
        if g:
            qkv_sum[g - 1].advance()
        mixed, lse = order(lambda a: attend_forward(a, members, block), qkv)
        all_mixed.append(mixed)
        out_sum.append(start_sum(grad_sides, mixed))
        if g:
            qkv_sum[g - 1].advance()
        gathers[b].finish()
        hop(a + 2)
        hop(b + 2)
        out_weights.append(gathers[b].halves())
        own, other = out_weights[g]
        if not more:
            first = scattered(0)
        grad_mixed = product(grad_sides, own, other)
        if g:
            qkv_sum[g - 1].finish()
        out_sum[g].advance()
        grad_qkv = order(
            lambda a, b, c: attend_backward(a, b, c, members, block), qkv, grad_mixed, lse
        )
        hop(a + 2)
        if more:
            qkv_sum.append(start_sum(x_sides, grad_qkv, out_sum[g].advance))
        else:
            second = []
            qkv_sum.append(
                start_sum(x_sides, grad_qkv, lambda: second.append(scattered(1)))
            )
            out_sum[g].advance()
        hop(b + 2)
        out_sum[g].finish()
    qkv_sum[-1].advance()
    grad_out = [line.result for line in out_sum]
    if groups > 1:
        grad_out = order(lambda *a: jnp.concatenate(a, axis=1), *grad_out)
    else:
        grad_out = grad_out[0]
    qkv_sum[-1].advance()

    def finish_outputs(activations, own, other):
        left, right = jnp.where(core == 0, own, other), jnp.where(core == 0, other, own)
        pieces = []
        for at in range(0, own.shape[1], rows):
            pieces += [left[:, at : at + rows], right[:, at : at + rows]]
        summed = jnp.concatenate(pieces, axis=1)
        share = summed.shape[1]
        own_columns = lax.dynamic_slice_in_dim(
            activations, lax.axis_index("narrow") * share, share, 1
        )
        return (own_columns.astype(F32) + summed.astype(F32)).astype(BF16)

    outputs = order(finish_outputs, activations, first, second[0])
    qkv_sum[-1].finish()

    def joined(pieces):
        return pieces[0] if len(pieces) == 1 else jnp.concatenate(pieces, axis=1)

    grad_query = joined([s.result[:, :span] for s in qkv_sum])
    grad_key = joined([s.result[:, span : span + width] for s in qkv_sum])
    grad_value = joined([s.result[:, span + width :] for s in qkv_sum])
    return (outputs, grad_query, grad_key, grad_value, grad_out)


def solution(mesh):
    return jax.shard_map(
        functools.partial(shards, mesh.shape["wide"]),
        mesh=mesh,
        in_specs=(
            P("wide", None),
            P(),
            P("wide", "narrow"),
            P("wide", "narrow"),
            P("wide", "narrow"),
            P("wide", "narrow"),
            P("wide", None),
        ),
        out_specs=(
            P("wide", "narrow"),
            P("wide", "narrow"),
            P("wide", "narrow"),
            P("wide", "narrow"),
            P("wide", "narrow"),
        ),
        check_vma=False,
    )
```

```python
import functools
import jax
import jax.numpy as jnp
from jax import lax
from jax.experimental import pallas as pl
from jax.experimental.pallas import tpu as pltpu
from jax.sharding import PartitionSpec as P

HEAD_DIM = 128
BLOCK = 256
EPSILON = 1e-05
MASKED = -1e30
F32 = jnp.float32
BF16 = jnp.bfloat16
SHORT = pl.CostEstimate(flops=1, bytes_accessed=1, transcendentals=0)


def normalize(rows, gain):
    values32 = rows.astype(F32)
    mean_square = jnp.mean(values32 * values32, axis=-1, keepdims=True)
    return (values32 * lax.rsqrt(mean_square + EPSILON) * gain.astype(F32)).astype(BF16)


def nt(a, b):
    return lax.dot_general(a, b, (((1,), (1,)), ((), ())), preferred_element_type=F32)


def nn(a, b):
    return lax.dot_general(a, b, (((1,), (0,)), ((), ())), preferred_element_type=F32)


def masked_scores(keys, queries, start, size):
    scores = nt(keys, queries) * HEAD_DIM ** (-0.5)
    key_at = lax.broadcasted_iota(jnp.int32, (size, size), 0)
    query_at = lax.broadcasted_iota(jnp.int32, (size, size), 1)
    last = jnp.where(key_at <= query_at, scores[start:], MASKED)
    if start == 0:
        return last
    return jnp.concatenate([scores[:start], last], axis=0)


def forward_kernel(members, block, qkv_ref, mixed_ref, lse_ref):
    length = qkv_ref.shape[0]
    width = HEAD_DIM
    key_col, value_col = members * width, (members + 1) * width
    values_t = qkv_ref[:, value_col : value_col + width].T
    for h in range(members):
        for start in range(0, length, block):
            stop = start + block
            queries = qkv_ref[start:stop, h * width : (h + 1) * width]
            keys = qkv_ref[:stop, key_col : key_col + width]
            scores = masked_scores(keys, queries, start, block)
            highest = jnp.max(scores, axis=0, keepdims=True)
            exponent = jnp.exp(scores - highest)
            total = jnp.sum(exponent, axis=0, keepdims=True)
            rounded = (exponent * (1.0 / total)).astype(BF16)
            mixed_t = nn(values_t[:, :stop], rounded)
            mixed_ref[start:stop, h * width : (h + 1) * width] = mixed_t.T.astype(BF16)
            lse_ref[h : h + 1, start:stop] = highest + jnp.log(total)


def attend_forward(qkv, members, block):
    length = qkv.shape[0]
    width = HEAD_DIM
    vmem = pl.BlockSpec(memory_space=pltpu.VMEM)
    return pl.pallas_call(
        functools.partial(forward_kernel, members, block),
        out_shape=(
            jax.ShapeDtypeStruct((length, members * width), BF16),
            jax.ShapeDtypeStruct((members, length), F32),
        ),
        in_specs=[vmem],
        out_specs=(vmem, vmem),
        compiler_params=pltpu.CompilerParams(vmem_limit_bytes=40 * 2**20),
        cost_estimate=SHORT,
        name="attend_forward",
    )(qkv)


def backward_kernel(members, block, qkv_ref, grad_ref, lse_ref, out_ref, gk_ref, gv_ref):
    length = qkv_ref.shape[0]
    width = HEAD_DIM
    key_col, value_col = members * width, (members + 1) * width
    keys_t = qkv_ref[:, key_col : key_col + width].T
    gk_ref[...] = jnp.zeros_like(gk_ref)
    gv_ref[...] = jnp.zeros_like(gv_ref)
    for h in range(members):
        cols = slice(h * width, (h + 1) * width)
        for start in range(0, length, block):
            stop = start + block
            queries = qkv_ref[start:stop, cols]
            grads = grad_ref[start:stop, cols]
            keys = qkv_ref[:stop, key_col : key_col + width]
            values = qkv_ref[:stop, value_col : value_col + width]
            scores = masked_scores(keys, queries, start, block)
            probs = jnp.exp(scores - lse_ref[h : h + 1, start:stop])
            grad_probs = nt(values, grads)
            gv_ref[:stop, :] += nn(probs.astype(BF16), grads)
            inner = jnp.sum(grad_probs * probs, axis=0, keepdims=True)
            grad_scores = (probs * (grad_probs - inner) * width ** (-0.5)).astype(BF16)
            gk_ref[:stop, :] += nn(grad_scores, queries)
            out_ref[start:stop, cols] = nn(keys_t[:, :stop], grad_scores).T.astype(BF16)
    out_ref[:, key_col : key_col + width] = gk_ref[...].astype(BF16)
    out_ref[:, value_col : value_col + width] = gv_ref[...].astype(BF16)


def attend_backward(qkv, grad_mixed, lse, members, block):
    length = qkv.shape[0]
    width = HEAD_DIM
    vmem = pl.BlockSpec(memory_space=pltpu.VMEM)
    return pl.pallas_call(
        functools.partial(backward_kernel, members, block),
        out_shape=jax.ShapeDtypeStruct(qkv.shape, BF16),
        in_specs=[vmem, vmem, vmem],
        out_specs=vmem,
        scratch_shapes=[pltpu.VMEM((length, width), F32), pltpu.VMEM((length, width), F32)],
        compiler_params=pltpu.CompilerParams(vmem_limit_bytes=40 * 2**20),
        cost_estimate=SHORT,
        name="attend_backward",
    )(qkv, grad_mixed, lse)


def take(blocks, at):
    return lax.dynamic_index_in_dim(blocks, at, 0, keepdims=False)


def split_kernel(chips, core_ref, x_ref, gain_ref, grad_ref, *outs):
    features = x_ref.shape[1]
    rows = features // (2 * chips)
    core = core_ref[0]
    total = None
    for w in range(2 * chips):
        values = x_ref[:, w * rows : (w + 1) * rows].astype(F32)
        part = jnp.sum(values * values, axis=-1, keepdims=True)
        total = part if total is None else total + part
    scale = lax.rsqrt(total / features + EPSILON)
    for side, (x_out, xt_out, grad_out, gradt_out) in ((core, outs[:4]), (1 - core, outs[4:])):
        for chip in range(chips):
            cols = pl.ds(pl.multiple_of((2 * chip + side) * rows, 128), rows)
            to = slice(chip * rows, (chip + 1) * rows)
            normed = (x_ref[:, cols].astype(F32) * scale * gain_ref[:, cols]).astype(BF16)
            x_out[:, to] = normed
            xt_out[to, :] = normed.T
            grad = grad_ref[:, cols]
            grad_out[:, to] = grad
            gradt_out[to, :] = grad.T


def norm_and_split(core, activations, gain, cotangent, chips):
    length, features = activations.shape
    step = 128 if length % 128 == 0 else length
    whole = pl.BlockSpec((step, features), lambda i: (i, 0))
    plain = pl.BlockSpec((step, features // 2), lambda i: (i, 0))
    turned = pl.BlockSpec((features // 2, step), lambda i: (0, i))
    shape = jax.ShapeDtypeStruct((length, features // 2), BF16)
    shape_t = jax.ShapeDtypeStruct((features // 2, length), BF16)
    return pl.pallas_call(
        functools.partial(split_kernel, chips),
        grid=(length // step,),
        out_shape=(shape, shape_t) * 4,
        in_specs=[
            pl.BlockSpec(memory_space=pltpu.SMEM),
            whole,
            pl.BlockSpec((1, features), lambda i: (0, 0)),
            whole,
        ],
        out_specs=(plain, turned) * 4,
        compiler_params=pltpu.CompilerParams(vmem_limit_bytes=32 * 2**20),
        cost_estimate=SHORT,
        name="norm_and_split",
    )(core.reshape(1), activations, gain.astype(F32).reshape(1, -1), cotangent)


def product_kernel(a_own, a_other, w_own, w_other, out, total):
    part = nn(a_own[...], w_own[...]) + nn(a_other[...], w_other[...])
    at = pl.program_id(0)

    @pl.when(at == 0)
    def _():
        total[...] = part

    @pl.when(at > 0)
    def _():
        total[...] += part

    @pl.when(at == pl.num_programs(0) - 1)
    def _():
        out[...] = total[...].astype(BF16)


def product(sides, weights):
    length, depth = sides[0].shape
    cols = weights[0].shape[1]
    step = 512 if depth % 512 == 0 else depth
    left = pl.BlockSpec((length, step), lambda i: (0, i))
    right = pl.BlockSpec((step, cols), lambda i: (i, 0))
    return pl.pallas_call(
        product_kernel,
        grid=(depth // step,),
        out_shape=jax.ShapeDtypeStruct((length, cols), BF16),
        in_specs=[left, left, right, right],
        out_specs=pl.BlockSpec((length, cols), lambda i: (0, 0)),
        scratch_shapes=[pltpu.VMEM((length, cols), F32)],
        compiler_params=pltpu.CompilerParams(vmem_limit_bytes=32 * 2**20),
        cost_estimate=SHORT,
        name="product",
    )(*sides, *weights)


def term_kernel(a, b, out):
    out[...] = nn(a[...], b[...]).astype(BF16)


def term(a, b):
    features, length = a.shape
    cols = b.shape[1]
    step = 512 if features % 512 == 0 else features
    return pl.pallas_call(
        term_kernel,
        grid=(features // step,),
        out_shape=jax.ShapeDtypeStruct((features, cols), BF16),
        in_specs=[
            pl.BlockSpec((step, length), lambda i: (i, 0)),
            pl.BlockSpec((length, cols), lambda i: (0, 0)),
        ],
        out_specs=pl.BlockSpec((step, cols), lambda i: (i, 0)),
        compiler_params=pltpu.CompilerParams(vmem_limit_bytes=32 * 2**20),
        cost_estimate=SHORT,
        name="term",
    )(a, b)


def collect_kernel(chips, chip_ref, *refs):
    ups, downs, out = refs[:chips], refs[chips:-1], refs[-1]
    rows = ups[0].shape[0]
    chip = chip_ref[0]

    def store(source, at):
        out[pl.ds(pl.multiple_of(at * rows, rows), rows), :] = source[...]

    store(ups[0], chip)
    for r in range(1, chips):
        pl.when(chip >= r)(functools.partial(store, ups[r], chip - r))
        pl.when(chip < r)(functools.partial(store, downs[chips - r - 1], chip - r + chips))


def collect(chip, chips, ups, downs):
    rows, cols = ups[0].shape
    vmem = pl.BlockSpec(memory_space=pltpu.VMEM)
    return pl.pallas_call(
        functools.partial(collect_kernel, chips),
        out_shape=jax.ShapeDtypeStruct((chips * rows, cols), BF16),
        in_specs=[pl.BlockSpec(memory_space=pltpu.SMEM)] + [vmem] * (len(ups) + len(downs)),
        out_specs=vmem,
        compiler_params=pltpu.CompilerParams(vmem_limit_bytes=24 * 2**20),
        cost_estimate=SHORT,
        name="collect",
    )(chip.reshape(1), *ups, *downs)


def project_kernel(count, *refs):
    out = refs[-1]
    total = None
    for mixed, side in zip(refs[:count], refs[count : 2 * count]):
        part = nt(mixed[...], side[...])
        total = part if total is None else total + part
    out[...] = total.astype(BF16)


def project(mixed, sides):
    length, span = mixed[0].shape
    features = sides[0].shape[0]
    step = 512 if features % 512 == 0 else features
    count = len(mixed)
    return pl.pallas_call(
        functools.partial(project_kernel, count),
        grid=(features // step,),
        out_shape=jax.ShapeDtypeStruct((length, features), BF16),
        in_specs=[pl.BlockSpec((length, span), lambda i: (0, 0))] * count
        + [pl.BlockSpec((step, span), lambda i: (i, 0))] * count,
        out_specs=pl.BlockSpec((length, step), lambda i: (0, i)),
        compiler_params=pltpu.CompilerParams(vmem_limit_bytes=32 * 2**20),
        cost_estimate=SHORT,
        name="project",
    )(*mixed, *sides)


class Order:
    def __init__(self):
        self.last = None

    def __call__(self, compute, *operands):
        result = compute(*self.after(*operands))
        leaves, form = jax.tree.flatten(result)
        if len(leaves) > 1:
            leaves = lax.optimization_barrier(tuple(leaves))
        self.last = leaves[0]
        return jax.tree.unflatten(form, leaves)

    def after(self, *operands):
        if self.last is None:
            return operands
        least = min(range(len(operands)), key=lambda i: operands[i].size)
        tied = lax.optimization_barrier((self.last, operands[least]))[1]
        return operands[:least] + (tied,) + operands[least + 1 :]

    def wait(self, *arrays):
        if self.last is None:
            return arrays
        arrays = lax.optimization_barrier((self.last, *arrays))[1:]
        self.last = arrays[0]
        return arrays


def swap_cores(array, chips):
    return lax.ppermute(array, "wide", [(w, w ^ 1) for w in range(2 * chips)])


class LineGather:
    def __init__(self, order, chips, piece):
        self.order, self.chips, self.piece = order, chips, piece
        self.chip = lax.axis_index("wide") // 2
        self.ups = []
        self.downs = []

    def hop(self):
        chips, t = self.chips, len(self.ups) or 1
        if not self.ups:
            (self.piece,) = self.order.after(self.piece)
            self.ups = [self.piece]
            up = down = self.piece
        else:
            up, down = self.wait()
        if t >= chips:
            return False
        self.ups.append(
            lax.ppermute(up, "wide", [(w, w + 2) for w in range(2 * (t - 1), 2 * (chips - 1))])
        )
        self.downs.append(
            lax.ppermute(down, "wide", [(w, w - 2) for w in range(2, 2 * (chips - t + 1))])
        )
        return True

    def wait(self):
        if not self.downs:
            return self.piece, self.piece
        self.ups[-1], self.downs[-1] = self.order.wait(self.ups[-1], self.downs[-1])
        return self.ups[-1], self.downs[-1]

    def halves(self):
        own = self.order(
            lambda *refs: collect(self.chip, self.chips, refs[: self.chips], refs[self.chips :]),
            *self.ups,
            *self.downs,
        )
        return own, swap_cores(own, self.chips)


class LineSum:
    def __init__(self, order, chips):
        self.order, self.chips = order, chips
        self.chip = lax.axis_index("wide") // 2
        self.arrived = ()
        self.hops = 0

    def blocks(self, array):
        return array.reshape(self.chips, -1, array.shape[-1])

    def swap(self, send):
        self.received = self.blocks(swap_cores(send, self.chips))

    def hold(self, keep):
        self.keep = self.blocks(keep)

    def advance(self):
        self.hops += 1
        t, chips, chip = self.hops, self.chips, self.chip
        far = chips - t

        def messages(keep, received, *arrived):
            sums = []
            for i, at in enumerate((jnp.minimum(chip + far, chips - 1), jnp.maximum(chip - far, 0))):
                total = take(keep, at).astype(F32) + take(received, at).astype(F32)
                if arrived:
                    total = total + arrived[i].astype(F32)
                sums.append(total.astype(BF16))
            return tuple(sums)

        up, down = self.order(messages, self.keep, self.received, *self.arrived)
        self.arrived = (
            lax.ppermute(up, "wide", [(w, w + 2) for w in range(2 * t)]),
            lax.ppermute(down, "wide", [(w, w - 2) for w in range(2 * far, 2 * chips)]),
        )

    def total(self):
        def add(keep, received, *arrived):
            result = take(keep, self.chip).astype(F32) + take(received, self.chip).astype(F32)
            for part in arrived:
                result = result + part.astype(F32)
            return result

        return self.order(add, self.keep, self.received, *self.arrived)


def plan(groups, chips):
    if (groups, chips) == (2, 4):
        return [(name[0], int(name[1:])) for name in PLAN]
    steps = [("H", 0), ("N", 0)]
    for g in range(groups):
        for k in (2 * g, 2 * g + 1):
            hops = chips - 1 - (k == 0)
            steps += [("H", k)] * hops + [("C", k), ("P", k)]
            steps += [("F", g)] if k % 2 == 0 else [("B", g)]
            steps += [("S", k), ("W", k)] + [("M", k)] * (chips - 1) + [("T", k)]
    return steps + [("J", 0), ("J", 1), ("O", 0)]


PLAN = (
    "H0", "N0", "H1", "H0", "H1", "H0", "H2", "C0", "P0", "F0", "H2", "S0", "W0", "M0",
    "H1", "M0", "H2", "C1", "P1", "M0", "B0", "H3", "S1", "C2", "T0", "W1", "M1", "H3",
    "P2", "F1", "W2", "H3", "M1", "S2", "M2", "C3", "J0", "P3", "M1", "B1", "S3", "M2",
    "W3", "M3", "J1", "T1", "M2", "M3", "T2", "O0", "M3", "T3",
)


def shards(wide, activations, gain, w_query, w_key, w_value, w_out, cotangent):
    width = HEAD_DIM
    length, features = activations.shape
    chips = wide // 2
    groups = w_key.shape[1] // width
    members = w_query.shape[1] // w_key.shape[1]
    block = BLOCK if length % BLOCK == 0 else length
    span = members * width
    rows = features // wide
    core = lax.axis_index("wide") % 2
    order = Order()

    def columns(g):
        cols = slice(g * span, (g + 1) * span)
        heads = slice(g * width, (g + 1) * width)
        return jnp.concatenate([w_query[:, cols], w_key[:, heads], w_value[:, heads]], axis=1)

    gathers = []
    for g in range(groups):
        gathers.append(LineGather(order, chips, columns(g)))
        gathers.append(LineGather(order, chips, w_out[:, g * span : (g + 1) * span]))
    sums = [LineSum(order, chips) for _ in gathers]
    made = {}

    def finish_outputs(activations, own, other):
        left, right = jnp.where(core == 0, own, other), jnp.where(core == 0, other, own)
        pieces = []
        for at in range(0, own.shape[1], rows):
            pieces += [left[:, at : at + rows], right[:, at : at + rows]]
        summed = jnp.concatenate(pieces, axis=1)
        share = summed.shape[1]
        own_columns = lax.dynamic_slice_in_dim(
            activations, lax.axis_index("narrow") * share, share, 1
        )
        return (own_columns.astype(F32) + summed.astype(F32)).astype(BF16)

    def step(name, i):
        g = i // 2
        if name == "N":
            parts = order(
                lambda a, b, c: norm_and_split(core, a, b, c, chips), activations, gain, cotangent
            )
            made["x"], made["grad"] = parts[0::4], parts[2::4]
            made["xt"], made["gradt"] = parts[1::4], parts[3::4]
        elif name == "H":
            gathers[i].hop()
        elif name == "C":
            gathers[i].wait()
            made["w", i] = gathers[i].halves()
        elif name == "P":
            left = made["grad" if i % 2 else "x"]
            made["p", i] = order(
                lambda *a: product(a[:2], a[2:]), *left, *made["w", i]
            )
        elif name == "F":
            made["mixed", i], made["lse", i] = order(
                lambda a: attend_forward(a, members, block), made["p", 2 * i]
            )
        elif name == "B":
            made["back", i] = order(
                lambda a, b, c: attend_backward(a, b, c, members, block),
                made["p", 2 * i],
                made["p", 2 * i + 1],
                made["lse", i],
            )
        elif name in "SW":
            left = made["xt" if i % 2 else "gradt"][name == "S"]
            result = order(term, left, made["back" if i % 2 else "mixed", g])
            if name == "S":
                sums[i].swap(result)
            else:
                sums[i].hold(result)
        elif name == "M":
            sums[i].advance()
        elif name == "T":
            made["sum", i] = sums[i].total()
        elif name == "J":
            mixed = [made["mixed", g] for g in range(groups)]
            halves = [made["w", 2 * g + 1][i] for g in range(groups)]
            part = order(lambda *a: project(a[:groups], a[groups:]), *mixed, *halves)
            made["out", i] = lax.psum_scatter(
                part, "narrow", scatter_dimension=1, tiled=True
            )
        elif name == "O":
            made["out"] = order(finish_outputs, activations, made["out", 0], made["out", 1])

    for name, i in plan(groups, chips):
        step(name, i)
    outputs = made["out"]
    out_sum = [made["sum", 2 * g] for g in range(groups)]
    qkv_sum = [made["sum", 2 * g + 1] for g in range(groups)]

    def joined(pieces):
        return pieces[0] if len(pieces) == 1 else jnp.concatenate(pieces, axis=1)

    grad_query = joined([s[:, :span] for s in qkv_sum])
    grad_key = joined([s[:, span : span + width] for s in qkv_sum])
    grad_value = joined([s[:, span + width :] for s in qkv_sum])
    grad_out = joined(out_sum)
    return (outputs, grad_query, grad_key, grad_value, grad_out)


def solution(mesh):
    return jax.shard_map(
        functools.partial(shards, mesh.shape["wide"]),
        mesh=mesh,
        in_specs=(
            P("wide", None),
            P(),
            P("wide", "narrow"),
            P("wide", "narrow"),
            P("wide", "narrow"),
            P("wide", "narrow"),
            P("wide", None),
        ),
        out_specs=(
            P("wide", "narrow"),
            P("wide", "narrow"),
            P("wide", "narrow"),
            P("wide", "narrow"),
            P("wide", "narrow"),
        ),
        check_vma=False,
    )
```

```python
import functools
import jax
import jax.numpy as jnp
from jax import lax
from jax.experimental import pallas as pl
from jax.experimental.pallas import tpu as pltpu
from jax.sharding import PartitionSpec as P

HEAD_DIM = 128
BLOCK = 256
EPSILON = 1e-05
MASKED = -1e30
F32 = jnp.float32
BF16 = jnp.bfloat16
SHORT = pl.CostEstimate(flops=1, bytes_accessed=1, transcendentals=0)


def normalize(rows, gain):
    values32 = rows.astype(F32)
    mean_square = jnp.mean(values32 * values32, axis=-1, keepdims=True)
    return (values32 * lax.rsqrt(mean_square + EPSILON) * gain.astype(F32)).astype(BF16)


def nt(a, b):
    return lax.dot_general(a, b, (((1,), (1,)), ((), ())), preferred_element_type=F32)


def nn(a, b):
    return lax.dot_general(a, b, (((1,), (0,)), ((), ())), preferred_element_type=F32)


def masked_scores(keys, queries, start, size):
    scores = nt(keys, queries) * HEAD_DIM ** (-0.5)
    key_at = lax.broadcasted_iota(jnp.int32, (size, size), 0)
    query_at = lax.broadcasted_iota(jnp.int32, (size, size), 1)
    last = jnp.where(key_at <= query_at, scores[start:], MASKED)
    if start == 0:
        return last
    return jnp.concatenate([scores[:start], last], axis=0)


def forward_kernel(members, block, qkv_ref, mixed_ref, lse_ref):
    length = qkv_ref.shape[0]
    width = HEAD_DIM
    key_col, value_col = members * width, (members + 1) * width
    values_t = qkv_ref[:, value_col : value_col + width].T
    for h in range(members):
        for start in range(0, length, block):
            stop = start + block
            queries = qkv_ref[start:stop, h * width : (h + 1) * width]
            keys = qkv_ref[:stop, key_col : key_col + width]
            scores = masked_scores(keys, queries, start, block)
            highest = jnp.max(scores, axis=0, keepdims=True)
            exponent = jnp.exp(scores - highest)
            total = jnp.sum(exponent, axis=0, keepdims=True)
            rounded = (exponent * (1.0 / total)).astype(BF16)
            mixed_t = nn(values_t[:, :stop], rounded)
            mixed_ref[start:stop, h * width : (h + 1) * width] = mixed_t.T.astype(BF16)
            lse_ref[h : h + 1, start:stop] = highest + jnp.log(total)


def attend_forward(qkv, members, block):
    length = qkv.shape[0]
    width = HEAD_DIM
    vmem = pl.BlockSpec(memory_space=pltpu.VMEM)
    return pl.pallas_call(
        functools.partial(forward_kernel, members, block),
        out_shape=(
            jax.ShapeDtypeStruct((length, members * width), BF16),
            jax.ShapeDtypeStruct((members, length), F32),
        ),
        in_specs=[vmem],
        out_specs=(vmem, vmem),
        compiler_params=pltpu.CompilerParams(vmem_limit_bytes=40 * 2**20),
        cost_estimate=SHORT,
        name="attend_forward",
    )(qkv)


def backward_kernel(members, block, qkv_ref, grad_ref, lse_ref, out_ref, gk_ref, gv_ref):
    length = qkv_ref.shape[0]
    width = HEAD_DIM
    key_col, value_col = members * width, (members + 1) * width
    keys_t = qkv_ref[:, key_col : key_col + width].T
    gk_ref[...] = jnp.zeros_like(gk_ref)
    gv_ref[...] = jnp.zeros_like(gv_ref)
    for h in range(members):
        cols = slice(h * width, (h + 1) * width)
        for start in range(0, length, block):
            stop = start + block
            queries = qkv_ref[start:stop, cols]
            grads = grad_ref[start:stop, cols]
            keys = qkv_ref[:stop, key_col : key_col + width]
            values = qkv_ref[:stop, value_col : value_col + width]
            scores = masked_scores(keys, queries, start, block)
            probs = jnp.exp(scores - lse_ref[h : h + 1, start:stop])
            grad_probs = nt(values, grads)
            gv_ref[:stop, :] += nn(probs.astype(BF16), grads)
            inner = jnp.sum(grad_probs * probs, axis=0, keepdims=True)
            grad_scores = (probs * (grad_probs - inner) * width ** (-0.5)).astype(BF16)
            gk_ref[:stop, :] += nn(grad_scores, queries)
            out_ref[start:stop, cols] = nn(keys_t[:, :stop], grad_scores).T.astype(BF16)
    out_ref[:, key_col : key_col + width] = gk_ref[...].astype(BF16)
    out_ref[:, value_col : value_col + width] = gv_ref[...].astype(BF16)


def attend_backward(qkv, grad_mixed, lse, members, block):
    length = qkv.shape[0]
    width = HEAD_DIM
    vmem = pl.BlockSpec(memory_space=pltpu.VMEM)
    return pl.pallas_call(
        functools.partial(backward_kernel, members, block),
        out_shape=jax.ShapeDtypeStruct(qkv.shape, BF16),
        in_specs=[vmem, vmem, vmem],
        out_specs=vmem,
        scratch_shapes=[pltpu.VMEM((length, width), F32), pltpu.VMEM((length, width), F32)],
        compiler_params=pltpu.CompilerParams(vmem_limit_bytes=40 * 2**20),
        cost_estimate=SHORT,
        name="attend_backward",
    )(qkv, grad_mixed, lse)


def take(blocks, at):
    return lax.dynamic_index_in_dim(blocks, at, 0, keepdims=False)


def split_kernel(chips, core_ref, x_ref, gain_ref, grad_ref, out, xt_own, gt_own, xt_other, gt_other):
    features = x_ref.shape[1]
    rows = features // (2 * chips)
    core = core_ref[0]
    total = None
    for w in range(2 * chips):
        values = x_ref[:, w * rows : (w + 1) * rows].astype(F32)
        part = jnp.sum(values * values, axis=-1, keepdims=True)
        total = part if total is None else total + part
    scale = lax.rsqrt(total / features + EPSILON)
    for side, xt_out, gt_out in ((core, xt_own, gt_own), (1 - core, xt_other, gt_other)):
        for chip in range(chips):
            cols = pl.ds(pl.multiple_of((2 * chip + side) * rows, 128), rows)
            to = slice(chip * rows, (chip + 1) * rows)
            normed = (x_ref[:, cols].astype(F32) * scale * gain_ref[:, cols]).astype(BF16)
            out[:, cols] = normed
            xt_out[to, :] = normed.T
            gt_out[to, :] = grad_ref[:, cols].T


def norm_and_split(core, activations, gain, cotangent, chips):
    length, features = activations.shape
    step = 128 if length % 128 == 0 else length
    whole = pl.BlockSpec((step, features), lambda i: (i, 0))
    turned = pl.BlockSpec((features // 2, step), lambda i: (0, i))
    shape_t = jax.ShapeDtypeStruct((features // 2, length), BF16)
    return pl.pallas_call(
        functools.partial(split_kernel, chips),
        grid=(length // step,),
        out_shape=(jax.ShapeDtypeStruct((length, features), BF16),) + (shape_t,) * 4,
        in_specs=[
            pl.BlockSpec(memory_space=pltpu.SMEM),
            whole,
            pl.BlockSpec((1, features), lambda i: (0, 0)),
            whole,
        ],
        out_specs=(whole,) + (turned,) * 4,
        compiler_params=pltpu.CompilerParams(vmem_limit_bytes=32 * 2**20),
        cost_estimate=SHORT,
        name="norm_and_split",
    )(core.reshape(1), activations, gain.astype(F32).reshape(1, -1), cotangent)


def product_kernel(a, b, out, total):
    part = nn(a[...], b[...])
    at = pl.program_id(0)

    @pl.when(at == 0)
    def _():
        total[...] = part

    @pl.when(at > 0)
    def _():
        total[...] += part

    @pl.when(at == pl.num_programs(0) - 1)
    def _():
        out[...] = total[...].astype(BF16)


def product(rows, weights):
    length, depth = rows.shape
    cols = weights.shape[1]
    step = 1024 if depth % 1024 == 0 else depth
    return pl.pallas_call(
        product_kernel,
        grid=(depth // step,),
        out_shape=jax.ShapeDtypeStruct((length, cols), BF16),
        in_specs=[
            pl.BlockSpec((length, step), lambda i: (0, i)),
            pl.BlockSpec((step, cols), lambda i: (i, 0)),
        ],
        out_specs=pl.BlockSpec((length, cols), lambda i: (0, 0)),
        scratch_shapes=[pltpu.VMEM((length, cols), F32)],
        compiler_params=pltpu.CompilerParams(vmem_limit_bytes=32 * 2**20),
        cost_estimate=SHORT,
        name="product",
    )(rows, weights)


def term_kernel(a, b, out):
    out[...] = nn(a[...], b[...]).astype(BF16)


def term(a, b):
    features, length = a.shape
    cols = b.shape[1]
    step = 512 if features % 512 == 0 else features
    return pl.pallas_call(
        term_kernel,
        grid=(features // step,),
        out_shape=jax.ShapeDtypeStruct((features, cols), BF16),
        in_specs=[
            pl.BlockSpec((step, length), lambda i: (i, 0)),
            pl.BlockSpec((length, cols), lambda i: (0, 0)),
        ],
        out_specs=pl.BlockSpec((step, cols), lambda i: (i, 0)),
        compiler_params=pltpu.CompilerParams(vmem_limit_bytes=32 * 2**20),
        cost_estimate=SHORT,
        name="term",
    )(a, b)


def project_kernel(count, *refs):
    out = refs[-1]
    total = None
    for mixed, side in zip(refs[:count], refs[count : 2 * count]):
        part = nt(mixed[...], side[...])
        total = part if total is None else total + part
    out[...] = total.astype(BF16)


def project(mixed, sides):
    length, span = mixed[0].shape
    features = sides[0].shape[0]
    step = 512 if features % 512 == 0 else features
    count = len(mixed)
    return pl.pallas_call(
        functools.partial(project_kernel, count),
        grid=(features // step,),
        out_shape=jax.ShapeDtypeStruct((length, features), BF16),
        in_specs=[pl.BlockSpec((length, span), lambda i: (0, 0))] * count
        + [pl.BlockSpec((step, span), lambda i: (i, 0))] * count,
        out_specs=pl.BlockSpec((length, step), lambda i: (0, i)),
        compiler_params=pltpu.CompilerParams(vmem_limit_bytes=32 * 2**20),
        cost_estimate=SHORT,
        name="project",
    )(*mixed, *sides)


class Order:
    def __init__(self):
        self.last = None

    def __call__(self, compute, *operands):
        result = compute(*self.after(*operands))
        leaves, form = jax.tree.flatten(result)
        if len(leaves) > 1:
            leaves = lax.optimization_barrier(tuple(leaves))
        self.last = leaves[0]
        return jax.tree.unflatten(form, leaves)

    def after(self, *operands):
        if self.last is None:
            return operands
        least = min(range(len(operands)), key=lambda i: operands[i].size)
        tied = lax.optimization_barrier((self.last, operands[least]))[1]
        return operands[:least] + (tied,) + operands[least + 1 :]


def swap_cores(array, chips):
    return lax.ppermute(array, "wide", [(w, w ^ 1) for w in range(2 * chips)])


class LineSum:
    def __init__(self, order, chips):
        self.order, self.chips = order, chips
        self.chip = lax.axis_index("wide") // 2
        self.arrived = ()
        self.hops = 0

    def blocks(self, array):
        return array.reshape(self.chips, -1, array.shape[-1])

    def swap(self, send):
        self.received = self.blocks(swap_cores(send, self.chips))

    def hold(self, keep):
        self.keep = self.blocks(keep)

    def advance(self):
        self.hops += 1
        t, chips, chip = self.hops, self.chips, self.chip
        far = chips - t

        def messages(keep, received, *arrived):
            sums = []
            for i, at in enumerate((jnp.minimum(chip + far, chips - 1), jnp.maximum(chip - far, 0))):
                total = take(keep, at).astype(F32) + take(received, at).astype(F32)
                if arrived:
                    total = total + arrived[i].astype(F32)
                sums.append(total.astype(BF16))
            return tuple(sums)

        up, down = self.order(messages, self.keep, self.received, *self.arrived)
        self.arrived = (
            lax.ppermute(up, "wide", [(w, w + 2) for w in range(2 * t)]),
            lax.ppermute(down, "wide", [(w, w - 2) for w in range(2 * far, 2 * chips)]),
        )

    def total(self):
        def add(keep, received, *arrived):
            result = take(keep, self.chip).astype(F32) + take(received, self.chip).astype(F32)
            for part in arrived:
                result = result + part.astype(F32)
            return result

        return self.order(add, self.keep, self.received, *self.arrived)


def plan(groups, chips):
    steps = [("N", 0)]
    under_way = []

    def hops(count):
        for _ in range(count):
            if under_way:
                k = under_way[0]
                steps.append(("M", k))
                left[k] -= 1
                if not left[k]:
                    steps.append(("T", k))
                    under_way.pop(0)

    left = {k: chips - 1 for k in range(2 * groups)}
    for k in range(2 * groups):
        g = k // 2
        steps.append(("P", k))
        if k == 2 * groups - 1:
            steps.append(("J", 0))
        hops(1)
        steps.append(("F", g) if k % 2 == 0 else ("B", g))
        hops(1)
        steps += [("S", k), ("W", k)]
        under_way.append(k)
        hops(1)
        if k < 2 * groups - 1:
            hops(1)
    hops(chips * 2)
    steps.insert(-1, ("O", 0))
    return steps


def shards(wide, activations, gain, w_query, w_key, w_value, w_out, cotangent):
    width = HEAD_DIM
    length, features = activations.shape
    chips = wide // 2
    groups = w_key.shape[1] // width
    members = w_query.shape[1] // w_key.shape[1]
    block = BLOCK if length % BLOCK == 0 else length
    span = members * width
    rows = features // wide
    core = lax.axis_index("wide") % 2
    order = Order()

    def columns(g):
        cols = slice(g * span, (g + 1) * span)
        heads = slice(g * width, (g + 1) * width)
        return jnp.concatenate([w_query[:, cols], w_key[:, heads], w_value[:, heads]], axis=1)

    pieces = []
    for g in range(groups):
        pieces += [columns(g), w_out[:, g * span : (g + 1) * span]]
    weights = []
    for piece in pieces:
        if weights:
            piece = lax.optimization_barrier((pieces[len(weights) - 1], piece))[1]
        pieces[len(weights)] = piece
        weights.append(lax.all_gather(piece, "wide", axis=0, tiled=True))
    sums = [LineSum(order, chips) for _ in weights]
    made = {}

    def finish_outputs(activations, summed):
        share = summed.shape[1]
        own_columns = lax.dynamic_slice_in_dim(
            activations, lax.axis_index("narrow") * share, share, 1
        )
        return (own_columns.astype(F32) + summed.astype(F32)).astype(BF16)

    def step(name, i):
        g = i // 2
        if name == "N":
            parts = order(
                lambda a, b, c: norm_and_split(core, a, b, c, chips), activations, gain, cotangent
            )
            made["x"], made["xt"], made["gradt"] = parts[0], parts[1::2], parts[2::2]
        elif name == "P":
            left = cotangent if i % 2 else made["x"]
            made["p", i] = order(product, left, weights[i])
        elif name == "F":
            made["mixed", i], made["lse", i] = order(
                lambda a: attend_forward(a, members, block), made["p", 2 * i]
            )
        elif name == "B":
            made["back", i] = order(
                lambda a, b, c: attend_backward(a, b, c, members, block),
                made["p", 2 * i],
                made["p", 2 * i + 1],
                made["lse", i],
            )
        elif name in "SW":
            left = made["xt" if i % 2 else "gradt"][name == "S"]
            result = order(term, left, made["back" if i % 2 else "mixed", g])
            if name == "S":
                sums[i].swap(result)
            else:
                sums[i].hold(result)
        elif name == "M":
            sums[i].advance()
        elif name == "T":
            made["sum", i] = sums[i].total()
        elif name == "J":
            mixed = [made["mixed", g] for g in range(groups)]
            part = order(
                lambda *a: project(a[:groups], a[groups:]), *mixed, *weights[1::2]
            )
            made["summed"] = lax.psum_scatter(
                part, "narrow", scatter_dimension=1, tiled=True
            )
        elif name == "O":
            made["out"] = order(finish_outputs, activations, made["summed"])

    for name, i in plan(groups, chips):
        step(name, i)
    outputs = made["out"]
    out_sum = [made["sum", 2 * g] for g in range(groups)]
    qkv_sum = [made["sum", 2 * g + 1] for g in range(groups)]

    def joined(pieces):
        return pieces[0] if len(pieces) == 1 else jnp.concatenate(pieces, axis=1)

    grad_query = joined([s[:, :span] for s in qkv_sum])
    grad_key = joined([s[:, span : span + width] for s in qkv_sum])
    grad_value = joined([s[:, span + width :] for s in qkv_sum])
    grad_out = joined(out_sum)
    return (outputs, grad_query, grad_key, grad_value, grad_out)


def solution(mesh):
    return jax.shard_map(
        functools.partial(shards, mesh.shape["wide"]),
        mesh=mesh,
        in_specs=(
            P("wide", None),
            P(),
            P("wide", "narrow"),
            P("wide", "narrow"),
            P("wide", "narrow"),
            P("wide", "narrow"),
            P("wide", None),
        ),
        out_specs=(
            P("wide", "narrow"),
            P("wide", "narrow"),
            P("wide", "narrow"),
            P("wide", "narrow"),
            P("wide", "narrow"),
        ),
        check_vma=False,
    )
```

```python
import functools
import jax
import jax.numpy as jnp
from jax import lax
from jax.experimental import pallas as pl
from jax.experimental.pallas import tpu as pltpu
from jax.sharding import PartitionSpec as P

HEAD_DIM = 128
BLOCK = 256
EPSILON = 1e-05
MASKED = -1e30
F32 = jnp.float32
BF16 = jnp.bfloat16
SHORT = pl.CostEstimate(flops=1, bytes_accessed=1, transcendentals=0)


def normalize(rows, gain):
    values32 = rows.astype(F32)
    mean_square = jnp.mean(values32 * values32, axis=-1, keepdims=True)
    return (values32 * lax.rsqrt(mean_square + EPSILON) * gain.astype(F32)).astype(BF16)


def nt(a, b):
    return lax.dot_general(a, b, (((1,), (1,)), ((), ())), preferred_element_type=F32)


def nn(a, b):
    return lax.dot_general(a, b, (((1,), (0,)), ((), ())), preferred_element_type=F32)


def masked_scores(keys, queries, start, size):
    scores = nt(keys, queries) * HEAD_DIM ** (-0.5)
    key_at = lax.broadcasted_iota(jnp.int32, (size, size), 0)
    query_at = lax.broadcasted_iota(jnp.int32, (size, size), 1)
    last = jnp.where(key_at <= query_at, scores[start:], MASKED)
    if start == 0:
        return last
    return jnp.concatenate([scores[:start], last], axis=0)


def forward_kernel(members, block, qkv_ref, mixed_ref, lse_ref):
    length = qkv_ref.shape[0]
    width = HEAD_DIM
    key_col, value_col = members * width, (members + 1) * width
    values_t = qkv_ref[:, value_col : value_col + width].T
    for h in range(members):
        for start in range(0, length, block):
            stop = start + block
            queries = qkv_ref[start:stop, h * width : (h + 1) * width]
            keys = qkv_ref[:stop, key_col : key_col + width]
            scores = masked_scores(keys, queries, start, block)
            highest = jnp.max(scores, axis=0, keepdims=True)
            exponent = jnp.exp(scores - highest)
            total = jnp.sum(exponent, axis=0, keepdims=True)
            rounded = (exponent * (1.0 / total)).astype(BF16)
            mixed_t = nn(values_t[:, :stop], rounded)
            mixed_ref[start:stop, h * width : (h + 1) * width] = mixed_t.T.astype(BF16)
            lse_ref[h : h + 1, start:stop] = highest + jnp.log(total)


def attend_forward(qkv, members, block):
    length = qkv.shape[0]
    width = HEAD_DIM
    vmem = pl.BlockSpec(memory_space=pltpu.VMEM)
    return pl.pallas_call(
        functools.partial(forward_kernel, members, block),
        out_shape=(
            jax.ShapeDtypeStruct((length, members * width), BF16),
            jax.ShapeDtypeStruct((members, length), F32),
        ),
        in_specs=[vmem],
        out_specs=(vmem, vmem),
        compiler_params=pltpu.CompilerParams(vmem_limit_bytes=40 * 2**20),
        cost_estimate=SHORT,
        name="attend_forward",
    )(qkv)


def backward_kernel(members, block, qkv_ref, grad_ref, lse_ref, out_ref, gk_ref, gv_ref):
    length = qkv_ref.shape[0]
    width = HEAD_DIM
    key_col, value_col = members * width, (members + 1) * width
    keys_t = qkv_ref[:, key_col : key_col + width].T
    gk_ref[...] = jnp.zeros_like(gk_ref)
    gv_ref[...] = jnp.zeros_like(gv_ref)
    for h in range(members):
        cols = slice(h * width, (h + 1) * width)
        for start in range(0, length, block):
            stop = start + block
            queries = qkv_ref[start:stop, cols]
            grads = grad_ref[start:stop, cols]
            keys = qkv_ref[:stop, key_col : key_col + width]
            values = qkv_ref[:stop, value_col : value_col + width]
            scores = masked_scores(keys, queries, start, block)
            probs = jnp.exp(scores - lse_ref[h : h + 1, start:stop])
            grad_probs = nt(values, grads)
            gv_ref[:stop, :] += nn(probs.astype(BF16), grads)
            inner = jnp.sum(grad_probs * probs, axis=0, keepdims=True)
            grad_scores = (probs * (grad_probs - inner) * width ** (-0.5)).astype(BF16)
            gk_ref[:stop, :] += nn(grad_scores, queries)
            out_ref[start:stop, cols] = nn(keys_t[:, :stop], grad_scores).T.astype(BF16)
    out_ref[:, key_col : key_col + width] = gk_ref[...].astype(BF16)
    out_ref[:, value_col : value_col + width] = gv_ref[...].astype(BF16)


def attend_backward(qkv, grad_mixed, lse, members, block):
    length = qkv.shape[0]
    width = HEAD_DIM
    vmem = pl.BlockSpec(memory_space=pltpu.VMEM)
    return pl.pallas_call(
        functools.partial(backward_kernel, members, block),
        out_shape=jax.ShapeDtypeStruct(qkv.shape, BF16),
        in_specs=[vmem, vmem, vmem],
        out_specs=vmem,
        scratch_shapes=[pltpu.VMEM((length, width), F32), pltpu.VMEM((length, width), F32)],
        compiler_params=pltpu.CompilerParams(vmem_limit_bytes=40 * 2**20),
        cost_estimate=SHORT,
        name="attend_backward",
    )(qkv, grad_mixed, lse)


def take(blocks, at):
    return lax.dynamic_index_in_dim(blocks, at, 0, keepdims=False)


def split_kernel(chips, core_ref, x_ref, gain_ref, grad_ref, *outs):
    features = x_ref.shape[1]
    rows = features // (2 * chips)
    core = core_ref[0]
    total = None
    for w in range(2 * chips):
        values = x_ref[:, w * rows : (w + 1) * rows].astype(F32)
        part = jnp.sum(values * values, axis=-1, keepdims=True)
        total = part if total is None else total + part
    scale = lax.rsqrt(total / features + EPSILON)
    for side, (x_out, xt_out, grad_out, gradt_out) in ((core, outs[:4]), (1 - core, outs[4:])):
        for chip in range(chips):
            cols = pl.ds(pl.multiple_of((2 * chip + side) * rows, 128), rows)
            to = slice(chip * rows, (chip + 1) * rows)
            normed = (x_ref[:, cols].astype(F32) * scale * gain_ref[:, cols]).astype(BF16)
            x_out[:, to] = normed
            xt_out[to, :] = normed.T
            grad = grad_ref[:, cols]
            grad_out[:, to] = grad
            gradt_out[to, :] = grad.T


def norm_and_split(core, activations, gain, cotangent, chips):
    length, features = activations.shape
    step = 128 if length % 128 == 0 else length
    whole = pl.BlockSpec((step, features), lambda i: (i, 0))
    plain = pl.BlockSpec((step, features // 2), lambda i: (i, 0))
    turned = pl.BlockSpec((features // 2, step), lambda i: (0, i))
    shape = jax.ShapeDtypeStruct((length, features // 2), BF16)
    shape_t = jax.ShapeDtypeStruct((features // 2, length), BF16)
    return pl.pallas_call(
        functools.partial(split_kernel, chips),
        grid=(length // step,),
        out_shape=(shape, shape_t) * 4,
        in_specs=[
            pl.BlockSpec(memory_space=pltpu.SMEM),
            whole,
            pl.BlockSpec((1, features), lambda i: (0, 0)),
            whole,
        ],
        out_specs=(plain, turned) * 4,
        compiler_params=pltpu.CompilerParams(vmem_limit_bytes=32 * 2**20),
        cost_estimate=SHORT,
        name="norm_and_split",
    )(core.reshape(1), activations, gain.astype(F32).reshape(1, -1), cotangent)


def product_kernel(a_own, a_other, w_own, w_other, out, total):
    part = nn(a_own[...], w_own[...]) + nn(a_other[...], w_other[...])
    at = pl.program_id(0)

    @pl.when(at == 0)
    def _():
        total[...] = part

    @pl.when(at > 0)
    def _():
        total[...] += part

    @pl.when(at == pl.num_programs(0) - 1)
    def _():
        out[...] = total[...].astype(BF16)


def product(sides, weights):
    length, depth = sides[0].shape
    cols = weights[0].shape[1]
    step = 512 if depth % 512 == 0 else depth
    left = pl.BlockSpec((length, step), lambda i: (0, i))
    right = pl.BlockSpec((step, cols), lambda i: (i, 0))
    return pl.pallas_call(
        product_kernel,
        grid=(depth // step,),
        out_shape=jax.ShapeDtypeStruct((length, cols), BF16),
        in_specs=[left, left, right, right],
        out_specs=pl.BlockSpec((length, cols), lambda i: (0, 0)),
        scratch_shapes=[pltpu.VMEM((length, cols), F32)],
        compiler_params=pltpu.CompilerParams(vmem_limit_bytes=32 * 2**20),
        cost_estimate=SHORT,
        name="product",
    )(*sides, *weights)


def term_kernel(a, b, out):
    out[...] = nn(a[...], b[...]).astype(BF16)


def term(a, b):
    features, length = a.shape
    cols = b.shape[1]
    step = 512 if features % 512 == 0 else features
    return pl.pallas_call(
        term_kernel,
        grid=(features // step,),
        out_shape=jax.ShapeDtypeStruct((features, cols), BF16),
        in_specs=[
            pl.BlockSpec((step, length), lambda i: (i, 0)),
            pl.BlockSpec((length, cols), lambda i: (0, 0)),
        ],
        out_specs=pl.BlockSpec((step, cols), lambda i: (i, 0)),
        compiler_params=pltpu.CompilerParams(vmem_limit_bytes=32 * 2**20),
        cost_estimate=SHORT,
        name="term",
    )(a, b)


def collect_kernel(chips, chip_ref, *refs):
    ups, downs, out = refs[:chips], refs[chips:-1], refs[-1]
    rows = ups[0].shape[0]
    chip = chip_ref[0]

    def store(source, at):
        out[pl.ds(pl.multiple_of(at * rows, rows), rows), :] = source[...]

    store(ups[0], chip)
    for r in range(1, chips):
        pl.when(chip >= r)(functools.partial(store, ups[r], chip - r))
        pl.when(chip < r)(functools.partial(store, downs[chips - r - 1], chip - r + chips))


def collect(chip, chips, ups, downs):
    rows, cols = ups[0].shape
    vmem = pl.BlockSpec(memory_space=pltpu.VMEM)
    return pl.pallas_call(
        functools.partial(collect_kernel, chips),
        out_shape=jax.ShapeDtypeStruct((chips * rows, cols), BF16),
        in_specs=[pl.BlockSpec(memory_space=pltpu.SMEM)] + [vmem] * (len(ups) + len(downs)),
        out_specs=vmem,
        compiler_params=pltpu.CompilerParams(vmem_limit_bytes=24 * 2**20),
        cost_estimate=SHORT,
        name="collect",
    )(chip.reshape(1), *ups, *downs)


def project_kernel(count, *refs):
    out = refs[-1]
    total = None
    for mixed, side in zip(refs[:count], refs[count : 2 * count]):
        part = nt(mixed[...], side[...])
        total = part if total is None else total + part
    out[...] = total.astype(BF16)


def project(mixed, sides):
    length, span = mixed[0].shape
    features = sides[0].shape[0]
    step = 512 if features % 512 == 0 else features
    count = len(mixed)
    return pl.pallas_call(
        functools.partial(project_kernel, count),
        grid=(features // step,),
        out_shape=jax.ShapeDtypeStruct((length, features), BF16),
        in_specs=[pl.BlockSpec((length, span), lambda i: (0, 0))] * count
        + [pl.BlockSpec((step, span), lambda i: (i, 0))] * count,
        out_specs=pl.BlockSpec((length, step), lambda i: (0, i)),
        compiler_params=pltpu.CompilerParams(vmem_limit_bytes=32 * 2**20),
        cost_estimate=SHORT,
        name="project",
    )(*mixed, *sides)


class Order:
    def __init__(self):
        self.last = None

    def __call__(self, compute, *operands):
        result = compute(*self.after(*operands))
        leaves, form = jax.tree.flatten(result)
        if len(leaves) > 1:
            leaves = lax.optimization_barrier(tuple(leaves))
        self.last = leaves[0]
        return jax.tree.unflatten(form, leaves)

    def after(self, *operands):
        if self.last is None:
            return operands
        least = min(range(len(operands)), key=lambda i: operands[i].size)
        tied = lax.optimization_barrier((self.last, operands[least]))[1]
        return operands[:least] + (tied,) + operands[least + 1 :]

    def wait(self, *arrays):
        if not arrays:
            return arrays
        if self.last is None:
            arrays = lax.optimization_barrier(arrays)
        else:
            arrays = lax.optimization_barrier((self.last, *arrays))[1:]
        self.last = arrays[0]
        return arrays


def swap_cores(array, chips):
    return lax.ppermute(array, "wide", [(w, w ^ 1) for w in range(2 * chips)])


class LineGather:
    def __init__(self, order, chips, piece):
        self.order, self.chips, self.piece = order, chips, piece
        self.chip = lax.axis_index("wide") // 2
        self.ups, self.downs = [], []
        self.flying = []

    def hop(self):
        chips = self.chips
        if not self.ups:
            (self.piece,) = self.order.after(self.piece)
            self.ups = [self.piece]
        t = len(self.ups)
        up, down = (self.ups[-1], self.downs[-1]) if t > 1 else (self.piece, self.piece)
        up = lax.ppermute(up, "wide", [(w, w + 2) for w in range(2 * (t - 1), 2 * (chips - 1))])
        down = lax.ppermute(down, "wide", [(w, w - 2) for w in range(2, 2 * (chips - t + 1))])
        self.flying = [up, down]

    def land(self, arrays):
        self.ups.append(arrays[0])
        self.downs.append(arrays[1])

    def halves(self):
        own = self.order(
            lambda *refs: collect(self.chip, self.chips, refs[: self.chips], refs[self.chips :]),
            *self.ups,
            *self.downs,
        )
        return own, swap_cores(own, self.chips)


class LineSum:
    def __init__(self, order, chips):
        self.order, self.chips = order, chips
        self.chip = lax.axis_index("wide") // 2
        self.arrived = ()
        self.flying = []
        self.hops = 0

    def blocks(self, array):
        return array.reshape(self.chips, -1, array.shape[-1])

    def swap(self, send):
        self.flying = [swap_cores(send, self.chips)]

    def hold(self, keep):
        self.keep = self.blocks(keep)

    def advance(self):
        self.hops += 1
        t, chips, chip = self.hops, self.chips, self.chip
        far = chips - t

        def messages(keep, received, *arrived):
            sums = []
            for i, at in enumerate((jnp.minimum(chip + far, chips - 1), jnp.maximum(chip - far, 0))):
                total = take(keep, at).astype(F32) + take(received, at).astype(F32)
                if arrived:
                    total = total + arrived[i].astype(F32)
                sums.append(total.astype(BF16))
            return tuple(sums)

        up, down = self.order(messages, self.keep, self.received, *self.arrived)
        self.flying = [
            lax.ppermute(up, "wide", [(w, w + 2) for w in range(2 * t)]),
            lax.ppermute(down, "wide", [(w, w - 2) for w in range(2 * far, 2 * chips)]),
        ]

    def land(self, arrays):
        if len(arrays) == 1:
            self.received = self.blocks(arrays[0])
        else:
            self.arrived = tuple(arrays)

    def total(self):
        def add(keep, received, *arrived):
            result = take(keep, self.chip).astype(F32) + take(received, self.chip).astype(F32)
            for part in arrived:
                result = result + part.astype(F32)
            return result

        return self.order(add, self.keep, self.received, *self.arrived)


def plan(groups, chips):
    if (groups, chips) == (2, 4):
        return [[(name[0], int(name[1:])) for name in line] for line in ROUNDS]
    rounds = [[("H", 0), ("N", 0)]]
    for k in range(2 * groups):
        rounds += [[("H", k)]] * (chips - 1 - (k == 0))
        steps = [("C", k), ("P", k), ("F", k // 2) if k % 2 == 0 else ("B", k // 2)]
        rounds += [steps, [("S", k), ("W", k)]] + [[("M", k)]] * (chips - 1) + [[("T", k)]]
    return rounds + [[("J", 0), ("J", 1), ("O", 0)]]


ROUNDS = (
    ("H0", "N0"),
    ("H0", "H1"),
    ("H0", "H1"),
    ("H1", "H2", "C0", "P0", "F0"),
    ("H2", "S0", "C1", "W0", "P1"),
    ("H2", "M0", "B0"),
    ("H3", "M0", "C2", "P2", "F1"),
    ("H3", "M0", "S1", "W1"),
    ("H3", "M1", "T0", "S2", "W2"),
    ("M1", "M2", "C3", "J0", "P3", "B1"),
    ("M1", "M2", "S3", "J1", "W3"),
    ("M2", "M3", "T1"),
    ("M3", "T2"),
    ("M3", "O0"),
    ("T3",),
)


def shards(wide, activations, gain, w_query, w_key, w_value, w_out, cotangent):
    width = HEAD_DIM
    length, features = activations.shape
    chips = wide // 2
    groups = w_key.shape[1] // width
    members = w_query.shape[1] // w_key.shape[1]
    block = BLOCK if length % BLOCK == 0 else length
    span = members * width
    rows = features // wide
    core = lax.axis_index("wide") % 2
    order = Order()

    def columns(g):
        cols = slice(g * span, (g + 1) * span)
        heads = slice(g * width, (g + 1) * width)
        return jnp.concatenate([w_query[:, cols], w_key[:, heads], w_value[:, heads]], axis=1)

    gathers = []
    for g in range(groups):
        gathers.append(LineGather(order, chips, columns(g)))
        gathers.append(LineGather(order, chips, w_out[:, g * span : (g + 1) * span]))
    sums = [LineSum(order, chips) for _ in gathers]
    made = {}

    def finish_outputs(activations, own, other):
        left, right = jnp.where(core == 0, own, other), jnp.where(core == 0, other, own)
        pieces = []
        for at in range(0, own.shape[1], rows):
            pieces += [left[:, at : at + rows], right[:, at : at + rows]]
        summed = jnp.concatenate(pieces, axis=1)
        share = summed.shape[1]
        own_columns = lax.dynamic_slice_in_dim(
            activations, lax.axis_index("narrow") * share, share, 1
        )
        return (own_columns.astype(F32) + summed.astype(F32)).astype(BF16)

    def step(name, i):
        g = i // 2
        if name == "N":
            parts = order(
                lambda a, b, c: norm_and_split(core, a, b, c, chips), activations, gain, cotangent
            )
            made["x"], made["grad"] = parts[0::4], parts[2::4]
            made["xt"], made["gradt"] = parts[1::4], parts[3::4]
        elif name == "H":
            gathers[i].hop()
        elif name == "C":
            made["w", i] = gathers[i].halves()
        elif name == "P":
            left = made["grad" if i % 2 else "x"]
            made["p", i] = order(
                lambda *a: product(a[:2], a[2:]), *left, *made["w", i]
            )
        elif name == "F":
            made["mixed", i], made["lse", i] = order(
                lambda a: attend_forward(a, members, block), made["p", 2 * i]
            )
        elif name == "B":
            made["back", i] = order(
                lambda a, b, c: attend_backward(a, b, c, members, block),
                made["p", 2 * i],
                made["p", 2 * i + 1],
                made["lse", i],
            )
        elif name in "SW":
            left = made["xt" if i % 2 else "gradt"][name == "S"]
            result = order(term, left, made["back" if i % 2 else "mixed", g])
            if name == "S":
                sums[i].swap(result)
            else:
                sums[i].hold(result)
        elif name == "M":
            sums[i].advance()
        elif name == "T":
            made["sum", i] = sums[i].total()
        elif name == "J":
            mixed = [made["mixed", g] for g in range(groups)]
            halves = [made["w", 2 * g + 1][i] for g in range(groups)]
            part = order(lambda *a: project(a[:groups], a[groups:]), *mixed, *halves)
            made["out", i] = lax.psum_scatter(
                part, "narrow", scatter_dimension=1, tiled=True
            )
        elif name == "O":
            made["out"] = order(finish_outputs, activations, made["out", 0], made["out", 1])

    for steps in plan(groups, chips):
        for name, i in steps:
            step(name, i)
        lines = [line for line in gathers + sums if line.flying]
        landed = order.wait(*[array for line in lines for array in line.flying])
        for line in lines:
            count = len(line.flying)
            line.land(landed[:count])
            landed, line.flying = landed[count:], []
    outputs = made["out"]
    out_sum = [made["sum", 2 * g] for g in range(groups)]
    qkv_sum = [made["sum", 2 * g + 1] for g in range(groups)]

    def joined(pieces):
        return pieces[0] if len(pieces) == 1 else jnp.concatenate(pieces, axis=1)

    grad_query = joined([s[:, :span] for s in qkv_sum])
    grad_key = joined([s[:, span : span + width] for s in qkv_sum])
    grad_value = joined([s[:, span + width :] for s in qkv_sum])
    grad_out = joined(out_sum)
    return (outputs, grad_query, grad_key, grad_value, grad_out)


def solution(mesh):
    return jax.shard_map(
        functools.partial(shards, mesh.shape["wide"]),
        mesh=mesh,
        in_specs=(
            P("wide", None),
            P(),
            P("wide", "narrow"),
            P("wide", "narrow"),
            P("wide", "narrow"),
            P("wide", "narrow"),
            P("wide", None),
        ),
        out_specs=(
            P("wide", "narrow"),
            P("wide", "narrow"),
            P("wide", "narrow"),
            P("wide", "narrow"),
            P("wide", "narrow"),
        ),
        check_vma=False,
    )
```

```python
import functools
import jax
import jax.numpy as jnp
from jax import lax
from jax.experimental import pallas as pl
from jax.experimental.pallas import tpu as pltpu
from jax.sharding import PartitionSpec as P

HEAD_DIM = 128
BLOCK = 256
EPSILON = 1e-05
MASKED = -1e30
F32 = jnp.float32
BF16 = jnp.bfloat16
VMEM_LIMIT = 60 * 2**20
SHORT = pl.CostEstimate(flops=1, bytes_accessed=1, transcendentals=0)


def nt(a, b):
    return lax.dot_general(a, b, (((1,), (1,)), ((), ())), preferred_element_type=F32)


def nn(a, b):
    return lax.dot_general(a, b, (((1,), (0,)), ((), ())), preferred_element_type=F32)


def masked_scores(keys, queries, start, size):
    scores = nt(keys, queries) * HEAD_DIM ** (-0.5)
    key_at = lax.broadcasted_iota(jnp.int32, (size, size), 0)
    query_at = lax.broadcasted_iota(jnp.int32, (size, size), 1)
    last = jnp.where(key_at <= query_at, scores[start:], MASKED)
    if start == 0:
        return last
    return jnp.concatenate([scores[:start], last], axis=0)


def forward_kernel(members, block, qkv_ref, mixed_ref, lse_ref):
    length = qkv_ref.shape[0]
    width = HEAD_DIM
    key_col, value_col = members * width, (members + 1) * width
    values_t = qkv_ref[:, value_col : value_col + width].T
    for h in range(members):
        for start in range(0, length, block):
            stop = start + block
            queries = qkv_ref[start:stop, h * width : (h + 1) * width]
            keys = qkv_ref[:stop, key_col : key_col + width]
            scores = masked_scores(keys, queries, start, block)
            highest = jnp.max(scores, axis=0, keepdims=True)
            exponent = jnp.exp(scores - highest)
            total = jnp.sum(exponent, axis=0, keepdims=True)
            rounded = (exponent * (1.0 / total)).astype(BF16)
            mixed_t = nn(values_t[:, :stop], rounded)
            mixed_ref[start:stop, h * width : (h + 1) * width] = mixed_t.T.astype(BF16)
            lse_ref[h : h + 1, start:stop] = highest + jnp.log(total)


def attend_forward(qkv, members, block):
    length = qkv.shape[0]
    width = HEAD_DIM
    vmem = pl.BlockSpec(memory_space=pltpu.VMEM)
    return pl.pallas_call(
        functools.partial(forward_kernel, members, block),
        out_shape=(
            jax.ShapeDtypeStruct((length, members * width), BF16),
            jax.ShapeDtypeStruct((members, length), F32),
        ),
        in_specs=[vmem],
        out_specs=(vmem, vmem),
        compiler_params=pltpu.CompilerParams(vmem_limit_bytes=VMEM_LIMIT),
        cost_estimate=SHORT,
        name="attend_forward",
    )(qkv)


def backward_kernel(members, block, qkv_ref, grad_ref, lse_ref, out_ref, gk_ref, gv_ref):
    length = qkv_ref.shape[0]
    width = HEAD_DIM
    key_col, value_col = members * width, (members + 1) * width
    keys_t = qkv_ref[:, key_col : key_col + width].T
    gk_ref[...] = jnp.zeros_like(gk_ref)
    gv_ref[...] = jnp.zeros_like(gv_ref)
    for h in range(members):
        cols = slice(h * width, (h + 1) * width)
        for start in range(0, length, block):
            stop = start + block
            queries = qkv_ref[start:stop, cols]
            grads = grad_ref[start:stop, cols]
            keys = qkv_ref[:stop, key_col : key_col + width]
            values = qkv_ref[:stop, value_col : value_col + width]
            scores = masked_scores(keys, queries, start, block)
            probs = jnp.exp(scores - lse_ref[h : h + 1, start:stop])
            grad_probs = nt(values, grads)
            gv_ref[:stop, :] += nn(probs.astype(BF16), grads)
            inner = jnp.sum(grad_probs * probs, axis=0, keepdims=True)
            grad_scores = (probs * (grad_probs - inner) * width ** (-0.5)).astype(BF16)
            gk_ref[:stop, :] += nn(grad_scores, queries)
            out_ref[start:stop, cols] = nn(keys_t[:, :stop], grad_scores).T.astype(BF16)
    out_ref[:, key_col : key_col + width] = gk_ref[...].astype(BF16)
    out_ref[:, value_col : value_col + width] = gv_ref[...].astype(BF16)


def attend_backward(qkv, grad_mixed, lse, members, block):
    length = qkv.shape[0]
    width = HEAD_DIM
    vmem = pl.BlockSpec(memory_space=pltpu.VMEM)
    return pl.pallas_call(
        functools.partial(backward_kernel, members, block),
        out_shape=jax.ShapeDtypeStruct(qkv.shape, BF16),
        in_specs=[vmem, vmem, vmem],
        out_specs=vmem,
        scratch_shapes=[pltpu.VMEM((length, width), F32), pltpu.VMEM((length, width), F32)],
        compiler_params=pltpu.CompilerParams(vmem_limit_bytes=VMEM_LIMIT),
        cost_estimate=SHORT,
        name="attend_backward",
    )(qkv, grad_mixed, lse)


def pack_kernel(groups, query, key, value, out, first, second):
    width = HEAD_DIM
    span = query.shape[1] // groups
    at = 0

    def put(source, start, cols):
        nonlocal at
        first[:, at : at + cols] = source[:, start : start + cols]
        at += cols

    for g in range(groups):
        put(query, g * span, span)
        put(key, g * width, width)
        put(value, g * width, width)
    if groups > 1:
        put(out, 0, (groups - 1) * span)
    second[...] = out[:, (groups - 1) * span :]


def pack(query, key, value, out):
    rows, cols = query.shape
    groups = key.shape[1] // HEAD_DIM
    span = cols // groups
    early = 2 * cols - span + key.shape[1] + value.shape[1]
    return pl.pallas_call(
        functools.partial(pack_kernel, groups),
        out_shape=(
            jax.ShapeDtypeStruct((rows, early), BF16),
            jax.ShapeDtypeStruct((rows, span), BF16),
        ),
        compiler_params=pltpu.CompilerParams(vmem_limit_bytes=VMEM_LIMIT),
        cost_estimate=SHORT,
        name="pack",
    )(query, key, value, out)


def norm_kernel(x_ref, gain_ref, grad_ref, out, out_t, grad_t):
    features = x_ref.shape[1]
    step = 512 if features % 512 == 0 else features
    total = None
    for at in range(0, features, step):
        values = x_ref[:, at : at + step].astype(F32)
        part = jnp.sum(values * values, axis=-1, keepdims=True)
        total = part if total is None else total + part
    scale = lax.rsqrt(total / features + EPSILON)
    for at in range(0, features, step):
        cols = slice(at, at + step)
        normed = (x_ref[:, cols].astype(F32) * scale * gain_ref[:, cols]).astype(BF16)
        out[:, cols] = normed
        out_t[cols, :] = normed.T
        grad_t[cols, :] = grad_ref[:, cols].T


def normalize(activations, gain, cotangent):
    length, features = activations.shape
    step = 128 if length % 128 == 0 else length
    whole = pl.BlockSpec((step, features), lambda i: (i, 0))
    turned = pl.BlockSpec((features, step), lambda i: (0, i))
    shape_t = jax.ShapeDtypeStruct((features, length), BF16)
    return pl.pallas_call(
        norm_kernel,
        grid=(length // step,),
        out_shape=(jax.ShapeDtypeStruct((length, features), BF16), shape_t, shape_t),
        in_specs=[whole, pl.BlockSpec((1, features), lambda i: (0, 0)), whole],
        out_specs=(whole, turned, turned),
        compiler_params=pltpu.CompilerParams(vmem_limit_bytes=VMEM_LIMIT),
        cost_estimate=SHORT,
        name="normalize",
    )(activations, gain.astype(F32).reshape(1, -1), cotangent)


def product_kernel(a, b, out, total):
    part = nn(a[...], b[...])
    at = pl.program_id(0)

    @pl.when(at == 0)
    def _():
        total[...] = part

    @pl.when(at > 0)
    def _():
        total[...] += part

    @pl.when(at == pl.num_programs(0) - 1)
    def _():
        out[...] = total[...].astype(BF16)


def product(rows, weights, at, cols):
    length, depth = rows.shape
    step = 1024 if depth % 1024 == 0 else depth
    return pl.pallas_call(
        product_kernel,
        grid=(depth // step,),
        out_shape=jax.ShapeDtypeStruct((length, cols), BF16),
        in_specs=[
            pl.BlockSpec((length, step), lambda i: (0, i)),
            pl.BlockSpec((step, cols), lambda i: (i, at)),
        ],
        out_specs=pl.BlockSpec((length, cols), lambda i: (0, 0)),
        scratch_shapes=[pltpu.VMEM((length, cols), F32)],
        compiler_params=pltpu.CompilerParams(vmem_limit_bytes=VMEM_LIMIT),
        cost_estimate=SHORT,
        name="product",
    )(rows, weights)


def terms_kernel(count, *refs):
    lefts, rights, out = refs[:count], refs[count : 2 * count], refs[-1]
    at = 0
    for left, right in zip(lefts, rights):
        cols = right.shape[1]
        out[:, at : at + cols] = nn(left[...], right[...]).astype(BF16)
        at += cols


def terms(lefts, rights):
    features, length = lefts[0].shape
    cols = sum(right.shape[1] for right in rights)
    step = 512 if features % 512 == 0 else features
    count = len(lefts)
    return pl.pallas_call(
        functools.partial(terms_kernel, count),
        grid=(features // step,),
        out_shape=jax.ShapeDtypeStruct((features, cols), BF16),
        in_specs=[pl.BlockSpec((step, length), lambda i: (i, 0))] * count
        + [pl.BlockSpec(right.shape, lambda i: (0, 0)) for right in rights],
        out_specs=pl.BlockSpec((step, cols), lambda i: (i, 0)),
        compiler_params=pltpu.CompilerParams(vmem_limit_bytes=VMEM_LIMIT),
        cost_estimate=SHORT,
        name="terms",
    )(*lefts, *rights)


def project_kernel(count, *refs):
    out = refs[-1]
    total = None
    for mixed, side in zip(refs[:count], refs[count : 2 * count]):
        part = nt(mixed[...], side[...])
        total = part if total is None else total + part
    out[...] = total.astype(BF16)


def project(mixed, sides, places):
    length, span = mixed[0].shape
    features = sides[0].shape[0]
    step = 512 if features % 512 == 0 else features
    count = len(mixed)
    return pl.pallas_call(
        functools.partial(project_kernel, count),
        grid=(features // step,),
        out_shape=jax.ShapeDtypeStruct((length, features), BF16),
        in_specs=[pl.BlockSpec((length, span), lambda i: (0, 0))] * count
        + [pl.BlockSpec((step, span), lambda i, at=at: (i, at)) for at in places],
        out_specs=pl.BlockSpec((length, step), lambda i: (0, i)),
        compiler_params=pltpu.CompilerParams(vmem_limit_bytes=VMEM_LIMIT),
        cost_estimate=SHORT,
        name="project",
    )(*mixed, *sides)


class Order:
    def __init__(self):
        self.last = None

    def __call__(self, compute, *operands):
        result = compute(*self.after(*operands))
        leaves, form = jax.tree.flatten(result)
        if len(leaves) > 1:
            leaves = lax.optimization_barrier(tuple(leaves))
        self.last = leaves[0]
        return jax.tree.unflatten(form, leaves)

    def after(self, *operands):
        if self.last is None:
            return operands
        least = min(range(len(operands)), key=lambda i: operands[i].size)
        tied = lax.optimization_barrier((self.last, operands[least]))[1]
        return operands[:least] + (tied,) + operands[least + 1 :]


def narrow_sum(parts, size):
    own = lax.axis_index("narrow")
    share = parts.shape[1] // size
    even = size & (size - 1) == 0

    def columns_of(device):
        return lax.dynamic_slice_in_dim(parts, device * share, share, 1)

    arrived = []
    for shift in range(1, size):
        to = [n ^ shift if even else (n + shift) % size for n in range(size)]
        mine = own ^ shift if even else (own + shift) % size
        arrived.append(lax.ppermute(columns_of(mine), "narrow", list(enumerate(to))))
    return columns_of(own), arrived


def shards(sizes, activations, gain, w_query, w_key, w_value, w_out, cotangent):
    wide, narrow = sizes
    width = HEAD_DIM
    length, features = activations.shape
    groups = w_key.shape[1] // width
    members = w_query.shape[1] // w_key.shape[1]
    block = BLOCK if length % BLOCK == 0 else length
    span = members * width
    full = span + 2 * width
    order = Order()

    first, second = pack(w_query, w_key, w_value, w_out)
    first = lax.all_gather(first, "wide", axis=0, tiled=True)
    second = lax.all_gather(second, "wide", axis=0, tiled=True)

    def out_place(g):
        if g == groups - 1:
            return second, 0
        at = groups * full + g * span
        if at % span:
            return first[:, at : at + span], 0
        return first, at // span

    normed, normed_t, cotangent_t = order(normalize, activations, gain, cotangent)
    qkv, mixed, lse, back = [], [], [], []

    def backward(g):
        weights, at = out_place(g)
        grad_mixed = order(lambda a, b: product(a, b, at, span), cotangent, weights)
        back.append(
            order(
                lambda a, b, c: attend_backward(a, b, c, members, block),
                qkv[g],
                grad_mixed,
                lse[g],
            )
        )

    for g in range(groups):
        qkv.append(order(lambda a, b: product(a, b, g, full), normed, first))
        rows, stats = order(lambda a: attend_forward(a, members, block), qkv[g])
        mixed.append(rows)
        lse.append(stats)
        if g < groups - 1:
            backward(g)

    def combined(lefts, rights):
        count = len(lefts)
        return order(lambda *a: terms(a[:count], a[count:]), *lefts, *rights)

    def scattered(part):
        return lax.psum_scatter(part, "wide", scatter_dimension=0, tiled=True)

    early = scattered(
        combined([cotangent_t] * groups + [normed_t] * (groups - 1), mixed + back[: groups - 1])
    )
    backward(groups - 1)
    late = combined([normed_t], [back[groups - 1]])
    places = [out_place(g) for g in range(groups)]
    parts = order(
        lambda *a: project(a[:groups], a[groups:], [at for _, at in places]),
        *mixed,
        *[weights for weights, _ in places],
    )
    own, arrived = narrow_sum(parts, narrow)

    def finish_outputs(activations, *parts):
        share = parts[0].shape[1]
        at = lax.axis_index("narrow") * share
        result = lax.dynamic_slice_in_dim(activations, at, share, 1).astype(F32)
        return (result + sum(part.astype(F32) for part in parts)).astype(BF16)

    outputs = order(finish_outputs, activations, own, *arrived)
    outputs, early, late = lax.optimization_barrier((outputs, early, late))
    late = scattered(late)

    grad_out = early[:, : groups * span].astype(F32)
    sums = [
        early[:, groups * span + g * full : groups * span + (g + 1) * full]
        for g in range(groups - 1)
    ] + [late]

    def joined(pieces):
        pieces = [piece.astype(F32) for piece in pieces]
        return pieces[0] if len(pieces) == 1 else jnp.concatenate(pieces, axis=1)

    grad_query = joined([s[:, :span] for s in sums])
    grad_key = joined([s[:, span : span + width] for s in sums])
    grad_value = joined([s[:, span + width :] for s in sums])
    return (outputs, grad_query, grad_key, grad_value, grad_out)


def solution(mesh):
    return jax.shard_map(
        functools.partial(shards, (mesh.shape["wide"], mesh.shape["narrow"])),
        mesh=mesh,
        in_specs=(
            P("wide", None),
            P(),
            P("wide", "narrow"),
            P("wide", "narrow"),
            P("wide", "narrow"),
            P("wide", "narrow"),
            P("wide", None),
        ),
        out_specs=(
            P("wide", "narrow"),
            P("wide", "narrow"),
            P("wide", "narrow"),
            P("wide", "narrow"),
            P("wide", "narrow"),
        ),
        check_vma=False,
    )
```

```python
import functools
import jax
import jax.numpy as jnp
from jax import lax
from jax.experimental import pallas as pl
from jax.experimental.pallas import tpu as pltpu
from jax.sharding import PartitionSpec as P

HEAD_DIM = 128
BLOCK = 256
EPSILON = 1e-05
MASKED = -1e30
F32 = jnp.float32
BF16 = jnp.bfloat16
VMEM_LIMIT = 60 * 2**20
SHORT = pl.CostEstimate(flops=1, bytes_accessed=1, transcendentals=0)


def nt(a, b):
    return lax.dot_general(a, b, (((1,), (1,)), ((), ())), preferred_element_type=F32)


def nn(a, b):
    return lax.dot_general(a, b, (((1,), (0,)), ((), ())), preferred_element_type=F32)


def masked_scores(keys, queries, start, size):
    scores = nt(keys, queries) * HEAD_DIM ** (-0.5)
    key_at = lax.broadcasted_iota(jnp.int32, (size, size), 0)
    query_at = lax.broadcasted_iota(jnp.int32, (size, size), 1)
    last = jnp.where(key_at <= query_at, scores[start:], MASKED)
    if start == 0:
        return last
    return jnp.concatenate([scores[:start], last], axis=0)


def forward_kernel(members, block, qkv_ref, mixed_ref, lse_ref):
    length = qkv_ref.shape[0]
    width = HEAD_DIM
    key_col, value_col = members * width, (members + 1) * width
    values_t = qkv_ref[:, value_col : value_col + width].T
    for h in range(members):
        for start in range(0, length, block):
            stop = start + block
            queries = qkv_ref[start:stop, h * width : (h + 1) * width]
            keys = qkv_ref[:stop, key_col : key_col + width]
            scores = masked_scores(keys, queries, start, block)
            highest = jnp.max(scores, axis=0, keepdims=True)
            exponent = jnp.exp(scores - highest)
            total = jnp.sum(exponent, axis=0, keepdims=True)
            rounded = (exponent * (1.0 / total)).astype(BF16)
            mixed_t = nn(values_t[:, :stop], rounded)
            mixed_ref[start:stop, h * width : (h + 1) * width] = mixed_t.T.astype(BF16)
            lse_ref[h : h + 1, start:stop] = highest + jnp.log(total)


def attend_forward(qkv, members, block):
    length = qkv.shape[0]
    width = HEAD_DIM
    vmem = pl.BlockSpec(memory_space=pltpu.VMEM)
    return pl.pallas_call(
        functools.partial(forward_kernel, members, block),
        out_shape=(
            jax.ShapeDtypeStruct((length, members * width), BF16),
            jax.ShapeDtypeStruct((members, length), F32),
        ),
        in_specs=[vmem],
        out_specs=(vmem, vmem),
        compiler_params=pltpu.CompilerParams(vmem_limit_bytes=VMEM_LIMIT),
        cost_estimate=SHORT,
        name="attend_forward",
    )(qkv)


def backward_kernel(members, block, qkv_ref, grad_ref, lse_ref, out_ref, gk_ref, gv_ref):
    length = qkv_ref.shape[0]
    width = HEAD_DIM
    key_col, value_col = members * width, (members + 1) * width
    keys_t = qkv_ref[:, key_col : key_col + width].T
    gk_ref[...] = jnp.zeros_like(gk_ref)
    gv_ref[...] = jnp.zeros_like(gv_ref)
    for h in range(members):
        cols = slice(h * width, (h + 1) * width)
        for start in range(0, length, block):
            stop = start + block
            queries = qkv_ref[start:stop, cols]
            grads = grad_ref[start:stop, cols]
            keys = qkv_ref[:stop, key_col : key_col + width]
            values = qkv_ref[:stop, value_col : value_col + width]
            scores = masked_scores(keys, queries, start, block)
            probs = jnp.exp(scores - lse_ref[h : h + 1, start:stop])
            grad_probs = nt(values, grads)
            gv_ref[:stop, :] += nn(probs.astype(BF16), grads)
            inner = jnp.sum(grad_probs * probs, axis=0, keepdims=True)
            grad_scores = (probs * (grad_probs - inner) * width ** (-0.5)).astype(BF16)
            gk_ref[:stop, :] += nn(grad_scores, queries)
            out_ref[start:stop, cols] = nn(keys_t[:, :stop], grad_scores).T.astype(BF16)
    out_ref[:, key_col : key_col + width] = gk_ref[...].astype(BF16)
    out_ref[:, value_col : value_col + width] = gv_ref[...].astype(BF16)


def attend_backward(qkv, grad_mixed, lse, members, block):
    length = qkv.shape[0]
    width = HEAD_DIM
    vmem = pl.BlockSpec(memory_space=pltpu.VMEM)
    return pl.pallas_call(
        functools.partial(backward_kernel, members, block),
        out_shape=jax.ShapeDtypeStruct(qkv.shape, BF16),
        in_specs=[vmem, vmem, vmem],
        out_specs=vmem,
        scratch_shapes=[pltpu.VMEM((length, width), F32), pltpu.VMEM((length, width), F32)],
        compiler_params=pltpu.CompilerParams(vmem_limit_bytes=VMEM_LIMIT),
        cost_estimate=SHORT,
        name="attend_backward",
    )(qkv, grad_mixed, lse)


def pack_kernel(groups, query, key, value, out, *packed):
    width = HEAD_DIM
    span = query.shape[1] // groups
    for g, piece in enumerate(packed):
        heads = slice(g * span, (g + 1) * span)
        group = slice(g * width, (g + 1) * width)
        piece[:, :span] = query[:, heads]
        piece[:, span : span + width] = key[:, group]
        piece[:, span + width : span + 2 * width] = value[:, group]
        piece[:, span + 2 * width :] = out[:, heads]


def pack(query, key, value, out):
    rows, cols = query.shape
    groups = key.shape[1] // HEAD_DIM
    wide = 2 * cols // groups + 2 * HEAD_DIM
    return pl.pallas_call(
        functools.partial(pack_kernel, groups),
        out_shape=(jax.ShapeDtypeStruct((rows, wide), BF16),) * groups,
        compiler_params=pltpu.CompilerParams(vmem_limit_bytes=VMEM_LIMIT),
        cost_estimate=SHORT,
        name="pack",
    )(query, key, value, out)


def unpack_kernel(*refs):
    sums, (grad_query, grad_key, grad_value, grad_out) = refs[:-4], refs[-4:]
    width = HEAD_DIM
    span = grad_query.shape[1] // len(sums)
    for g, part in enumerate(sums):
        heads = slice(g * span, (g + 1) * span)
        group = slice(g * width, (g + 1) * width)
        grad_query[:, heads] = part[:, :span].astype(F32)
        grad_key[:, group] = part[:, span : span + width].astype(F32)
        grad_value[:, group] = part[:, span + width : span + 2 * width].astype(F32)
        grad_out[:, heads] = part[:, span + 2 * width :].astype(F32)


def unpack(sums, span):
    rows = sums[0].shape[0]
    groups = len(sums)
    shapes = [
        jax.ShapeDtypeStruct((rows, groups * cols), F32)
        for cols in (span, HEAD_DIM, HEAD_DIM, span)
    ]
    step = 128 if rows % 128 == 0 else rows
    return pl.pallas_call(
        unpack_kernel,
        grid=(rows // step,),
        out_shape=shapes,
        in_specs=[pl.BlockSpec((step, part.shape[1]), lambda i: (i, 0)) for part in sums],
        out_specs=[pl.BlockSpec((step, shape.shape[1]), lambda i: (i, 0)) for shape in shapes],
        compiler_params=pltpu.CompilerParams(vmem_limit_bytes=VMEM_LIMIT),
        cost_estimate=SHORT,
        name="unpack",
    )(*sums)


def norm_kernel(x_ref, gain_ref, grad_ref, out, out_t, grad_t):
    features = x_ref.shape[1]
    step = 512 if features % 512 == 0 else features
    total = None
    for at in range(0, features, step):
        values = x_ref[:, at : at + step].astype(F32)
        part = jnp.sum(values * values, axis=-1, keepdims=True)
        total = part if total is None else total + part
    scale = lax.rsqrt(total / features + EPSILON)
    for at in range(0, features, step):
        cols = slice(at, at + step)
        normed = (x_ref[:, cols].astype(F32) * scale * gain_ref[:, cols]).astype(BF16)
        out[:, cols] = normed
        out_t[cols, :] = normed.T
        grad_t[cols, :] = grad_ref[:, cols].T


def normalize(activations, gain, cotangent):
    length, features = activations.shape
    step = 128 if length % 128 == 0 else length
    whole = pl.BlockSpec((step, features), lambda i: (i, 0))
    turned = pl.BlockSpec((features, step), lambda i: (0, i))
    shape_t = jax.ShapeDtypeStruct((features, length), BF16)
    return pl.pallas_call(
        norm_kernel,
        grid=(length // step,),
        out_shape=(jax.ShapeDtypeStruct((length, features), BF16), shape_t, shape_t),
        in_specs=[whole, pl.BlockSpec((1, features), lambda i: (0, 0)), whole],
        out_specs=(whole, turned, turned),
        compiler_params=pltpu.CompilerParams(vmem_limit_bytes=VMEM_LIMIT),
        cost_estimate=SHORT,
        name="normalize",
    )(activations, gain.astype(F32).reshape(1, -1), cotangent)


def product_kernel(first, a, b, out, total):
    part = nn(a[...], b[:, first : first + out.shape[1]])
    at = pl.program_id(0)

    @pl.when(at == 0)
    def _():
        total[...] = part

    @pl.when(at > 0)
    def _():
        total[...] += part

    @pl.when(at == pl.num_programs(0) - 1)
    def _():
        out[...] = total[...].astype(BF16)


def product(rows, weights, first, cols):
    length, depth = rows.shape
    step = 1024 if depth % 1024 == 0 else depth
    return pl.pallas_call(
        functools.partial(product_kernel, first),
        grid=(depth // step,),
        out_shape=jax.ShapeDtypeStruct((length, cols), BF16),
        in_specs=[
            pl.BlockSpec((length, step), lambda i: (0, i)),
            pl.BlockSpec((step, weights.shape[1]), lambda i: (i, 0)),
        ],
        out_specs=pl.BlockSpec((length, cols), lambda i: (0, 0)),
        scratch_shapes=[pltpu.VMEM((length, cols), F32)],
        compiler_params=pltpu.CompilerParams(vmem_limit_bytes=VMEM_LIMIT),
        cost_estimate=SHORT,
        name="product",
    )(rows, weights)


def terms_kernel(count, *refs):
    lefts, rights, out = refs[:count], refs[count : 2 * count], refs[-1]
    at = 0
    for left, right in zip(lefts, rights):
        cols = right.shape[1]
        out[:, at : at + cols] = nn(left[...], right[...]).astype(BF16)
        at += cols


def terms(lefts, rights):
    features, length = lefts[0].shape
    cols = sum(right.shape[1] for right in rights)
    step = 512 if features % 512 == 0 else features
    count = len(lefts)
    return pl.pallas_call(
        functools.partial(terms_kernel, count),
        grid=(features // step,),
        out_shape=jax.ShapeDtypeStruct((features, cols), BF16),
        in_specs=[pl.BlockSpec((step, length), lambda i: (i, 0))] * count
        + [pl.BlockSpec(right.shape, lambda i: (0, 0)) for right in rights],
        out_specs=pl.BlockSpec((step, cols), lambda i: (i, 0)),
        compiler_params=pltpu.CompilerParams(vmem_limit_bytes=VMEM_LIMIT),
        cost_estimate=SHORT,
        name="terms",
    )(*lefts, *rights)


def project_kernel(count, *refs):
    out = refs[-1]
    total = None
    for mixed, side in zip(refs[:count], refs[count : 2 * count]):
        part = nt(mixed[...], side[:, side.shape[1] - mixed.shape[1] :])
        total = part if total is None else total + part
    out[...] = total.astype(BF16)


def project(mixed, sides):
    length, span = mixed[0].shape
    features = sides[0].shape[0]
    step = 512 if features % 512 == 0 else features
    count = len(mixed)
    return pl.pallas_call(
        functools.partial(project_kernel, count),
        grid=(features // step,),
        out_shape=jax.ShapeDtypeStruct((length, features), BF16),
        in_specs=[pl.BlockSpec((length, span), lambda i: (0, 0))] * count
        + [pl.BlockSpec((step, side.shape[1]), lambda i: (i, 0)) for side in sides],
        out_specs=pl.BlockSpec((length, step), lambda i: (0, i)),
        compiler_params=pltpu.CompilerParams(vmem_limit_bytes=VMEM_LIMIT),
        cost_estimate=SHORT,
        name="project",
    )(*mixed, *sides)


class Order:
    def __init__(self):
        self.last = None

    def __call__(self, compute, *operands):
        result = compute(*self.after(*operands))
        leaves, form = jax.tree.flatten(result)
        if len(leaves) > 1:
            leaves = lax.optimization_barrier(tuple(leaves))
        self.last = leaves[0]
        return jax.tree.unflatten(form, leaves)

    def after(self, *operands):
        if self.last is None:
            return operands
        least = min(range(len(operands)), key=lambda i: operands[i].size)
        tied = lax.optimization_barrier((self.last, operands[least]))[1]
        return operands[:least] + (tied,) + operands[least + 1 :]


def narrow_sum(parts, size):
    own = lax.axis_index("narrow")
    share = parts.shape[1] // size
    even = size & (size - 1) == 0

    def columns_of(device):
        return lax.dynamic_slice_in_dim(parts, device * share, share, 1)

    arrived = []
    for shift in range(1, size):
        to = [n ^ shift if even else (n + shift) % size for n in range(size)]
        mine = own ^ shift if even else (own + shift) % size
        arrived.append(lax.ppermute(columns_of(mine), "narrow", list(enumerate(to))))
    return columns_of(own), arrived


def shards(sizes, activations, gain, w_query, w_key, w_value, w_out, cotangent):
    wide, narrow = sizes
    width = HEAD_DIM
    length, features = activations.shape
    groups = w_key.shape[1] // width
    members = w_query.shape[1] // w_key.shape[1]
    block = BLOCK if length % BLOCK == 0 else length
    span = members * width
    full = span + 2 * width
    order = Order()

    pieces = pack(w_query, w_key, w_value, w_out)
    weights = [lax.all_gather(piece, "wide", axis=0, tiled=True) for piece in pieces]
    normed, normed_t, cotangent_t = order(normalize, activations, gain, cotangent)

    mixed, sums = [], []
    for g in range(groups):
        qkv = order(lambda a, b: product(a, b, 0, full), normed, weights[g])
        rows, lse = order(lambda a: attend_forward(a, members, block), qkv)
        mixed.append(rows)
        grad_mixed = order(lambda a, b: product(a, b, full, span), cotangent, weights[g])
        back = order(
            lambda a, b, c: attend_backward(a, b, c, members, block), qkv, grad_mixed, lse
        )
        part = order(
            lambda *a: terms(a[:2], a[2:]), normed_t, cotangent_t, back, rows
        )
        if g == groups - 1:
            parts = order(
                lambda *a: project(a[:groups], a[groups:]), *mixed, *weights
            )
            own, arrived = narrow_sum(parts, narrow)
        if sums:
            part = lax.optimization_barrier((sums[-1], part))[1]
        sums.append(lax.psum_scatter(part, "wide", scatter_dimension=0, tiled=True))

    def finish_outputs(activations, *parts):
        share = parts[0].shape[1]
        at = lax.axis_index("narrow") * share
        result = lax.dynamic_slice_in_dim(activations, at, share, 1).astype(F32)
        return (result + sum(part.astype(F32) for part in parts)).astype(BF16)

    outputs = order(finish_outputs, activations, own, *arrived)
    grad_query, grad_key, grad_value, grad_out = unpack(sums, span)
    return (outputs, grad_query, grad_key, grad_value, grad_out)


def solution(mesh):
    return jax.shard_map(
        functools.partial(shards, (mesh.shape["wide"], mesh.shape["narrow"])),
        mesh=mesh,
        in_specs=(
            P("wide", None),
            P(),
            P("wide", "narrow"),
            P("wide", "narrow"),
            P("wide", "narrow"),
            P("wide", "narrow"),
            P("wide", None),
        ),
        out_specs=(
            P("wide", "narrow"),
            P("wide", "narrow"),
            P("wide", "narrow"),
            P("wide", "narrow"),
            P("wide", "narrow"),
        ),
        check_vma=False,
    )
```

```python
import functools
import jax
import jax.numpy as jnp
from jax import lax
from jax.experimental import pallas as pl
from jax.experimental.pallas import tpu as pltpu
from jax.sharding import PartitionSpec as P

HEAD_DIM = 128
BLOCK = 256
EPSILON = 1e-05
MASKED = -1e30
F32 = jnp.float32
BF16 = jnp.bfloat16
VMEM_LIMIT = 60 * 2**20
SHORT = pl.CostEstimate(flops=1, bytes_accessed=1, transcendentals=0)


def nt(a, b):
    return lax.dot_general(a, b, (((1,), (1,)), ((), ())), preferred_element_type=F32)


def nn(a, b):
    return lax.dot_general(a, b, (((1,), (0,)), ((), ())), preferred_element_type=F32)


def masked_scores(keys, queries, start, size):
    scores = nt(keys, queries) * HEAD_DIM ** (-0.5)
    key_at = lax.broadcasted_iota(jnp.int32, (size, size), 0)
    query_at = lax.broadcasted_iota(jnp.int32, (size, size), 1)
    last = jnp.where(key_at <= query_at, scores[start:], MASKED)
    if start == 0:
        return last
    return jnp.concatenate([scores[:start], last], axis=0)


def forward_kernel(members, block, qkv_ref, mixed_ref, lse_ref):
    length = qkv_ref.shape[0]
    width = HEAD_DIM
    key_col, value_col = members * width, (members + 1) * width
    values_t = qkv_ref[:, value_col : value_col + width].T
    for h in range(members):
        for start in range(0, length, block):
            stop = start + block
            queries = qkv_ref[start:stop, h * width : (h + 1) * width]
            keys = qkv_ref[:stop, key_col : key_col + width]
            scores = masked_scores(keys, queries, start, block)
            highest = jnp.max(scores, axis=0, keepdims=True)
            exponent = jnp.exp(scores - highest)
            total = jnp.sum(exponent, axis=0, keepdims=True)
            rounded = (exponent * (1.0 / total)).astype(BF16)
            mixed_t = nn(values_t[:, :stop], rounded)
            mixed_ref[start:stop, h * width : (h + 1) * width] = mixed_t.T.astype(BF16)
            lse_ref[h : h + 1, start:stop] = highest + jnp.log(total)


def attend_forward(qkv, members, block):
    length = qkv.shape[0]
    width = HEAD_DIM
    vmem = pl.BlockSpec(memory_space=pltpu.VMEM)
    return pl.pallas_call(
        functools.partial(forward_kernel, members, block),
        out_shape=(
            jax.ShapeDtypeStruct((length, members * width), BF16),
            jax.ShapeDtypeStruct((members, length), F32),
        ),
        in_specs=[vmem],
        out_specs=(vmem, vmem),
        compiler_params=pltpu.CompilerParams(vmem_limit_bytes=VMEM_LIMIT),
        cost_estimate=SHORT,
        name="attend_forward",
    )(qkv)


def backward_kernel(members, block, qkv_ref, grad_ref, lse_ref, out_ref, gk_ref, gv_ref):
    length = qkv_ref.shape[0]
    width = HEAD_DIM
    key_col, value_col = members * width, (members + 1) * width
    keys_t = qkv_ref[:, key_col : key_col + width].T
    gk_ref[...] = jnp.zeros_like(gk_ref)
    gv_ref[...] = jnp.zeros_like(gv_ref)
    for h in range(members):
        cols = slice(h * width, (h + 1) * width)
        for start in range(0, length, block):
            stop = start + block
            queries = qkv_ref[start:stop, cols]
            grads = grad_ref[start:stop, cols]
            keys = qkv_ref[:stop, key_col : key_col + width]
            values = qkv_ref[:stop, value_col : value_col + width]
            scores = masked_scores(keys, queries, start, block)
            probs = jnp.exp(scores - lse_ref[h : h + 1, start:stop])
            grad_probs = nt(values, grads)
            gv_ref[:stop, :] += nn(probs.astype(BF16), grads)
            inner = jnp.sum(grad_probs * probs, axis=0, keepdims=True)
            grad_scores = (probs * (grad_probs - inner) * width ** (-0.5)).astype(BF16)
            gk_ref[:stop, :] += nn(grad_scores, queries)
            out_ref[start:stop, cols] = nn(keys_t[:, :stop], grad_scores).T.astype(BF16)
    out_ref[:, key_col : key_col + width] = gk_ref[...].astype(BF16)
    out_ref[:, value_col : value_col + width] = gv_ref[...].astype(BF16)


def attend_backward(qkv, grad_mixed, lse, members, block):
    length = qkv.shape[0]
    width = HEAD_DIM
    vmem = pl.BlockSpec(memory_space=pltpu.VMEM)
    return pl.pallas_call(
        functools.partial(backward_kernel, members, block),
        out_shape=jax.ShapeDtypeStruct(qkv.shape, BF16),
        in_specs=[vmem, vmem, vmem],
        out_specs=vmem,
        scratch_shapes=[pltpu.VMEM((length, width), F32), pltpu.VMEM((length, width), F32)],
        compiler_params=pltpu.CompilerParams(vmem_limit_bytes=VMEM_LIMIT),
        cost_estimate=SHORT,
        name="attend_backward",
    )(qkv, grad_mixed, lse)


def pack_kernel(groups, query, key, value, out, *packed):
    width = HEAD_DIM
    span = query.shape[1] // groups
    for g, piece in enumerate(packed):
        heads = slice(g * span, (g + 1) * span)
        group = slice(g * width, (g + 1) * width)
        piece[:, :span] = query[:, heads]
        piece[:, span : span + width] = key[:, group]
        piece[:, span + width : span + 2 * width] = value[:, group]
        piece[:, span + 2 * width :] = out[:, heads]


def pack(query, key, value, out):
    rows, cols = query.shape
    groups = key.shape[1] // HEAD_DIM
    wide = 2 * cols // groups + 2 * HEAD_DIM
    return pl.pallas_call(
        functools.partial(pack_kernel, groups),
        out_shape=(jax.ShapeDtypeStruct((rows, wide), BF16),) * groups,
        compiler_params=pltpu.CompilerParams(vmem_limit_bytes=VMEM_LIMIT),
        cost_estimate=SHORT,
        name="pack",
    )(query, key, value, out)


def unpack_kernel(*refs):
    sums, (grad_query, grad_key, grad_value, grad_out) = refs[:-4], refs[-4:]
    width = HEAD_DIM
    span = grad_query.shape[1] // len(sums)
    for g, part in enumerate(sums):
        heads = slice(g * span, (g + 1) * span)
        group = slice(g * width, (g + 1) * width)
        grad_query[:, heads] = part[:, :span].astype(F32)
        grad_key[:, group] = part[:, span : span + width].astype(F32)
        grad_value[:, group] = part[:, span + width : span + 2 * width].astype(F32)
        grad_out[:, heads] = part[:, span + 2 * width :].astype(F32)


def unpack(sums, span):
    rows = sums[0].shape[0]
    groups = len(sums)
    shapes = [
        jax.ShapeDtypeStruct((rows, groups * cols), F32)
        for cols in (span, HEAD_DIM, HEAD_DIM, span)
    ]
    step = 128 if rows % 128 == 0 else rows
    return pl.pallas_call(
        unpack_kernel,
        grid=(rows // step,),
        out_shape=shapes,
        in_specs=[pl.BlockSpec((step, part.shape[1]), lambda i: (i, 0)) for part in sums],
        out_specs=[pl.BlockSpec((step, shape.shape[1]), lambda i: (i, 0)) for shape in shapes],
        compiler_params=pltpu.CompilerParams(vmem_limit_bytes=VMEM_LIMIT),
        cost_estimate=SHORT,
        name="unpack",
    )(*sums)


def norm_kernel(x_ref, gain_ref, grad_ref, out, out_t, grad_t):
    features = x_ref.shape[1]
    step = 512 if features % 512 == 0 else features
    total = None
    for at in range(0, features, step):
        values = x_ref[:, at : at + step].astype(F32)
        part = jnp.sum(values * values, axis=-1, keepdims=True)
        total = part if total is None else total + part
    scale = lax.rsqrt(total / features + EPSILON)
    for at in range(0, features, step):
        cols = slice(at, at + step)
        normed = (x_ref[:, cols].astype(F32) * scale * gain_ref[:, cols]).astype(BF16)
        out[:, cols] = normed
        out_t[cols, :] = normed.T
        grad_t[cols, :] = grad_ref[:, cols].T


def normalize(activations, gain, cotangent):
    length, features = activations.shape
    step = 128 if length % 128 == 0 else length
    whole = pl.BlockSpec((step, features), lambda i: (i, 0))
    turned = pl.BlockSpec((features, step), lambda i: (0, i))
    shape_t = jax.ShapeDtypeStruct((features, length), BF16)
    return pl.pallas_call(
        norm_kernel,
        grid=(length // step,),
        out_shape=(jax.ShapeDtypeStruct((length, features), BF16), shape_t, shape_t),
        in_specs=[whole, pl.BlockSpec((1, features), lambda i: (0, 0)), whole],
        out_specs=(whole, turned, turned),
        compiler_params=pltpu.CompilerParams(vmem_limit_bytes=VMEM_LIMIT),
        cost_estimate=SHORT,
        name="normalize",
    )(activations, gain.astype(F32).reshape(1, -1), cotangent)


def product_kernel(first, a, b, out, total):
    part = nn(a[...], b[:, first : first + out.shape[1]])
    at = pl.program_id(0)

    @pl.when(at == 0)
    def _():
        total[...] = part

    @pl.when(at > 0)
    def _():
        total[...] += part

    @pl.when(at == pl.num_programs(0) - 1)
    def _():
        out[...] = total[...].astype(BF16)


def product(rows, weights, first, cols):
    length, depth = rows.shape
    step = 1024 if depth % 1024 == 0 else depth
    return pl.pallas_call(
        functools.partial(product_kernel, first),
        grid=(depth // step,),
        out_shape=jax.ShapeDtypeStruct((length, cols), BF16),
        in_specs=[
            pl.BlockSpec((length, step), lambda i: (0, i)),
            pl.BlockSpec((step, weights.shape[1]), lambda i: (i, 0)),
        ],
        out_specs=pl.BlockSpec((length, cols), lambda i: (0, 0)),
        scratch_shapes=[pltpu.VMEM((length, cols), F32)],
        compiler_params=pltpu.CompilerParams(vmem_limit_bytes=VMEM_LIMIT),
        cost_estimate=SHORT,
        name="product",
    )(rows, weights)


def terms_kernel(count, *refs):
    lefts, rights, out = refs[:count], refs[count : 2 * count], refs[-1]
    at = 0
    for left, right in zip(lefts, rights):
        cols = right.shape[1]
        out[:, at : at + cols] = nn(left[...], right[...]).astype(BF16)
        at += cols


def terms(lefts, rights):
    features, length = lefts[0].shape
    cols = sum(right.shape[1] for right in rights)
    step = 512 if features % 512 == 0 else features
    count = len(lefts)
    return pl.pallas_call(
        functools.partial(terms_kernel, count),
        grid=(features // step,),
        out_shape=jax.ShapeDtypeStruct((features, cols), BF16),
        in_specs=[pl.BlockSpec((step, length), lambda i: (i, 0))] * count
        + [pl.BlockSpec(right.shape, lambda i: (0, 0)) for right in rights],
        out_specs=pl.BlockSpec((step, cols), lambda i: (i, 0)),
        compiler_params=pltpu.CompilerParams(vmem_limit_bytes=VMEM_LIMIT),
        cost_estimate=SHORT,
        name="terms",
    )(*lefts, *rights)


def side_terms_kernel(count, side, *refs):
    terms_kernel(count, *refs)


def side_terms(side, lefts, rights, wide):
    features, length = lefts[0].shape
    cols = sum(right.shape[1] for right in rights)
    rows = features // wide
    count = len(lefts)
    return pl.pallas_call(
        functools.partial(side_terms_kernel, count),
        grid_spec=pltpu.PrefetchScalarGridSpec(
            num_scalar_prefetch=1,
            grid=(wide // 2,),
            in_specs=[pl.BlockSpec((rows, length), lambda i, side: (2 * i + side[0], 0))] * count
            + [pl.BlockSpec(right.shape, lambda i, side: (0, 0)) for right in rights],
            out_specs=pl.BlockSpec((rows, cols), lambda i, side: (i, 0)),
        ),
        out_shape=jax.ShapeDtypeStruct((features // 2, cols), BF16),
        compiler_params=pltpu.CompilerParams(vmem_limit_bytes=VMEM_LIMIT),
        cost_estimate=SHORT,
        name="side_terms",
    )(side.reshape(1), *lefts, *rights)


def project_kernel(count, *refs):
    out = refs[-1]
    total = None
    for mixed, side in zip(refs[:count], refs[count : 2 * count]):
        part = nt(mixed[...], side[:, side.shape[1] - mixed.shape[1] :])
        total = part if total is None else total + part
    out[...] = total.astype(BF16)


def project(mixed, sides):
    length, span = mixed[0].shape
    features = sides[0].shape[0]
    step = 512 if features % 512 == 0 else features
    count = len(mixed)
    return pl.pallas_call(
        functools.partial(project_kernel, count),
        grid=(features // step,),
        out_shape=jax.ShapeDtypeStruct((length, features), BF16),
        in_specs=[pl.BlockSpec((length, span), lambda i: (0, 0))] * count
        + [pl.BlockSpec((step, side.shape[1]), lambda i: (i, 0)) for side in sides],
        out_specs=pl.BlockSpec((length, step), lambda i: (0, i)),
        compiler_params=pltpu.CompilerParams(vmem_limit_bytes=VMEM_LIMIT),
        cost_estimate=SHORT,
        name="project",
    )(*mixed, *sides)


class Order:
    def __init__(self):
        self.last = None

    def __call__(self, compute, *operands):
        result = compute(*self.after(*operands))
        leaves, form = jax.tree.flatten(result)
        if len(leaves) > 1:
            leaves = lax.optimization_barrier(tuple(leaves))
        self.last = leaves[0]
        return jax.tree.unflatten(form, leaves)

    def after(self, *operands):
        if self.last is None:
            return operands
        least = min(range(len(operands)), key=lambda i: operands[i].size)
        tied = lax.optimization_barrier((self.last, operands[least]))[1]
        return operands[:least] + (tied,) + operands[least + 1 :]


def take(blocks, at):
    return lax.dynamic_index_in_dim(blocks, at, 0, keepdims=False)


def swap_cores(array, chips):
    return lax.ppermute(array, "wide", [(w, w ^ 1) for w in range(2 * chips)])


class LineSum:
    def __init__(self, order, chips):
        self.order, self.chips = order, chips
        self.chip = lax.axis_index("wide") // 2
        self.arrived = ()
        self.hops = 0

    def blocks(self, array):
        return array.reshape(self.chips, -1, array.shape[-1])

    def swap(self, send):
        self.received = self.blocks(swap_cores(send, self.chips))

    def hold(self, keep):
        self.keep = self.blocks(keep)

    def advance(self):
        self.hops += 1
        t, chips, chip = self.hops, self.chips, self.chip
        far = chips - t

        def messages(keep, received, *arrived):
            sums = []
            for i, at in enumerate((jnp.minimum(chip + far, chips - 1), jnp.maximum(chip - far, 0))):
                total = take(keep, at).astype(F32) + take(received, at).astype(F32)
                if arrived:
                    total = total + arrived[i].astype(F32)
                sums.append(total.astype(BF16))
            return tuple(sums)

        up, down = self.order(messages, self.keep, self.received, *self.arrived)
        self.arrived = (
            lax.ppermute(up, "wide", [(w, w + 2) for w in range(2 * t)]),
            lax.ppermute(down, "wide", [(w, w - 2) for w in range(2 * far, 2 * chips)]),
        )

    def total(self):
        def add(keep, received, *arrived):
            result = take(keep, self.chip).astype(F32) + take(received, self.chip).astype(F32)
            for part in arrived:
                result = result + part.astype(F32)
            return result

        return self.order(add, self.keep, self.received, *self.arrived)


def narrow_sum(parts, size):
    own = lax.axis_index("narrow")
    share = parts.shape[1] // size
    even = size & (size - 1) == 0

    def columns_of(device):
        return lax.dynamic_slice_in_dim(parts, device * share, share, 1)

    arrived = []
    for shift in range(1, size):
        to = [n ^ shift if even else (n + shift) % size for n in range(size)]
        mine = own ^ shift if even else (own + shift) % size
        arrived.append(lax.ppermute(columns_of(mine), "narrow", list(enumerate(to))))
    return columns_of(own), arrived


def shards(sizes, activations, gain, w_query, w_key, w_value, w_out, cotangent):
    wide, narrow = sizes
    width = HEAD_DIM
    length, features = activations.shape
    groups = w_key.shape[1] // width
    members = w_query.shape[1] // w_key.shape[1]
    block = BLOCK if length % BLOCK == 0 else length
    span = members * width
    full = span + 2 * width
    order = Order()

    pieces = pack(w_query, w_key, w_value, w_out)
    weights = [lax.all_gather(piece, "wide", axis=0, tiled=True) for piece in pieces]
    normed, normed_t, cotangent_t = order(normalize, activations, gain, cotangent)

    core = lax.axis_index("wide") % 2
    chips = wide // 2
    mixed, sums = [], []
    line = None
    for g in range(groups):
        if line is not None and line.hops < chips - 1:
            line.advance()
        qkv = order(lambda a, b: product(a, b, 0, full), normed, weights[g])
        rows, lse = order(lambda a: attend_forward(a, members, block), qkv)
        mixed.append(rows)
        grad_mixed = order(lambda a, b: product(a, b, full, span), cotangent, weights[g])
        while line is not None and line.hops < chips - 1:
            line.advance()
        back = order(
            lambda a, b, c: attend_backward(a, b, c, members, block), qkv, grad_mixed, lse
        )

        def side(which):
            return order(
                lambda *a: side_terms(which, a[:2], a[2:], wide), normed_t, cotangent_t, back, rows
            )

        if g < groups - 1:
            if line is not None:
                sums.append(line.total())
            line = LineSum(order, chips)
            line.swap(side(1 - core))
            line.hold(side(core))
            line.advance()
            continue
        part = order(lambda *a: terms(a[:2], a[2:]), normed_t, cotangent_t, back, rows)
        if line is not None:
            part, *line.arrived = lax.optimization_barrier((part, *line.arrived))
        last = lax.psum_scatter(part, "wide", scatter_dimension=0, tiled=True)
        if line is not None:
            sums.append(line.total())
        sums.append(last)
        parts = order(lambda *a: project(a[:groups], a[groups:]), *mixed, *weights)
        own, arrived = narrow_sum(parts, narrow)

    def finish_outputs(activations, *parts):
        share = parts[0].shape[1]
        at = lax.axis_index("narrow") * share
        result = lax.dynamic_slice_in_dim(activations, at, share, 1).astype(F32)
        return (result + sum(part.astype(F32) for part in parts)).astype(BF16)

    outputs = order(finish_outputs, activations, own, *arrived)
    grad_query, grad_key, grad_value, grad_out = unpack(sums, span)
    return (outputs, grad_query, grad_key, grad_value, grad_out)


def solution(mesh):
    return jax.shard_map(
        functools.partial(shards, (mesh.shape["wide"], mesh.shape["narrow"])),
        mesh=mesh,
        in_specs=(
            P("wide", None),
            P(),
            P("wide", "narrow"),
            P("wide", "narrow"),
            P("wide", "narrow"),
            P("wide", "narrow"),
            P("wide", None),
        ),
        out_specs=(
            P("wide", "narrow"),
            P("wide", "narrow"),
            P("wide", "narrow"),
            P("wide", "narrow"),
            P("wide", "narrow"),
        ),
        check_vma=False,
    )
```

```python
import functools
import jax
import jax.numpy as jnp
from jax import lax
from jax.experimental import pallas as pl
from jax.experimental.pallas import tpu as pltpu
from jax.sharding import PartitionSpec as P

HEAD_DIM = 128
BLOCK = 256
EPSILON = 1e-05
MASKED = -1e30
F32 = jnp.float32
BF16 = jnp.bfloat16
VMEM_LIMIT = 51 * 2**20
SHORT = pl.CostEstimate(flops=1, bytes_accessed=1, transcendentals=0)


def nt(a, b):
    return lax.dot_general(a, b, (((1,), (1,)), ((), ())), preferred_element_type=F32)


def nn(a, b):
    return lax.dot_general(a, b, (((1,), (0,)), ((), ())), preferred_element_type=F32)


def masked_scores(keys, queries, start, size):
    scores = nt(keys, queries) * HEAD_DIM ** (-0.5)
    key_at = lax.broadcasted_iota(jnp.int32, (size, size), 0)
    query_at = lax.broadcasted_iota(jnp.int32, (size, size), 1)
    last = jnp.where(key_at <= query_at, scores[start:], MASKED)
    if start == 0:
        return last
    return jnp.concatenate([scores[:start], last], axis=0)


def forward_kernel(members, block, qkv_ref, mixed_ref, lse_ref):
    length = qkv_ref.shape[0]
    width = HEAD_DIM
    key_col, value_col = members * width, (members + 1) * width
    values_t = qkv_ref[:, value_col : value_col + width].T
    for h in range(members):
        for start in range(0, length, block):
            stop = start + block
            queries = qkv_ref[start:stop, h * width : (h + 1) * width]
            keys = qkv_ref[:stop, key_col : key_col + width]
            scores = masked_scores(keys, queries, start, block)
            highest = jnp.max(scores, axis=0, keepdims=True)
            exponent = jnp.exp(scores - highest)
            total = jnp.sum(exponent, axis=0, keepdims=True)
            rounded = (exponent * (1.0 / total)).astype(BF16)
            mixed_t = nn(values_t[:, :stop], rounded)
            mixed_ref[start:stop, h * width : (h + 1) * width] = mixed_t.T.astype(BF16)
            lse_ref[h : h + 1, start:stop] = highest + jnp.log(total)


def attend_forward(qkv, members, block):
    length = qkv.shape[0]
    width = HEAD_DIM
    vmem = pl.BlockSpec(memory_space=pltpu.VMEM)
    return pl.pallas_call(
        functools.partial(forward_kernel, members, block),
        out_shape=(
            jax.ShapeDtypeStruct((length, members * width), BF16),
            jax.ShapeDtypeStruct((members, length), F32),
        ),
        in_specs=[vmem],
        out_specs=(vmem, vmem),
        compiler_params=pltpu.CompilerParams(vmem_limit_bytes=VMEM_LIMIT),
        cost_estimate=SHORT,
        name="attend_forward",
    )(qkv)


def backward_kernel(members, block, qkv_ref, grad_ref, lse_ref, out_ref, gk_ref, gv_ref):
    length = qkv_ref.shape[0]
    width = HEAD_DIM
    key_col, value_col = members * width, (members + 1) * width
    keys_t = qkv_ref[:, key_col : key_col + width].T
    gk_ref[...] = jnp.zeros_like(gk_ref)
    gv_ref[...] = jnp.zeros_like(gv_ref)
    for h in range(members):
        cols = slice(h * width, (h + 1) * width)
        for start in range(0, length, block):
            stop = start + block
            queries = qkv_ref[start:stop, cols]
            grads = grad_ref[start:stop, cols]
            keys = qkv_ref[:stop, key_col : key_col + width]
            values = qkv_ref[:stop, value_col : value_col + width]
            scores = masked_scores(keys, queries, start, block)
            probs = jnp.exp(scores - lse_ref[h : h + 1, start:stop])
            grad_probs = nt(values, grads)
            gv_ref[:stop, :] += nn(probs.astype(BF16), grads)
            inner = jnp.sum(grad_probs * probs, axis=0, keepdims=True)
            grad_scores = (probs * (grad_probs - inner) * width ** (-0.5)).astype(BF16)
            gk_ref[:stop, :] += nn(grad_scores, queries)
            out_ref[start:stop, cols] = nn(keys_t[:, :stop], grad_scores).T.astype(BF16)
    out_ref[:, key_col : key_col + width] = gk_ref[...].astype(BF16)
    out_ref[:, value_col : value_col + width] = gv_ref[...].astype(BF16)


def attend_backward(qkv, grad_mixed, lse, members, block):
    length = qkv.shape[0]
    width = HEAD_DIM
    vmem = pl.BlockSpec(memory_space=pltpu.VMEM)
    return pl.pallas_call(
        functools.partial(backward_kernel, members, block),
        out_shape=jax.ShapeDtypeStruct(qkv.shape, BF16),
        in_specs=[vmem, vmem, vmem],
        out_specs=vmem,
        scratch_shapes=[pltpu.VMEM((length, width), F32), pltpu.VMEM((length, width), F32)],
        compiler_params=pltpu.CompilerParams(vmem_limit_bytes=VMEM_LIMIT),
        cost_estimate=SHORT,
        name="attend_backward",
    )(qkv, grad_mixed, lse)


def pack_kernel(groups, query, key, value, out, *packed):
    width = HEAD_DIM
    span = query.shape[1] // groups
    for g, piece in enumerate(packed):
        heads = slice(g * span, (g + 1) * span)
        group = slice(g * width, (g + 1) * width)
        piece[:, :span] = query[:, heads]
        piece[:, span : span + width] = key[:, group]
        piece[:, span + width : span + 2 * width] = value[:, group]
        piece[:, span + 2 * width :] = out[:, heads]


def pack(query, key, value, out):
    rows, cols = query.shape
    groups = key.shape[1] // HEAD_DIM
    wide = 2 * cols // groups + 2 * HEAD_DIM
    return pl.pallas_call(
        functools.partial(pack_kernel, groups),
        out_shape=(jax.ShapeDtypeStruct((rows, wide), BF16),) * groups,
        compiler_params=pltpu.CompilerParams(vmem_limit_bytes=60 * 2**20),
        cost_estimate=SHORT,
        name="pack",
    )(query, key, value, out)


def unpack_kernel(*refs):
    sums, (grad_query, grad_key, grad_value, grad_out) = refs[:-4], refs[-4:]
    width = HEAD_DIM
    span = grad_query.shape[1] // len(sums)
    for g, part in enumerate(sums):
        heads = slice(g * span, (g + 1) * span)
        group = slice(g * width, (g + 1) * width)
        grad_query[:, heads] = part[:, :span].astype(F32)
        grad_key[:, group] = part[:, span : span + width].astype(F32)
        grad_value[:, group] = part[:, span + width : span + 2 * width].astype(F32)
        grad_out[:, heads] = part[:, span + 2 * width :].astype(F32)


def unpack(sums, span):
    rows = sums[0].shape[0]
    groups = len(sums)
    shapes = [
        jax.ShapeDtypeStruct((rows, groups * cols), F32)
        for cols in (span, HEAD_DIM, HEAD_DIM, span)
    ]
    step = 128 if rows % 128 == 0 else rows
    return pl.pallas_call(
        unpack_kernel,
        grid=(rows // step,),
        out_shape=shapes,
        in_specs=[pl.BlockSpec((step, part.shape[1]), lambda i: (i, 0)) for part in sums],
        out_specs=[pl.BlockSpec((step, shape.shape[1]), lambda i: (i, 0)) for shape in shapes],
        compiler_params=pltpu.CompilerParams(vmem_limit_bytes=VMEM_LIMIT),
        cost_estimate=SHORT,
        name="unpack",
    )(*sums)


def norm_kernel(x_ref, gain_ref, grad_ref, out, out_t, grad_t):
    features = x_ref.shape[1]
    step = 512 if features % 512 == 0 else features
    total = None
    for at in range(0, features, step):
        values = x_ref[:, at : at + step].astype(F32)
        part = jnp.sum(values * values, axis=-1, keepdims=True)
        total = part if total is None else total + part
    scale = lax.rsqrt(total / features + EPSILON)
    for at in range(0, features, step):
        cols = slice(at, at + step)
        normed = (x_ref[:, cols].astype(F32) * scale * gain_ref[:, cols]).astype(BF16)
        out[:, cols] = normed
        out_t[cols, :] = normed.T
        grad_t[cols, :] = grad_ref[:, cols].T


def normalize(activations, gain, cotangent):
    length, features = activations.shape
    step = 128 if length % 128 == 0 else length
    whole = pl.BlockSpec((step, features), lambda i: (i, 0))
    turned = pl.BlockSpec((features, step), lambda i: (0, i))
    shape_t = jax.ShapeDtypeStruct((features, length), BF16)
    return pl.pallas_call(
        norm_kernel,
        grid=(length // step,),
        out_shape=(jax.ShapeDtypeStruct((length, features), BF16), shape_t, shape_t),
        in_specs=[whole, pl.BlockSpec((1, features), lambda i: (0, 0)), whole],
        out_specs=(whole, turned, turned),
        compiler_params=pltpu.CompilerParams(vmem_limit_bytes=VMEM_LIMIT),
        cost_estimate=SHORT,
        name="normalize",
    )(activations, gain.astype(F32).reshape(1, -1), cotangent)


def product_kernel(a, b, out):
    out[...] = nn(a[...], b[...]).astype(BF16)


def product(rows, weights, first, cols):
    length, depth = rows.shape
    step = 256 if first % 256 == 0 and cols % 256 == 0 else HEAD_DIM
    return pl.pallas_call(
        product_kernel,
        grid=(cols // step,),
        out_shape=jax.ShapeDtypeStruct((length, cols), BF16),
        in_specs=[
            pl.BlockSpec((length, depth), lambda i: (0, 0)),
            pl.BlockSpec((depth, step), lambda i: (0, i + first // step)),
        ],
        out_specs=pl.BlockSpec((length, step), lambda i: (0, i)),
        compiler_params=pltpu.CompilerParams(vmem_limit_bytes=VMEM_LIMIT),
        cost_estimate=SHORT,
        name="product",
    )(rows, weights)


def terms_kernel(count, *refs):
    lefts, rights, out = refs[:count], refs[count : 2 * count], refs[-1]
    at = 0
    for left, right in zip(lefts, rights):
        cols = right.shape[1]
        out[:, at : at + cols] = nn(left[...], right[...]).astype(BF16)
        at += cols


def terms(lefts, rights):
    features, length = lefts[0].shape
    cols = sum(right.shape[1] for right in rights)
    step = 1024 if features % 1024 == 0 else features
    count = len(lefts)
    return pl.pallas_call(
        functools.partial(terms_kernel, count),
        grid=(features // step,),
        out_shape=jax.ShapeDtypeStruct((features, cols), BF16),
        in_specs=[pl.BlockSpec((step, length), lambda i: (i, 0))] * count
        + [pl.BlockSpec(right.shape, lambda i: (0, 0)) for right in rights],
        out_specs=pl.BlockSpec((step, cols), lambda i: (i, 0)),
        compiler_params=pltpu.CompilerParams(vmem_limit_bytes=VMEM_LIMIT),
        cost_estimate=SHORT,
        name="terms",
    )(*lefts, *rights)


def side_terms_kernel(count, side, *refs):
    terms_kernel(count, *refs)


def side_terms(side, lefts, rights, wide):
    features, length = lefts[0].shape
    cols = sum(right.shape[1] for right in rights)
    rows = features // wide
    count = len(lefts)
    return pl.pallas_call(
        functools.partial(side_terms_kernel, count),
        grid_spec=pltpu.PrefetchScalarGridSpec(
            num_scalar_prefetch=1,
            grid=(wide // 2,),
            in_specs=[pl.BlockSpec((rows, length), lambda i, side: (2 * i + side[0], 0))] * count
            + [pl.BlockSpec(right.shape, lambda i, side: (0, 0)) for right in rights],
            out_specs=pl.BlockSpec((rows, cols), lambda i, side: (i, 0)),
        ),
        out_shape=jax.ShapeDtypeStruct((features // 2, cols), BF16),
        compiler_params=pltpu.CompilerParams(vmem_limit_bytes=VMEM_LIMIT),
        cost_estimate=SHORT,
        name="side_terms",
    )(side.reshape(1), *lefts, *rights)


def project_kernel(count, *refs):
    out = refs[-1]
    total = None
    for mixed, side in zip(refs[:count], refs[count : 2 * count]):
        part = nt(mixed[...], side[:, side.shape[1] - mixed.shape[1] :])
        total = part if total is None else total + part
    out[...] = total.astype(BF16)


def project(mixed, sides):
    length, span = mixed[0].shape
    features = sides[0].shape[0]
    step = 512 if features % 512 == 0 else features
    count = len(mixed)
    return pl.pallas_call(
        functools.partial(project_kernel, count),
        grid=(features // step,),
        out_shape=jax.ShapeDtypeStruct((length, features), BF16),
        in_specs=[pl.BlockSpec((length, span), lambda i: (0, 0))] * count
        + [pl.BlockSpec((step, side.shape[1]), lambda i: (i, 0)) for side in sides],
        out_specs=pl.BlockSpec((length, step), lambda i: (0, i)),
        compiler_params=pltpu.CompilerParams(vmem_limit_bytes=VMEM_LIMIT),
        cost_estimate=SHORT,
        name="project",
    )(*mixed, *sides)


class Order:
    def __init__(self):
        self.last = None

    def __call__(self, compute, *operands):
        result = compute(*self.after(*operands))
        leaves, form = jax.tree.flatten(result)
        if len(leaves) > 1:
            leaves = lax.optimization_barrier(tuple(leaves))
        self.last = leaves[0]
        return jax.tree.unflatten(form, leaves)

    def after(self, *operands):
        if self.last is None:
            return operands
        least = min(range(len(operands)), key=lambda i: operands[i].size)
        tied = lax.optimization_barrier((self.last, operands[least]))[1]
        return operands[:least] + (tied,) + operands[least + 1 :]


def take(blocks, at):
    return lax.dynamic_index_in_dim(blocks, at, 0, keepdims=False)


def swap_cores(array, chips):
    return lax.ppermute(array, "wide", [(w, w ^ 1) for w in range(2 * chips)])


class LineSum:
    def __init__(self, order, chips):
        self.order, self.chips = order, chips
        self.chip = lax.axis_index("wide") // 2
        self.arrived = ()
        self.hops = 0

    def blocks(self, array):
        return array.reshape(self.chips, -1, array.shape[-1])

    def swap(self, send):
        self.received = self.blocks(swap_cores(send, self.chips))

    def hold(self, keep):
        self.keep = self.blocks(keep)

    def advance(self):
        self.hops += 1
        t, chips, chip = self.hops, self.chips, self.chip
        far = chips - t

        def messages(keep, received, *arrived):
            sums = []
            for i, at in enumerate((jnp.minimum(chip + far, chips - 1), jnp.maximum(chip - far, 0))):
                total = take(keep, at).astype(F32) + take(received, at).astype(F32)
                if arrived:
                    total = total + arrived[i].astype(F32)
                sums.append(total.astype(BF16))
            return tuple(sums)

        up, down = self.order(messages, self.keep, self.received, *self.arrived)
        self.arrived = (
            lax.ppermute(up, "wide", [(w, w + 2) for w in range(2 * t)]),
            lax.ppermute(down, "wide", [(w, w - 2) for w in range(2 * far, 2 * chips)]),
        )

    def total(self):
        def add(keep, received, *arrived):
            result = take(keep, self.chip).astype(F32) + take(received, self.chip).astype(F32)
            for part in arrived:
                result = result + part.astype(F32)
            return result

        return self.order(add, self.keep, self.received, *self.arrived)


def narrow_sum(parts, size):
    own = lax.axis_index("narrow")
    share = parts.shape[1] // size
    even = size & (size - 1) == 0

    def columns_of(device):
        return lax.dynamic_slice_in_dim(parts, device * share, share, 1)

    arrived = []
    for shift in range(1, size):
        to = [n ^ shift if even else (n + shift) % size for n in range(size)]
        mine = own ^ shift if even else (own + shift) % size
        arrived.append(lax.ppermute(columns_of(mine), "narrow", list(enumerate(to))))
    return columns_of(own), arrived


def shards(sizes, activations, gain, w_query, w_key, w_value, w_out, cotangent):
    wide, narrow = sizes
    width = HEAD_DIM
    length, features = activations.shape
    groups = w_key.shape[1] // width
    members = w_query.shape[1] // w_key.shape[1]
    block = BLOCK if length % BLOCK == 0 else length
    span = members * width
    full = span + 2 * width
    order = Order()

    pieces = pack(w_query, w_key, w_value, w_out)
    weights = [lax.all_gather(piece, "wide", axis=0, tiled=True) for piece in pieces]
    normed, normed_t, cotangent_t = order(normalize, activations, gain, cotangent)

    core = lax.axis_index("wide") % 2
    chips = wide // 2
    mixed, sums = [], []
    line = None
    for g in range(groups):
        if line is not None and line.hops < chips - 1:
            line.advance()
        qkv = order(lambda a, b: product(a, b, 0, full), normed, weights[g])
        rows, lse = order(lambda a: attend_forward(a, members, block), qkv)
        mixed.append(rows)
        grad_mixed = order(lambda a, b: product(a, b, full, span), cotangent, weights[g])
        while line is not None and line.hops < chips - 1:
            line.advance()
        back = order(
            lambda a, b, c: attend_backward(a, b, c, members, block), qkv, grad_mixed, lse
        )

        def side(which):
            return order(
                lambda *a: side_terms(which, a[:2], a[2:], wide), normed_t, cotangent_t, back, rows
            )

        if g < groups - 1:
            if line is not None:
                sums.append(line.total())
            line = LineSum(order, chips)
            line.swap(side(1 - core))
            line.hold(side(core))
            line.advance()
            continue
        part = order(lambda *a: terms(a[:2], a[2:]), normed_t, cotangent_t, back, rows)
        if line is not None:
            part, *line.arrived = lax.optimization_barrier((part, *line.arrived))
        last = lax.psum_scatter(part, "wide", scatter_dimension=0, tiled=True)
        if line is not None:
            sums.append(line.total())
        sums.append(last)
        parts = order(lambda *a: project(a[:groups], a[groups:]), *mixed, *weights)
        own, arrived = narrow_sum(parts, narrow)

    def finish_outputs(activations, *parts):
        share = parts[0].shape[1]
        at = lax.axis_index("narrow") * share
        result = lax.dynamic_slice_in_dim(activations, at, share, 1).astype(F32)
        return (result + sum(part.astype(F32) for part in parts)).astype(BF16)

    outputs = order(finish_outputs, activations, own, *arrived)
    grad_query, grad_key, grad_value, grad_out = unpack(sums, span)
    return (outputs, grad_query, grad_key, grad_value, grad_out)


def solution(mesh):
    return jax.shard_map(
        functools.partial(shards, (mesh.shape["wide"], mesh.shape["narrow"])),
        mesh=mesh,
        in_specs=(
            P("wide", None),
            P(),
            P("wide", "narrow"),
            P("wide", "narrow"),
            P("wide", "narrow"),
            P("wide", "narrow"),
            P("wide", None),
        ),
        out_specs=(
            P("wide", "narrow"),
            P("wide", "narrow"),
            P("wide", "narrow"),
            P("wide", "narrow"),
            P("wide", "narrow"),
        ),
        check_vma=False,
    )
```

```python
import functools
import jax
import jax.numpy as jnp
from jax import lax
from jax.experimental import pallas as pl
from jax.experimental.pallas import tpu as pltpu
from jax.sharding import PartitionSpec as P

HEAD_DIM = 128
BLOCK = 256
EPSILON = 1e-05
MASKED = -1e30
F32 = jnp.float32
BF16 = jnp.bfloat16
VMEM_LIMIT = 51 * 2**20
SHORT = pl.CostEstimate(flops=1, bytes_accessed=1, transcendentals=0)


def nt(a, b):
    return lax.dot_general(a, b, (((1,), (1,)), ((), ())), preferred_element_type=F32)


def nn(a, b):
    return lax.dot_general(a, b, (((1,), (0,)), ((), ())), preferred_element_type=F32)


def masked_scores(keys, queries, start, size):
    scores = nt(keys, queries) * HEAD_DIM ** (-0.5)
    key_at = lax.broadcasted_iota(jnp.int32, (size, size), 0)
    query_at = lax.broadcasted_iota(jnp.int32, (size, size), 1)
    last = jnp.where(key_at <= query_at, scores[start:], MASKED)
    if start == 0:
        return last
    return jnp.concatenate([scores[:start], last], axis=0)


def forward_kernel(members, block, qkv_ref, mixed_ref, lse_ref):
    length = qkv_ref.shape[0]
    width = HEAD_DIM
    key_col, value_col = members * width, (members + 1) * width
    values_t = qkv_ref[:, value_col : value_col + width].T
    for h in range(members):
        for start in range(0, length, block):
            stop = start + block
            queries = qkv_ref[start:stop, h * width : (h + 1) * width]
            keys = qkv_ref[:stop, key_col : key_col + width]
            scores = masked_scores(keys, queries, start, block)
            highest = jnp.max(scores, axis=0, keepdims=True)
            exponent = jnp.exp(scores - highest)
            total = jnp.sum(exponent, axis=0, keepdims=True)
            rounded = (exponent * (1.0 / total)).astype(BF16)
            mixed_t = nn(values_t[:, :stop], rounded)
            mixed_ref[start:stop, h * width : (h + 1) * width] = mixed_t.T.astype(BF16)
            lse_ref[h : h + 1, start:stop] = highest + jnp.log(total)


def attend_forward(qkv, members, block):
    length = qkv.shape[0]
    width = HEAD_DIM
    vmem = pl.BlockSpec(memory_space=pltpu.VMEM)
    return pl.pallas_call(
        functools.partial(forward_kernel, members, block),
        out_shape=(
            jax.ShapeDtypeStruct((length, members * width), BF16),
            jax.ShapeDtypeStruct((members, length), F32),
        ),
        in_specs=[vmem],
        out_specs=(vmem, vmem),
        compiler_params=pltpu.CompilerParams(vmem_limit_bytes=VMEM_LIMIT),
        cost_estimate=SHORT,
        name="attend_forward",
    )(qkv)


def backward_kernel(members, block, qkv_ref, grad_ref, lse_ref, out_ref, gk_ref, gv_ref):
    length = qkv_ref.shape[0]
    width = HEAD_DIM
    key_col, value_col = members * width, (members + 1) * width
    keys_t = qkv_ref[:, key_col : key_col + width].T
    gk_ref[...] = jnp.zeros_like(gk_ref)
    gv_ref[...] = jnp.zeros_like(gv_ref)
    for h in range(members):
        cols = slice(h * width, (h + 1) * width)
        for start in range(0, length, block):
            stop = start + block
            queries = qkv_ref[start:stop, cols]
            grads = grad_ref[start:stop, cols]
            keys = qkv_ref[:stop, key_col : key_col + width]
            values = qkv_ref[:stop, value_col : value_col + width]
            scores = masked_scores(keys, queries, start, block)
            probs = jnp.exp(scores - lse_ref[h : h + 1, start:stop])
            grad_probs = nt(values, grads)
            gv_ref[:stop, :] += nn(probs.astype(BF16), grads)
            inner = jnp.sum(grad_probs * probs, axis=0, keepdims=True)
            grad_scores = (probs * (grad_probs - inner) * width ** (-0.5)).astype(BF16)
            gk_ref[:stop, :] += nn(grad_scores, queries)
            out_ref[start:stop, cols] = nn(keys_t[:, :stop], grad_scores).T.astype(BF16)
    out_ref[:, key_col : key_col + width] = gk_ref[...].astype(BF16)
    out_ref[:, value_col : value_col + width] = gv_ref[...].astype(BF16)


def attend_backward(qkv, grad_mixed, lse, members, block):
    length = qkv.shape[0]
    width = HEAD_DIM
    vmem = pl.BlockSpec(memory_space=pltpu.VMEM)
    return pl.pallas_call(
        functools.partial(backward_kernel, members, block),
        out_shape=jax.ShapeDtypeStruct(qkv.shape, BF16),
        in_specs=[vmem, vmem, vmem],
        out_specs=vmem,
        scratch_shapes=[pltpu.VMEM((length, width), F32), pltpu.VMEM((length, width), F32)],
        compiler_params=pltpu.CompilerParams(vmem_limit_bytes=VMEM_LIMIT),
        cost_estimate=SHORT,
        name="attend_backward",
    )(qkv, grad_mixed, lse)


def group_specs(rows, span, g):
    step = 128 if rows % 128 == 0 else rows
    return [
        pl.BlockSpec((step, cols), lambda i: (i, g))
        for cols in (span, HEAD_DIM, HEAD_DIM, span)
    ]


def pack_kernel(query, key, value, out, piece):
    at = 0
    for part in (query, key, value, out):
        piece[:, at : at + part.shape[1]] = part[...]
        at += part.shape[1]


def pack(query, key, value, out, span, g):
    rows = query.shape[0]
    cols = 2 * span + 2 * HEAD_DIM
    specs = group_specs(rows, span, g)
    step = specs[0].block_shape[0]
    return pl.pallas_call(
        pack_kernel,
        grid=(rows // step,),
        out_shape=jax.ShapeDtypeStruct((rows, cols), BF16),
        in_specs=specs,
        out_specs=pl.BlockSpec((step, cols), lambda i: (i, 0)),
        compiler_params=pltpu.CompilerParams(vmem_limit_bytes=60 * 2**20),
        cost_estimate=SHORT,
        name="pack",
    )(query, key, value, out)


def unpack_kernel(piece, *refs):
    at = 0
    for part in refs[-4:]:
        part[...] = piece[:, at : at + part.shape[1]].astype(F32)
        at += part.shape[1]


def unpack(piece, grads, span, groups, g):
    rows = piece.shape[0]
    specs = group_specs(rows, span, g)
    step = specs[0].block_shape[0]
    return pl.pallas_call(
        unpack_kernel,
        grid=(rows // step,),
        out_shape=[
            jax.ShapeDtypeStruct((rows, groups * cols), F32)
            for cols in (span, HEAD_DIM, HEAD_DIM, span)
        ],
        in_specs=[pl.BlockSpec((step, piece.shape[1]), lambda i: (i, 0))]
        + [pl.BlockSpec(memory_space=pl.ANY)] * len(grads),
        out_specs=specs,
        input_output_aliases={1 + i: i for i in range(len(grads))},
        compiler_params=pltpu.CompilerParams(vmem_limit_bytes=60 * 2**20),
        cost_estimate=SHORT,
        name="unpack",
    )(piece, *grads)


def norm_kernel(x_ref, gain_ref, grad_ref, out, out_t, grad_t):
    features = x_ref.shape[1]
    step = 512 if features % 512 == 0 else features
    total = None
    for at in range(0, features, step):
        values = x_ref[:, at : at + step].astype(F32)
        part = jnp.sum(values * values, axis=-1, keepdims=True)
        total = part if total is None else total + part
    scale = lax.rsqrt(total / features + EPSILON)
    for at in range(0, features, step):
        cols = slice(at, at + step)
        normed = (x_ref[:, cols].astype(F32) * scale * gain_ref[:, cols]).astype(BF16)
        out[:, cols] = normed
        out_t[cols, :] = normed.T
        grad_t[cols, :] = grad_ref[:, cols].T


def normalize(activations, gain, cotangent):
    length, features = activations.shape
    step = 128 if length % 128 == 0 else length
    whole = pl.BlockSpec((step, features), lambda i: (i, 0))
    turned = pl.BlockSpec((features, step), lambda i: (0, i))
    shape_t = jax.ShapeDtypeStruct((features, length), BF16)
    return pl.pallas_call(
        norm_kernel,
        grid=(length // step,),
        out_shape=(jax.ShapeDtypeStruct((length, features), BF16), shape_t, shape_t),
        in_specs=[whole, pl.BlockSpec((1, features), lambda i: (0, 0)), whole],
        out_specs=(whole, turned, turned),
        compiler_params=pltpu.CompilerParams(vmem_limit_bytes=VMEM_LIMIT),
        cost_estimate=SHORT,
        name="normalize",
    )(activations, gain.astype(F32).reshape(1, -1), cotangent)


def product_kernel(a, b, out):
    out[...] = nn(a[...], b[...]).astype(BF16)


def product(rows, weights, first, cols):
    length, depth = rows.shape
    step = 256 if first % 256 == 0 and cols % 256 == 0 else HEAD_DIM
    return pl.pallas_call(
        product_kernel,
        grid=(cols // step,),
        out_shape=jax.ShapeDtypeStruct((length, cols), BF16),
        in_specs=[
            pl.BlockSpec((length, depth), lambda i: (0, 0)),
            pl.BlockSpec((depth, step), lambda i: (0, i + first // step)),
        ],
        out_specs=pl.BlockSpec((length, step), lambda i: (0, i)),
        compiler_params=pltpu.CompilerParams(vmem_limit_bytes=VMEM_LIMIT),
        cost_estimate=SHORT,
        name="product",
    )(rows, weights)


def terms_kernel(count, *refs):
    lefts, rights, out = refs[:count], refs[count : 2 * count], refs[-1]
    at = 0
    for left, right in zip(lefts, rights):
        cols = right.shape[1]
        out[:, at : at + cols] = nn(left[...], right[...]).astype(BF16)
        at += cols


def terms(lefts, rights):
    features, length = lefts[0].shape
    cols = sum(right.shape[1] for right in rights)
    step = 1024 if features % 1024 == 0 else features
    count = len(lefts)
    return pl.pallas_call(
        functools.partial(terms_kernel, count),
        grid=(features // step,),
        out_shape=jax.ShapeDtypeStruct((features, cols), BF16),
        in_specs=[pl.BlockSpec((step, length), lambda i: (i, 0))] * count
        + [pl.BlockSpec(right.shape, lambda i: (0, 0)) for right in rights],
        out_specs=pl.BlockSpec((step, cols), lambda i: (i, 0)),
        compiler_params=pltpu.CompilerParams(vmem_limit_bytes=VMEM_LIMIT),
        cost_estimate=SHORT,
        name="terms",
    )(*lefts, *rights)


def side_terms_kernel(count, side, *refs):
    terms_kernel(count, *refs)


def side_terms(side, lefts, rights, wide):
    features, length = lefts[0].shape
    cols = sum(right.shape[1] for right in rights)
    rows = features // wide
    count = len(lefts)
    return pl.pallas_call(
        functools.partial(side_terms_kernel, count),
        grid_spec=pltpu.PrefetchScalarGridSpec(
            num_scalar_prefetch=1,
            grid=(wide // 2,),
            in_specs=[pl.BlockSpec((rows, length), lambda i, side: (2 * i + side[0], 0))] * count
            + [pl.BlockSpec(right.shape, lambda i, side: (0, 0)) for right in rights],
            out_specs=pl.BlockSpec((rows, cols), lambda i, side: (i, 0)),
        ),
        out_shape=jax.ShapeDtypeStruct((features // 2, cols), BF16),
        compiler_params=pltpu.CompilerParams(vmem_limit_bytes=VMEM_LIMIT),
        cost_estimate=SHORT,
        name="side_terms",
    )(side.reshape(1), *lefts, *rights)


def project_kernel(count, *refs):
    out = refs[-1]
    total = None
    for mixed, side in zip(refs[:count], refs[count : 2 * count]):
        part = nt(mixed[...], side[:, side.shape[1] - mixed.shape[1] :])
        total = part if total is None else total + part
    out[...] = total.astype(BF16)


def project(mixed, sides):
    length, span = mixed[0].shape
    features = sides[0].shape[0]
    step = 512 if features % 512 == 0 else features
    count = len(mixed)
    return pl.pallas_call(
        functools.partial(project_kernel, count),
        grid=(features // step,),
        out_shape=jax.ShapeDtypeStruct((length, features), BF16),
        in_specs=[pl.BlockSpec((length, span), lambda i: (0, 0))] * count
        + [pl.BlockSpec((step, side.shape[1]), lambda i: (i, 0)) for side in sides],
        out_specs=pl.BlockSpec((length, step), lambda i: (0, i)),
        compiler_params=pltpu.CompilerParams(vmem_limit_bytes=VMEM_LIMIT),
        cost_estimate=SHORT,
        name="project",
    )(*mixed, *sides)


class Order:
    def __init__(self):
        self.last = None

    def __call__(self, compute, *operands):
        result = compute(*self.after(*operands))
        leaves, form = jax.tree.flatten(result)
        if len(leaves) > 1:
            leaves = lax.optimization_barrier(tuple(leaves))
        self.last = leaves[0]
        return jax.tree.unflatten(form, leaves)

    def after(self, *operands):
        if self.last is None:
            return operands
        least = min(range(len(operands)), key=lambda i: operands[i].size)
        tied = lax.optimization_barrier((self.last, operands[least]))[1]
        return operands[:least] + (tied,) + operands[least + 1 :]


def take(blocks, at):
    return lax.dynamic_index_in_dim(blocks, at, 0, keepdims=False)


def swap_cores(array, chips):
    return lax.ppermute(array, "wide", [(w, w ^ 1) for w in range(2 * chips)])


class LineSum:
    def __init__(self, order, chips):
        self.order, self.chips = order, chips
        self.chip = lax.axis_index("wide") // 2
        self.arrived = ()
        self.hops = 0

    def blocks(self, array):
        return array.reshape(self.chips, -1, array.shape[-1])

    def swap(self, send):
        self.received = self.blocks(swap_cores(send, self.chips))

    def hold(self, keep):
        self.keep = self.blocks(keep)

    def advance(self):
        self.hops += 1
        t, chips, chip = self.hops, self.chips, self.chip
        far = chips - t

        def messages(keep, received, *arrived):
            sums = []
            for i, at in enumerate((jnp.minimum(chip + far, chips - 1), jnp.maximum(chip - far, 0))):
                total = take(keep, at).astype(F32) + take(received, at).astype(F32)
                if arrived:
                    total = total + arrived[i].astype(F32)
                sums.append(total.astype(BF16))
            return tuple(sums)

        up, down = self.order(messages, self.keep, self.received, *self.arrived)
        self.arrived = (
            lax.ppermute(up, "wide", [(w, w + 2) for w in range(2 * t)]),
            lax.ppermute(down, "wide", [(w, w - 2) for w in range(2 * far, 2 * chips)]),
        )

    def total(self):
        def add(keep, received, *arrived):
            result = take(keep, self.chip).astype(F32) + take(received, self.chip).astype(F32)
            for part in arrived:
                result = result + part.astype(F32)
            return result

        return self.order(add, self.keep, self.received, *self.arrived)


def narrow_sum(parts, size):
    own = lax.axis_index("narrow")
    share = parts.shape[1] // size
    even = size & (size - 1) == 0

    def columns_of(device):
        return lax.dynamic_slice_in_dim(parts, device * share, share, 1)

    arrived = []
    for shift in range(1, size):
        to = [n ^ shift if even else (n + shift) % size for n in range(size)]
        mine = own ^ shift if even else (own + shift) % size
        arrived.append(lax.ppermute(columns_of(mine), "narrow", list(enumerate(to))))
    return columns_of(own), arrived


def shards(sizes, activations, gain, w_query, w_key, w_value, w_out, cotangent):
    wide, narrow = sizes
    width = HEAD_DIM
    length, features = activations.shape
    groups = w_key.shape[1] // width
    members = w_query.shape[1] // w_key.shape[1]
    block = BLOCK if length % BLOCK == 0 else length
    span = members * width
    full = span + 2 * width
    order = Order()

    pieces = [pack(w_query, w_key, w_value, w_out, span, g) for g in range(groups)]
    weights = [lax.all_gather(piece, "wide", axis=0, tiled=True) for piece in pieces]
    normed, normed_t, cotangent_t = order(normalize, activations, gain, cotangent)

    core = lax.axis_index("wide") % 2
    chips = wide // 2
    mixed, grads = [], []
    line = None

    def write(piece, g):
        return order(lambda a, *b: unpack(a, b, span, groups, g), piece, *grads)

    for g in range(groups):
        if line is not None and line.hops < chips - 1:
            line.advance()
        qkv = order(lambda a, b: product(a, b, 0, full), normed, weights[g])
        rows, lse = order(lambda a: attend_forward(a, members, block), qkv)
        mixed.append(rows)
        grad_mixed = order(lambda a, b: product(a, b, full, span), cotangent, weights[g])
        while line is not None and line.hops < chips - 1:
            line.advance()
        back = order(
            lambda a, b, c: attend_backward(a, b, c, members, block), qkv, grad_mixed, lse
        )

        def side(which):
            return order(
                lambda *a: side_terms(which, a[:2], a[2:], wide), normed_t, cotangent_t, back, rows
            )

        if g < groups - 1:
            if line is not None:
                grads = write(line.total(), g - 1)
            line = LineSum(order, chips)
            line.swap(side(1 - core))
            line.hold(side(core))
            line.advance()
            continue
        part = order(lambda *a: terms(a[:2], a[2:]), normed_t, cotangent_t, back, rows)
        if line is not None:
            part, *line.arrived = lax.optimization_barrier((part, *line.arrived))
        last = lax.psum_scatter(part, "wide", scatter_dimension=0, tiled=True)
        if line is not None:
            grads = write(line.total(), g - 1)
        parts = order(lambda *a: project(a[:groups], a[groups:]), *mixed, *weights)
        own, arrived = narrow_sum(parts, narrow)

    def finish_outputs(activations, *parts):
        share = parts[0].shape[1]
        at = lax.axis_index("narrow") * share
        result = lax.dynamic_slice_in_dim(activations, at, share, 1).astype(F32)
        return (result + sum(part.astype(F32) for part in parts)).astype(BF16)

    outputs = order(finish_outputs, activations, own, *arrived)
    grad_query, grad_key, grad_value, grad_out = unpack(last, grads, span, groups, groups - 1)
    return (outputs, grad_query, grad_key, grad_value, grad_out)


def solution(mesh):
    return jax.shard_map(
        functools.partial(shards, (mesh.shape["wide"], mesh.shape["narrow"])),
        mesh=mesh,
        in_specs=(
            P("wide", None),
            P(),
            P("wide", "narrow"),
            P("wide", "narrow"),
            P("wide", "narrow"),
            P("wide", "narrow"),
            P("wide", None),
        ),
        out_specs=(
            P("wide", "narrow"),
            P("wide", "narrow"),
            P("wide", "narrow"),
            P("wide", "narrow"),
            P("wide", "narrow"),
        ),
        check_vma=False,
    )
```

```python
import functools
import jax
import jax.numpy as jnp
from jax import lax
from jax.experimental import pallas as pl
from jax.experimental.pallas import tpu as pltpu
from jax.sharding import PartitionSpec as P

HEAD_DIM = 128
BLOCK = 256
EPSILON = 1e-05
MASKED = -1e30
F32 = jnp.float32
BF16 = jnp.bfloat16
VMEM_LIMIT = 51 * 2**20
SHORT = pl.CostEstimate(flops=1, bytes_accessed=1, transcendentals=0)


def nt(a, b):
    return lax.dot_general(a, b, (((1,), (1,)), ((), ())), preferred_element_type=F32)


def nn(a, b):
    return lax.dot_general(a, b, (((1,), (0,)), ((), ())), preferred_element_type=F32)


def masked_scores(keys, queries, start, size):
    scores = nt(keys, queries) * HEAD_DIM ** (-0.5)
    key_at = lax.broadcasted_iota(jnp.int32, (size, size), 0)
    query_at = lax.broadcasted_iota(jnp.int32, (size, size), 1)
    last = jnp.where(key_at <= query_at, scores[start:], MASKED)
    if start == 0:
        return last
    return jnp.concatenate([scores[:start], last], axis=0)


def forward_kernel(members, block, qkv_ref, mixed_ref, lse_ref):
    length = qkv_ref.shape[0]
    width = HEAD_DIM
    key_col, value_col = members * width, (members + 1) * width
    values_t = qkv_ref[:, value_col : value_col + width].T
    for h in range(members):
        for start in range(0, length, block):
            stop = start + block
            queries = qkv_ref[start:stop, h * width : (h + 1) * width]
            keys = qkv_ref[:stop, key_col : key_col + width]
            scores = masked_scores(keys, queries, start, block)
            highest = jnp.max(scores, axis=0, keepdims=True)
            exponent = jnp.exp(scores - highest)
            total = jnp.sum(exponent, axis=0, keepdims=True)
            rounded = (exponent * (1.0 / total)).astype(BF16)
            mixed_t = nn(values_t[:, :stop], rounded)
            mixed_ref[start:stop, h * width : (h + 1) * width] = mixed_t.T.astype(BF16)
            lse_ref[h : h + 1, start:stop] = highest + jnp.log(total)


def attend_forward(qkv, members, block):
    length = qkv.shape[0]
    width = HEAD_DIM
    vmem = pl.BlockSpec(memory_space=pltpu.VMEM)
    return pl.pallas_call(
        functools.partial(forward_kernel, members, block),
        out_shape=(
            jax.ShapeDtypeStruct((length, members * width), BF16),
            jax.ShapeDtypeStruct((members, length), F32),
        ),
        in_specs=[vmem],
        out_specs=(vmem, vmem),
        compiler_params=pltpu.CompilerParams(vmem_limit_bytes=VMEM_LIMIT),
        cost_estimate=SHORT,
        name="attend_forward",
    )(qkv)


def backward_kernel(members, block, qkv_ref, grad_ref, lse_ref, out_ref, gk_ref, gv_ref):
    length = qkv_ref.shape[0]
    width = HEAD_DIM
    key_col, value_col = members * width, (members + 1) * width
    keys_t = qkv_ref[:, key_col : key_col + width].T
    gk_ref[...] = jnp.zeros_like(gk_ref)
    gv_ref[...] = jnp.zeros_like(gv_ref)
    for h in range(members):
        cols = slice(h * width, (h + 1) * width)
        for start in range(0, length, block):
            stop = start + block
            queries = qkv_ref[start:stop, cols]
            grads = grad_ref[start:stop, cols]
            keys = qkv_ref[:stop, key_col : key_col + width]
            values = qkv_ref[:stop, value_col : value_col + width]
            scores = masked_scores(keys, queries, start, block)
            probs = jnp.exp(scores - lse_ref[h : h + 1, start:stop])
            grad_probs = nt(values, grads)
            gv_ref[:stop, :] += nn(probs.astype(BF16), grads)
            inner = jnp.sum(grad_probs * probs, axis=0, keepdims=True)
            grad_scores = (probs * (grad_probs - inner) * width ** (-0.5)).astype(BF16)
            gk_ref[:stop, :] += nn(grad_scores, queries)
            out_ref[start:stop, cols] = nn(keys_t[:, :stop], grad_scores).T.astype(BF16)
    out_ref[:, key_col : key_col + width] = gk_ref[...].astype(BF16)
    out_ref[:, value_col : value_col + width] = gv_ref[...].astype(BF16)


def attend_backward(qkv, grad_mixed, lse, members, block):
    length = qkv.shape[0]
    width = HEAD_DIM
    vmem = pl.BlockSpec(memory_space=pltpu.VMEM)
    return pl.pallas_call(
        functools.partial(backward_kernel, members, block),
        out_shape=jax.ShapeDtypeStruct(qkv.shape, BF16),
        in_specs=[vmem, vmem, vmem],
        out_specs=vmem,
        scratch_shapes=[pltpu.VMEM((length, width), F32), pltpu.VMEM((length, width), F32)],
        compiler_params=pltpu.CompilerParams(vmem_limit_bytes=VMEM_LIMIT),
        cost_estimate=SHORT,
        name="attend_backward",
    )(qkv, grad_mixed, lse)


def group_specs(rows, span, g):
    step = 128 if rows % 128 == 0 else rows
    return [
        pl.BlockSpec((step, cols), lambda i: (i, g))
        for cols in (span, HEAD_DIM, HEAD_DIM, span)
    ]


def pack_kernel(query, key, value, out, piece):
    at = 0
    for part in (query, key, value, out):
        piece[:, at : at + part.shape[1]] = part[...]
        at += part.shape[1]


def pack(query, key, value, out, span, g):
    rows = query.shape[0]
    cols = 2 * span + 2 * HEAD_DIM
    specs = group_specs(rows, span, g)
    step = specs[0].block_shape[0]
    return pl.pallas_call(
        pack_kernel,
        grid=(rows // step,),
        out_shape=jax.ShapeDtypeStruct((rows, cols), BF16),
        in_specs=specs,
        out_specs=pl.BlockSpec((step, cols), lambda i: (i, 0)),
        compiler_params=pltpu.CompilerParams(vmem_limit_bytes=60 * 2**20),
        cost_estimate=SHORT,
        name="pack",
    )(query, key, value, out)


def unpack_kernel(piece, *refs):
    at = 0
    for part in refs[-4:]:
        part[...] = piece[:, at : at + part.shape[1]].astype(F32)
        at += part.shape[1]


def unpack(piece, grads, span, groups, g):
    rows = piece.shape[0]
    specs = group_specs(rows, span, g)
    step = specs[0].block_shape[0]
    return pl.pallas_call(
        unpack_kernel,
        grid=(rows // step,),
        out_shape=[
            jax.ShapeDtypeStruct((rows, groups * cols), F32)
            for cols in (span, HEAD_DIM, HEAD_DIM, span)
        ],
        in_specs=[pl.BlockSpec((step, piece.shape[1]), lambda i: (i, 0))]
        + [pl.BlockSpec(memory_space=pl.ANY)] * len(grads),
        out_specs=specs,
        input_output_aliases={1 + i: i for i in range(len(grads))},
        compiler_params=pltpu.CompilerParams(vmem_limit_bytes=60 * 2**20),
        cost_estimate=SHORT,
        name="unpack",
    )(piece, *grads)


def norm_kernel(x_ref, gain_ref, grad_ref, out, out_t, grad_t):
    features = x_ref.shape[1]
    step = 512 if features % 512 == 0 else features
    total = None
    for at in range(0, features, step):
        values = x_ref[:, at : at + step].astype(F32)
        part = jnp.sum(values * values, axis=-1, keepdims=True)
        total = part if total is None else total + part
    scale = lax.rsqrt(total / features + EPSILON)
    for at in range(0, features, step):
        cols = slice(at, at + step)
        normed = (x_ref[:, cols].astype(F32) * scale * gain_ref[:, cols]).astype(BF16)
        out[:, cols] = normed
        out_t[cols, :] = normed.T
        grad_t[cols, :] = grad_ref[:, cols].T


def normalize(activations, gain, cotangent):
    length, features = activations.shape
    step = 128 if length % 128 == 0 else length
    whole = pl.BlockSpec((step, features), lambda i: (i, 0))
    turned = pl.BlockSpec((features, step), lambda i: (0, i))
    shape_t = jax.ShapeDtypeStruct((features, length), BF16)
    return pl.pallas_call(
        norm_kernel,
        grid=(length // step,),
        out_shape=(jax.ShapeDtypeStruct((length, features), BF16), shape_t, shape_t),
        in_specs=[whole, pl.BlockSpec((1, features), lambda i: (0, 0)), whole],
        out_specs=(whole, turned, turned),
        compiler_params=pltpu.CompilerParams(vmem_limit_bytes=VMEM_LIMIT),
        cost_estimate=SHORT,
        name="normalize",
    )(activations, gain.astype(F32).reshape(1, -1), cotangent)


def product_kernel(a, b, out):
    out[...] = nn(a[...], b[...]).astype(BF16)


def product(rows, weights, first, cols):
    length, depth = rows.shape
    step = 256 if first % 256 == 0 and cols % 256 == 0 else HEAD_DIM
    return pl.pallas_call(
        product_kernel,
        grid=(cols // step,),
        out_shape=jax.ShapeDtypeStruct((length, cols), BF16),
        in_specs=[
            pl.BlockSpec((length, depth), lambda i: (0, 0)),
            pl.BlockSpec((depth, step), lambda i: (0, i + first // step)),
        ],
        out_specs=pl.BlockSpec((length, step), lambda i: (0, i)),
        compiler_params=pltpu.CompilerParams(vmem_limit_bytes=VMEM_LIMIT),
        cost_estimate=SHORT,
        name="product",
    )(rows, weights)


def terms_kernel(count, *refs):
    lefts, rights, out = refs[:count], refs[count : 2 * count], refs[-1]
    at = 0
    for left, right in zip(lefts, rights):
        cols = right.shape[1]
        out[:, at : at + cols] = nn(left[...], right[...]).astype(BF16)
        at += cols


def terms(lefts, rights):
    features, length = lefts[0].shape
    cols = sum(right.shape[1] for right in rights)
    step = 1024 if features % 1024 == 0 else features
    count = len(lefts)
    return pl.pallas_call(
        functools.partial(terms_kernel, count),
        grid=(features // step,),
        out_shape=jax.ShapeDtypeStruct((features, cols), BF16),
        in_specs=[pl.BlockSpec((step, length), lambda i: (i, 0))] * count
        + [pl.BlockSpec(right.shape, lambda i: (0, 0)) for right in rights],
        out_specs=pl.BlockSpec((step, cols), lambda i: (i, 0)),
        compiler_params=pltpu.CompilerParams(vmem_limit_bytes=VMEM_LIMIT),
        cost_estimate=SHORT,
        name="terms",
    )(*lefts, *rights)


def side_terms_kernel(count, side, *refs):
    terms_kernel(count, *refs)


def side_terms(side, lefts, rights, wide):
    features, length = lefts[0].shape
    cols = sum(right.shape[1] for right in rights)
    rows = features // wide
    count = len(lefts)
    return pl.pallas_call(
        functools.partial(side_terms_kernel, count),
        grid_spec=pltpu.PrefetchScalarGridSpec(
            num_scalar_prefetch=1,
            grid=(wide // 2,),
            in_specs=[pl.BlockSpec((rows, length), lambda i, side: (2 * i + side[0], 0))] * count
            + [pl.BlockSpec(right.shape, lambda i, side: (0, 0)) for right in rights],
            out_specs=pl.BlockSpec((rows, cols), lambda i, side: (i, 0)),
        ),
        out_shape=jax.ShapeDtypeStruct((features // 2, cols), BF16),
        compiler_params=pltpu.CompilerParams(vmem_limit_bytes=VMEM_LIMIT),
        cost_estimate=SHORT,
        name="side_terms",
    )(side.reshape(1), *lefts, *rights)


def project_kernel(count, *refs):
    out = refs[-1]
    total = None
    for mixed, side in zip(refs[:count], refs[count : 2 * count]):
        part = nt(mixed[...], side[:, side.shape[1] - mixed.shape[1] :])
        total = part if total is None else total + part
    out[...] = total.astype(BF16)


def project(mixed, sides):
    length, span = mixed[0].shape
    features = sides[0].shape[0]
    step = 512 if features % 512 == 0 else features
    count = len(mixed)
    return pl.pallas_call(
        functools.partial(project_kernel, count),
        grid=(features // step,),
        out_shape=jax.ShapeDtypeStruct((length, features), BF16),
        in_specs=[pl.BlockSpec((length, span), lambda i: (0, 0))] * count
        + [pl.BlockSpec((step, side.shape[1]), lambda i: (i, 0)) for side in sides],
        out_specs=pl.BlockSpec((length, step), lambda i: (0, i)),
        compiler_params=pltpu.CompilerParams(vmem_limit_bytes=VMEM_LIMIT),
        cost_estimate=SHORT,
        name="project",
    )(*mixed, *sides)


class Order:
    def __init__(self):
        self.last = None

    def __call__(self, compute, *operands):
        result = compute(*self.after(*operands))
        leaves, form = jax.tree.flatten(result)
        if len(leaves) > 1:
            leaves = lax.optimization_barrier(tuple(leaves))
        self.last = leaves[0]
        return jax.tree.unflatten(form, leaves)

    def after(self, *operands):
        if self.last is None:
            return operands
        least = min(range(len(operands)), key=lambda i: operands[i].size)
        tied = lax.optimization_barrier((self.last, operands[least]))[1]
        return operands[:least] + (tied,) + operands[least + 1 :]


def take(blocks, at):
    return lax.dynamic_index_in_dim(blocks, at, 0, keepdims=False)


def swap_cores(array, chips):
    return lax.ppermute(array, "wide", [(w, w ^ 1) for w in range(2 * chips)])


def add_kernel(a, b, out):
    out[...] = (a[...].astype(F32) + b[...].astype(F32)).astype(BF16)


def add_blocks(a, b):
    spec = pl.BlockSpec((1,) + a.shape[1:], lambda i: (i, 0, 0))
    return pl.pallas_call(
        add_kernel,
        grid=a.shape[:1],
        out_shape=jax.ShapeDtypeStruct(a.shape, BF16),
        in_specs=[spec, spec],
        out_specs=spec,
        compiler_params=pltpu.CompilerParams(vmem_limit_bytes=VMEM_LIMIT),
        cost_estimate=SHORT,
        name="add_blocks",
    )(a, b)


class LineSum:
    def __init__(self, order, chips):
        self.order, self.chips = order, chips
        self.chip = lax.axis_index("wide") // 2
        self.arrived = ()
        self.hops = 0

    def blocks(self, array):
        return array.reshape(self.chips, -1, array.shape[-1])

    def swap(self, send):
        self.received = self.blocks(swap_cores(send, self.chips))

    def hold(self, keep):
        self.held = (self.blocks(keep), self.received)

    def advance(self):
        self.hops += 1
        t, chips, chip = self.hops, self.chips, self.chip
        far = chips - t

        def messages(held, *arrived):
            sums = []
            for i, at in enumerate((jnp.minimum(chip + far, chips - 1), jnp.maximum(chip - far, 0))):
                total = sum(take(part, at).astype(F32) for part in held)
                if arrived:
                    total = total + arrived[i].astype(F32)
                sums.append(total.astype(BF16))
            return tuple(sums)

        count = len(self.held)
        up, down = self.order(
            lambda *a: messages(a[:count], *a[count:]), *self.held, *self.arrived
        )
        self.arrived = (
            lax.ppermute(up, "wide", [(w, w + 2) for w in range(2 * t)]),
            lax.ppermute(down, "wide", [(w, w - 2) for w in range(2 * far, 2 * chips)]),
        )
        if t == 1:
            self.held = (
                self.order(add_blocks, *self.held),
            )

    def total(self):
        def add(held, *arrived):
            result = take(held, self.chip).astype(F32)
            for part in arrived:
                result = result + part.astype(F32)
            return result

        return self.order(add, *self.held, *self.arrived)


def narrow_sum(parts, size):
    own = lax.axis_index("narrow")
    share = parts.shape[1] // size
    even = size & (size - 1) == 0

    def columns_of(device):
        return lax.dynamic_slice_in_dim(parts, device * share, share, 1)

    arrived = []
    for shift in range(1, size):
        to = [n ^ shift if even else (n + shift) % size for n in range(size)]
        mine = own ^ shift if even else (own + shift) % size
        arrived.append(lax.ppermute(columns_of(mine), "narrow", list(enumerate(to))))
    return columns_of(own), arrived


def shards(sizes, activations, gain, w_query, w_key, w_value, w_out, cotangent):
    wide, narrow = sizes
    width = HEAD_DIM
    length, features = activations.shape
    groups = w_key.shape[1] // width
    members = w_query.shape[1] // w_key.shape[1]
    block = BLOCK if length % BLOCK == 0 else length
    span = members * width
    full = span + 2 * width
    order = Order()

    pieces = [pack(w_query, w_key, w_value, w_out, span, g) for g in range(groups)]
    weights = [lax.all_gather(piece, "wide", axis=0, tiled=True) for piece in pieces]
    normed, normed_t, cotangent_t = order(normalize, activations, gain, cotangent)

    core = lax.axis_index("wide") % 2
    chips = wide // 2
    mixed, grads = [], []
    line = None

    def write(piece, g):
        return order(lambda a, *b: unpack(a, b, span, groups, g), piece, *grads)

    for g in range(groups):
        if line is not None and line.hops < chips - 1:
            line.advance()
        qkv = order(lambda a, b: product(a, b, 0, full), normed, weights[g])
        rows, lse = order(lambda a: attend_forward(a, members, block), qkv)
        mixed.append(rows)
        grad_mixed = order(lambda a, b: product(a, b, full, span), cotangent, weights[g])
        while line is not None and line.hops < chips - 1:
            line.advance()
        back = order(
            lambda a, b, c: attend_backward(a, b, c, members, block), qkv, grad_mixed, lse
        )

        def side(which):
            return order(
                lambda *a: side_terms(which, a[:2], a[2:], wide), normed_t, cotangent_t, back, rows
            )

        if g < groups - 1:
            if line is not None:
                grads = write(line.total(), g - 1)
            line = LineSum(order, chips)
            line.swap(side(1 - core))
            line.hold(side(core))
            line.advance()
            continue
        part = order(lambda *a: terms(a[:2], a[2:]), normed_t, cotangent_t, back, rows)
        if line is not None:
            part, *line.arrived = lax.optimization_barrier((part, *line.arrived))
        last = lax.psum_scatter(part, "wide", scatter_dimension=0, tiled=True)
        if line is not None:
            grads = write(line.total(), g - 1)
        parts = order(lambda *a: project(a[:groups], a[groups:]), *mixed, *weights)
        own, arrived = narrow_sum(parts, narrow)

    def finish_outputs(activations, *parts):
        share = parts[0].shape[1]
        at = lax.axis_index("narrow") * share
        result = lax.dynamic_slice_in_dim(activations, at, share, 1).astype(F32)
        return (result + sum(part.astype(F32) for part in parts)).astype(BF16)

    outputs = order(finish_outputs, activations, own, *arrived)
    grad_query, grad_key, grad_value, grad_out = unpack(last, grads, span, groups, groups - 1)
    return (outputs, grad_query, grad_key, grad_value, grad_out)


def solution(mesh):
    return jax.shard_map(
        functools.partial(shards, (mesh.shape["wide"], mesh.shape["narrow"])),
        mesh=mesh,
        in_specs=(
            P("wide", None),
            P(),
            P("wide", "narrow"),
            P("wide", "narrow"),
            P("wide", "narrow"),
            P("wide", "narrow"),
            P("wide", None),
        ),
        out_specs=(
            P("wide", "narrow"),
            P("wide", "narrow"),
            P("wide", "narrow"),
            P("wide", "narrow"),
            P("wide", "narrow"),
        ),
        check_vma=False,
    )
```
